512 devices in a mesh: box: 64 (over y, x, core), dir: 8 (over z).
Axes of the slice: x: 4, y: 8, z: 8, core: 2. Of those that a mesh axis runs over, the one named last changes fastest.
Arguments:
- currents: bfloat16 [2, 128, 16384], P(None, None, 'box'), may hold values from -6 to 6
- box_code: int32 [16384], P('box'), may hold values from 0 to 255, as said below
- box_count: int32 [64], P('box'), may hold values from 76 to 256, as said below
- radiation: bfloat16 [2, 128, 128], replicated, may hold values from -0.375 to 0.375
- near_block: bfloat16 [9, 2, 128, 128], replicated, may hold values from -0.125 to 0.125
- translation: float32 [40, 2, 16, 32], P(None, None, None, 'dir'), may hold values from -1.2 to 1.2
Outputs:
- result: bfloat16 [2, 128, 16384], P(None, None, ('box', 'dir'))
The draws below stay inside these ranges and needn't reach their ends.
Inputs may be any that keep to these rules, and one draw needn't show every extreme that they name: `box_code`: for each block the 256 entries are the Morton codes of its 16 x 16 cells, each once; the first box_count entries, ascending, are the live boxes. `box_count`: some block is full and some block holds exactly the least count.
All inputs are finite; a program needn't handle non-finite values.
Results may differ from the reference program's by a relative error of at most 0.0016.
Values may be sent and summed in bfloat16 or wider, within the bound.
A program may use at most 64 MiB of HBM per device.

```python
import math
import jax
import jax.numpy as jnp
from jax import lax

U = 128
NT0 = 8
NP0 = 16
NT1 = 16
NP1 = 32
BSIDE = 16
DISP = 40
NEAR = 9
BOX_DEV = 256
BOXES = 16384
K0 = 128
N_BOX = 64


def morton_code(row_index, column_index):
    code = jnp.zeros_like(row_index)
    for bit_place in range(6):
        code = code + ((column_index >> bit_place & 1) << 2 * bit_place) + ((row_index >> bit_place & 1) << 2 * bit_place + 1)
    return code


def block_layout(key):
    blocks = BOXES // BOX_DEV
    least = 3 * BOX_DEV // 10
    count_key, full_key, order_key = jax.random.split(key, 3)
    counts = jax.random.randint(count_key, (blocks,), least, BOX_DEV + 1)
    fullest = jax.random.randint(full_key, (), 0, blocks)
    emptiest = (fullest + 1) % blocks
    block_ids = jnp.arange(blocks)
    counts = jnp.where(block_ids == fullest, BOX_DEV, counts)
    counts = jnp.where(block_ids == emptiest, least, counts).astype(jnp.int32)
    ranks = jax.vmap(lambda sub_key: jax.random.permutation(sub_key, BOX_DEV))(jax.random.split(order_key, blocks))
    live = ranks < counts[:, None]
    cells = jnp.arange(BOX_DEV, dtype=jnp.int32)
    codes = morton_code(cells // BSIDE, cells % BSIDE)
    score = jnp.where(live, codes[None, :], codes[None, :] + 8192)
    order = jnp.argsort(score, axis=1)
    ordered = jnp.take(codes, order)
    return (ordered.reshape(-1).astype(jnp.int32), counts)


def draw_box_code(key, part):
    return block_layout(key)[0]


def draw_box_count(key, part):
    return block_layout(key)[1]


def block_levels(stream_key, shape, cuts, smallest, high):
    def one(dim, blocks):
        heights = jax.random.uniform(jax.random.fold_in(jax.random.fold_in(stream_key, 6), dim), (blocks,), jnp.float32, smallest / len(cuts), high / len(cuts))
        return jnp.repeat(jnp.exp(heights), shape[dim] // blocks).reshape((-1,) + (1,) * (len(shape) - dim - 1))

    loudness = one(*cuts[0])
    for cut in cuts[1:]:
        loudness = loudness * one(*cut)
    return loudness


def bell_draw(key, shape, scale, limit, cuts=(), kind=jnp.bfloat16):
    values = jax.random.normal(key, shape, jnp.float32) * scale
    if len(cuts) > 0:
        values = block_levels(key, shape, cuts, -0.22, 0.18) * values
    return jnp.clip(values, min=-limit, max=limit).astype(kind)


def setup_inputs(seed: int = 0) -> dict:
    seeds = jax.random.split(jax.random.key(seed), 7)
    return {
        "currents": bell_draw(seeds[0], (2, U, BOXES), 1.0, 6.0, ((2, 64),)),
        "box_code": draw_box_code(jax.random.fold_in(seeds[6], 71), 0),
        "box_count": draw_box_count(jax.random.fold_in(seeds[6], 71), 0),
        "radiation": bell_draw(seeds[3], (2, K0, U), (2 * U) ** -0.5, 0.375),
        "near_block": bell_draw(seeds[4], (NEAR, 2, U, U), (18 * U) ** -0.5, 0.125),
        "translation": bell_draw(seeds[5], (DISP, 2, NT1, NP1), 0.2, 1.2, ((3, 8),), jnp.float32),
    }


highest = lax.Precision.HIGHEST
wave_size = math.pi

def morton_split(code):
    row_index = jnp.zeros_like(code)
    column_index = jnp.zeros_like(code)
    for bit_place in range(6):
        column_index = column_index + ((code >> 2 * bit_place & 1) << bit_place)
        row_index = row_index + ((code >> 2 * bit_place + 1 & 1) << bit_place)
    return (row_index, column_index)

def lagrange(offset, node):
    first = -(offset - 1.0) * (offset - 2.0) * (offset - 3.0) / 6.0
    second = offset * (offset - 2.0) * (offset - 3.0) / 2.0
    third = -offset * (offset - 1.0) * (offset - 3.0) / 2.0
    fourth = offset * (offset - 1.0) * (offset - 2.0) / 6.0
    return jnp.where(node == 0, first, 0.0) + jnp.where(node == 1, second, 0.0) + jnp.where(node == 2, third, 0.0) + jnp.where(node == 3, fourth, 0.0)

def theta_table(coarse_count, fine_count):
    coarse = jnp.arange(coarse_count, dtype=jnp.int32)[:, None]
    fine = jnp.arange(fine_count, dtype=jnp.int32)[None, :]
    twice = 2 * coarse - 1
    base = jnp.clip(twice // 4 - 1, 0, fine_count - 4)
    offset = (twice - 4 * base).astype(jnp.float32) / 4.0
    return lagrange(offset, fine - base)

def phi_table(coarse, fine, period):
    twice = 2 * coarse[:, None] - 1
    base = twice // 4 - 1
    offset = (twice - 4 * base).astype(jnp.float32) / 4.0
    node = fine[None, :] - base
    if period > 0:
        node = node % period
    return lagrange(offset, node)

def phase_angle(theta_index, phi_index, theta_count, phi_count):
    theta = (theta_index.astype(jnp.float32) + 0.5) * math.pi / theta_count
    azimuth = (phi_index.astype(jnp.float32) + 0.5) * 2.0 * math.pi / phi_count
    along_column = jnp.sin(theta)[:, None] * jnp.cos(azimuth)[None, :]
    along_row = jnp.sin(theta)[:, None] * jnp.sin(azimuth)[None, :]
    halves = jnp.array([-0.5, 0.5], dtype=jnp.float32)
    return wave_size * (along_row[:, :, None, None] * halves[:, None] + along_column[:, :, None, None] * halves[None, :])

def displacements():
    return [(offset_row, offset_column) for offset_row in range(-3, 4) for offset_column in range(-3, 4) if max(abs(offset_row), abs(offset_column)) >= 2]

def gather_children(upper, angle, cells_side):
    parents_side = cells_side // 2
    shaped = upper.reshape(2, upper.shape[1], upper.shape[2], parents_side, 2, parents_side, 2)
    cosine = jnp.cos(angle)[:, :, None, :, None, :]
    sine = jnp.sin(angle)[:, :, None, :, None, :]
    real_part = lax.optimization_barrier(jnp.sum(shaped[0] * cosine + shaped[1] * sine, axis=(3, 5)))
    imaginary = lax.optimization_barrier(jnp.sum(shaped[1] * cosine - shaped[0] * sine, axis=(3, 5)))
    return jnp.stack([real_part, imaginary])

def spread_children(incoming, angle):
    cosine = jnp.cos(angle)[:, :, None, :, None, :]
    sine = jnp.sin(angle)[:, :, None, :, None, :]
    source_real = incoming[0][:, :, :, None, :, None]
    source_imag = incoming[1][:, :, :, None, :, None]
    real_part = source_real * cosine - source_imag * sine
    imaginary = source_imag * cosine + source_real * sine
    stacked = jnp.stack([real_part, imaginary])
    return stacked.reshape(2, stacked.shape[1], stacked.shape[2], -1)

def translate(parent, translation, global_rows, global_columns, count):
    total = jnp.zeros(parent.shape[:3] + (count, count), jnp.float32)
    for number, (offset_row, offset_column) in enumerate(displacements()):
        source = parent[:, :, :, 3 + offset_row:3 + offset_row + count, 3 + offset_column:3 + offset_column + count]
        keep_row = jnp.abs((global_rows + offset_row) // 2 - global_rows // 2) <= 1
        keep_column = jnp.abs((global_columns + offset_column) // 2 - global_columns // 2) <= 1
        keep = keep_row[:, None] & keep_column[None, :]
        op_real = translation[number, 0][:, :, None, None]
        op_imag = translation[number, 1][:, :, None, None]
        real_part = op_real * source[0] - op_imag * source[1]
        imaginary = op_real * source[1] + op_imag * source[0]
        total = total + jnp.where(keep, jnp.stack([real_part, imaginary]), 0.0)
    return total

def receive(radiation_wide, lower_flat):
    far_real = jnp.einsum('ku,kn->un', radiation_wide[0], lower_flat[0], precision=highest) + jnp.einsum('ku,kn->un', radiation_wide[1], lower_flat[1], precision=highest)
    far_imag = jnp.einsum('ku,kn->un', radiation_wide[0], lower_flat[1], precision=highest) - jnp.einsum('ku,kn->un', radiation_wide[1], lower_flat[0], precision=highest)
    return jnp.stack([far_real, far_imag])

def reference(currents, box_code, box_count, radiation, near_block, translation):
    blocks_across = math.isqrt(N_BOX)
    grid = BSIDE * blocks_across
    parents_side = grid // 2
    slot_ids = jnp.arange(BOX_DEV, dtype=jnp.int32)
    device_ids = jnp.arange(N_BOX, dtype=jnp.int32)
    codes = box_code.reshape(N_BOX, BOX_DEV)
    live = (slot_ids[None, :] < box_count[:, None]).reshape(-1)
    row_index, column_index = morton_split(codes)
    global_row = (device_ids // blocks_across)[:, None] * BSIDE + row_index
    global_column = (device_ids % blocks_across)[:, None] * BSIDE + column_index
    cell = (global_row * grid + global_column).reshape(-1).astype(jnp.int32)
    masked = jnp.where(live[None, None, :], currents, jnp.zeros_like(currents))
    field = jnp.zeros((2, U, grid * grid), jnp.bfloat16).at[:, :, cell].set(masked)
    pattern_real = jnp.dot(radiation[0], field[0], preferred_element_type=jnp.float32) - jnp.dot(radiation[1], field[1], preferred_element_type=jnp.float32)
    pattern_imag = jnp.dot(radiation[0], field[1], preferred_element_type=jnp.float32) + jnp.dot(radiation[1], field[0], preferred_element_type=jnp.float32)
    pattern = jnp.stack([pattern_real, pattern_imag]).reshape(2, NT0, NP0, grid * grid)
    theta_weight = theta_table(NT1, NT0)
    phi_weight = phi_table(jnp.arange(NP1, dtype=jnp.int32), jnp.arange(NP0, dtype=jnp.int32), NP0)
    upper = jnp.einsum('it,ctpn->cipn', theta_weight, pattern, precision=highest)
    upper = jnp.einsum('qp,cipn->ciqn', phi_weight, upper, precision=highest)
    angle = phase_angle(jnp.arange(NT1, dtype=jnp.int32), jnp.arange(NP1, dtype=jnp.int32), NT1, NP1)
    parent = gather_children(upper, angle, grid)
    padded = jnp.pad(parent, ((0, 0), (0, 0), (0, 0), (3, 3), (3, 3)))
    parent_rows = jnp.arange(parents_side, dtype=jnp.int32)
    incoming = translate(padded, translation, parent_rows, parent_rows, parents_side)
    child = spread_children(incoming, angle)
    lower = 0.25 * jnp.einsum('it,ciqn->ctqn', theta_weight, child, precision=highest)
    lower = jnp.einsum('qp,ctqn->ctpn', phi_weight, lower, precision=highest)
    far = receive(radiation.astype(jnp.float32), lower.reshape(2, NT0 * NP0, grid * grid))
    field_grid = jnp.pad(field.reshape(2, U, grid, grid), ((0, 0), (0, 0), (1, 1), (1, 1)))
    near_real = jnp.zeros((U, grid * grid), jnp.float32)
    near_imag = jnp.zeros((U, grid * grid), jnp.float32)
    for step_row in (-1, 0, 1):
        for step_column in (-1, 0, 1):
            number = (step_row + 1) * 3 + step_column + 1
            source = field_grid[:, :, 1 + step_row:1 + step_row + grid, 1 + step_column:1 + step_column + grid].reshape(2, U, grid * grid)
            block_real = near_block[number, 0]
            block_imag = near_block[number, 1]
            near_real = near_real + jnp.dot(block_real, source[0], preferred_element_type=jnp.float32) - jnp.dot(block_imag, source[1], preferred_element_type=jnp.float32)
            near_imag = near_imag + jnp.dot(block_real, source[1], preferred_element_type=jnp.float32) + jnp.dot(block_imag, source[0], preferred_element_type=jnp.float32)
    total = jnp.stack([near_real, near_imag]) + far
    by_slot = total[:, :, cell]
    return jnp.where(live[None, None, :], by_slot, 0.0).astype(jnp.bfloat16)
```

```python
import functools
import math

import jax
import jax.numpy as jnp
import ml_dtypes
import numpy as np
from jax import lax
from jax.experimental import pallas as pl
from jax.experimental.pallas import tpu as pltpu
from jax.sharding import PartitionSpec as P

U = 128
NT0 = 8
NP0 = 16
NT1 = 16
NP1 = 32
BSIDE = 16
PSIDE = 8
CELLS = 256
GROUPS = 8
QL = NP1 // GROUPS
SAMPLES = NT1 * QL
OWN = CELLS // GROUPS
STRIP = 16
DISP = 40
MESH = pl.DeviceIdType.MESH
F32 = jnp.float32
BF16 = jnp.bfloat16

FIELD_SENDS = (
    (1, 0, 1, 0),
    (-1, 0, 0, 1),
    (0, 1, 3, 2),
    (0, -1, 2, 3),
    (1, 1, 1, 4),
    (1, -1, 1, 5),
    (-1, 1, 0, 6),
    (-1, -1, 0, 7),
)


def lagrange(offset, node):
    first = -(offset - 1.0) * (offset - 2.0) * (offset - 3.0) / 6.0
    second = offset * (offset - 2.0) * (offset - 3.0) / 2.0
    third = -offset * (offset - 1.0) * (offset - 3.0) / 2.0
    fourth = offset * (offset - 1.0) * (offset - 2.0) / 6.0
    return (
        np.where(node == 0, first, 0.0)
        + np.where(node == 1, second, 0.0)
        + np.where(node == 2, third, 0.0)
        + np.where(node == 3, fourth, 0.0)
    )


def weight_tables():
    coarse = np.arange(NT1)[:, None]
    twice = 2 * coarse - 1
    base = np.clip(twice // 4 - 1, 0, NT0 - 4)
    theta = lagrange((twice - 4 * base) / 4.0, np.arange(NT0)[None, :] - base)
    coarse = np.arange(NP1)[:, None]
    twice = 2 * coarse - 1
    base = twice // 4 - 1
    phi = lagrange((twice - 4 * base) / 4.0, (np.arange(NP0)[None, :] - base) % NP0)
    return theta, phi


def halves(x):
    high = x.astype(ml_dtypes.bfloat16)
    low = (x - high.astype(np.float64)).astype(ml_dtypes.bfloat16)
    return high, low


def make_tables():
    theta, phi = weight_tables()
    polar = (np.arange(NT1) + 0.5) * math.pi / NT1
    azimuth = (np.arange(NP1) + 0.5) * 2.0 * math.pi / NP1
    mixed = np.zeros((GROUPS, 128, 128 + 512), ml_dtypes.bfloat16)
    phase = np.zeros((GROUPS, SAMPLES, 128), np.float32)
    for g in range(GROUPS):
        own = np.arange(g * QL, (g + 1) * QL)
        fold = np.einsum("it,qp->iqtp", theta, phi[own]).reshape(SAMPLES, NT0 * NP0)
        mixed[g, :, :128] = np.concatenate(halves(fold), axis=0)
        along_column = np.sin(polar)[:, None] * np.cos(azimuth[own])[None, :]
        along_row = np.sin(polar)[:, None] * np.sin(azimuth[own])[None, :]
        down = np.zeros((2, NT1, QL, 4, 2, NT0, QL))
        for child in range(4):
            oy, ox = child // 2, child % 2
            psi = math.pi * (along_column * (ox - 0.5) + along_row * (oy - 0.5))
            if child < 2:
                phase[g, :, 2 * child] = np.cos(psi).reshape(-1)
                phase[g, :, 2 * child + 1] = np.sin(psi).reshape(-1)
            for q in range(QL):
                real = 0.25 * theta * np.cos(psi[:, q])[:, None]
                imag = 0.25 * theta * np.sin(psi[:, q])[:, None]
                down[0, :, q, child, 0, :, q] = real
                down[1, :, q, child, 0, :, q] = -imag
                down[0, :, q, child, 1, :, q] = imag
                down[1, :, q, child, 1, :, q] = real
        mixed[g, :, 128:] = np.concatenate(halves(down.reshape(128, 256)), axis=1)
    back = np.zeros((GROUPS, 2, 2, NT0, QL, 2, NT0, NP0))
    for g in range(GROUPS):
        for part in range(2):
            for t in range(NT0):
                back[g, :, part, t, :, part, t, :] = phi[g * QL : (g + 1) * QL]
    back = back.reshape(GROUPS * 128, 256).astype(ml_dtypes.bfloat16)
    return mixed, phase, back


def split(x):
    high = x.astype(BF16)
    low = (x - high.astype(F32)).astype(BF16)
    return high, low


def iota(shape, dim):
    return lax.broadcasted_iota(jnp.int32, shape, dim)


def dot(a, b):
    return jnp.dot(a, b, preferred_element_type=F32)


def dot_nt(a, b):
    return lax.dot_general(a, b, (((1,), (1,)), ((), ())), preferred_element_type=F32)


def displacements():
    return [
        (dy, dx) for dy in range(-3, 4) for dx in range(-3, 4) if max(abs(dy), abs(dx)) >= 2
    ]


def kernel(
    across,
    code_ref,
    count_ref,
    cur_hbm,
    rad_hbm,
    near_hbm,
    trans_hbm,
    mixed_hbm,
    phase_hbm,
    back_hbm,
    out_ref,
    cur,
    rad,
    near,
    trans,
    mixed,
    phase,
    back,
    strips,
    fld,
    ext,
    index_col,
    ta,
    tb,
    radm,
    outbox,
    inbox,
    load_sem,
    fs_sem,
    fr_sem,
    ps_sem,
    pr_sem,
    zs_sem,
    zr_sem,
):
    block = lax.axis_index("box")
    group = lax.axis_index("dir")
    row = block // across
    col = block % across

    def neighbour(dr, dc):
        to_row = lax.rem(row + dr + across, across)
        to_col = lax.rem(col + dc + across, across)
        return (to_row * across + to_col, group)

    def peer(step):
        return (block, lax.rem(group + step, GROUPS))

    loads = []
    for number, (source, target) in enumerate(
        (
            (cur_hbm, cur),
            (rad_hbm, rad),
            (mixed_hbm.at[group], mixed),
            (phase_hbm.at[group], phase),
            (trans_hbm, trans),
            (near_hbm, near),
            (back_hbm, back),
        )
    ):
        copy = pltpu.make_async_copy(source, target, load_sem.at[number])
        copy.start()
        loads.append(copy)
    barrier = pltpu.get_barrier_semaphore()
    for dr, dc, _, _ in FIELD_SENDS:
        pl.semaphore_signal(barrier, inc=1, device_id=neighbour(dr, dc), device_id_type=MESH)
    for step in range(1, GROUPS):
        pl.semaphore_signal(barrier, inc=1, device_id=peer(step), device_id_type=MESH)

    code = code_ref[...]
    across_c = ((code >> 2) & 1) + ((code >> 4) & 1) * 2 + ((code >> 6) & 1) * 4
    down_r = ((code >> 3) & 1) + ((code >> 5) & 1) * 2 + ((code >> 7) & 1) * 4
    index_row = (code & 3) * 64 + down_r * 8 + across_c
    live_index = jnp.where(iota((1, CELLS), 1) < count_ref[0], index_row, -1)
    line = iota((64, CELLS), 0)
    kind = line // 16
    a, b = (line % 16) // 8, line % 8
    wanted = jnp.where(
        kind == 0,
        a * 64 + b,
        jnp.where(
            kind == 1,
            184 + a * 64 + b,
            jnp.where(kind == 2, a * 128 + b * 8, 71 + a * 128 + b * 8),
        ),
    )
    rows_wanted = jnp.concatenate([iota((CELLS, CELLS), 0), wanted], axis=0)
    place = jnp.where(rows_wanted == live_index, 1.0, 0.0).astype(BF16)
    loads[0].wait()
    placed = dot_nt(place, cur[...]).astype(BF16)
    fld[0:CELLS, :] = placed[:CELLS]
    strips[...] = placed[CELLS:]

    loads[1].wait()
    loads[2].wait()
    fold = mixed[:, 0:128]
    rr = dot(fold, rad[0:128, :])
    ri = dot(fold, rad[128:256, :])
    rr = rr[:64] + rr[64:]
    ri = ri[:64] + ri[64:]

    pl.semaphore_wait(barrier, len(FIELD_SENDS) + GROUPS - 1)
    sends = []
    for number, (dr, dc, which, slot) in enumerate(FIELD_SENDS):
        copy = pltpu.make_async_remote_copy(
            src_ref=strips.at[pl.ds(which * STRIP, STRIP)],
            dst_ref=fld.at[pl.ds(CELLS + slot * STRIP, STRIP)],
            send_sem=fs_sem.at[number],
            recv_sem=fr_sem.at[slot],
            device_id=neighbour(dr, dc),
            device_id_type=MESH,
        )
        copy.start()
        sends.append(copy)

    loads[3].wait()
    total = jnp.zeros((64, 256), F32)
    for pair in range(2):
        cosine = phase[:, 2 * pair : 2 * pair + 1]
        sine = phase[:, 2 * pair + 1 : 2 * pair + 2]
        cr, ci, sr, si = cosine * rr, cosine * ri, sine * rr, sine * ri
        for child, ar, ai in ((pair, cr + si, ci - sr), (3 - pair, cr - si, ci + sr)):
            arh, arl = split(ar)
            aih, ail = split(ai)
            matrix = jnp.concatenate(
                [
                    jnp.concatenate([arh, -aih], axis=1),
                    jnp.concatenate([aih, arh], axis=1),
                    jnp.concatenate([arl, -ail], axis=1),
                    jnp.concatenate([ail, arl], axis=1),
                ],
                axis=0,
            )
            total = total + dot_nt(placed[child * 64 : (child + 1) * 64], matrix)
    own_parent = total[:, :128] + total[:, 128:]
    ext[3:11, 8:16, :] = own_parent.reshape(PSIDE, PSIDE, 128)

    whole = (pl.ds(3, 8), pl.ds(8, 8))
    parent_sends = (
        (0, 1, whole, (pl.ds(3, 8), pl.ds(0, 8))),
        (0, -1, whole, (pl.ds(3, 8), pl.ds(16, 8))),
        (1, 0, (pl.ds(8, 3), pl.ds(8, 8)), (pl.ds(0, 3), pl.ds(8, 8))),
        (-1, 0, (pl.ds(3, 3), pl.ds(8, 8)), (pl.ds(11, 3), pl.ds(8, 8))),
        (1, 1, (pl.ds(8, 3), pl.ds(8, 8)), (pl.ds(0, 3), pl.ds(0, 8))),
        (1, -1, (pl.ds(8, 3), pl.ds(8, 8)), (pl.ds(0, 3), pl.ds(16, 8))),
        (-1, 1, (pl.ds(3, 3), pl.ds(8, 8)), (pl.ds(11, 3), pl.ds(0, 8))),
        (-1, -1, (pl.ds(3, 3), pl.ds(8, 8)), (pl.ds(11, 3), pl.ds(16, 8))),
    )
    parents = []
    for number, (dr, dc, source, target) in enumerate(parent_sends):
        copy = pltpu.make_async_remote_copy(
            src_ref=ext.at[source[0], source[1]],
            dst_ref=ext.at[target[0], target[1]],
            send_sem=ps_sem.at[number],
            recv_sem=pr_sem.at[number],
            device_id=neighbour(dr, dc),
            device_id_type=MESH,
        )
        copy.start()
        parents.append(copy)

    index_col[...] = jnp.transpose(jnp.broadcast_to(index_row, (128, CELLS)))
    by_slot = index_col[...]
    pick = jnp.concatenate(
        [
            jnp.where(by_slot == iota((CELLS, 128), 1) + first, 1.0, 0.0).astype(BF16)
            for first in (0, 128)
        ],
        axis=1,
    )
    loads[4].wait()
    by_disp = jnp.transpose(trans[...])
    turned = pltpu.roll(by_disp, 64, 1)
    left = iota((DISP, 128), 1) < 64
    ta[...] = jnp.where(left, by_disp, turned)
    tb[...] = jnp.where(left, turned, -by_disp)

    rad_real, rad_imag = rad[0:128, :], rad[128:256, :]
    radm[0:128, 0:128] = rad_real
    radm[0:128, 128:256] = -rad_imag
    radm[128:256, 0:128] = rad_imag
    radm[128:256, 128:256] = rad_real

    own_index = index_col[pl.ds(pl.multiple_of(group * OWN, OWN), OWN), :]
    own_r = ((own_index >> 3) & 7) * 2 + (own_index >> 7)
    own_c = (own_index & 7) * 2 + ((own_index >> 6) & 1)
    edge_n, edge_s = row == 0, row == across - 1
    edge_w, edge_e = col == 0, col == across - 1
    hot = []
    for dr in (-1, 0, 1):
        for dc in (-1, 0, 1):
            r, c = own_r + dr, own_c + dc
            rw, cw = r & 15, c & 15
            by_c = (cw & 1) * 8 + (cw >> 1)
            by_r = (rw & 1) * 8 + (rw >> 1)
            inside = ((rw & 1) * 2 + (cw & 1)) * 64 + (rw >> 1) * 8 + (cw >> 1)
            up, down, west, east = r < 0, r > 15, c < 0, c > 15
            at = jnp.where(west, 256 + 32 + by_r, jnp.where(east, 256 + 48 + by_r, inside))
            at = jnp.where(up, 256 + by_c + jnp.where(west, 64, jnp.where(east, 80, 0)), at)
            at = jnp.where(down, 256 + by_c + jnp.where(west, 96, jnp.where(east, 112, 16)), at)
            gone = (up & edge_n) | (down & edge_s) | (west & edge_w) | (east & edge_e)
            at = jnp.where(gone, -1, at)
            hot.append(
                jnp.concatenate(
                    [
                        jnp.where(at == iota((OWN, 128), 1) + first, 1.0, 0.0).astype(BF16)
                        for first in (0, 128, 256)
                    ],
                    axis=1,
                )
            )
    hot = jnp.concatenate(hot, axis=0)
    for copy in sends:
        copy.wait()
    around = dot(hot, fld[...]).astype(BF16)
    loads[5].wait()
    close = jnp.zeros((2 * OWN, 256), F32)
    for number in range(9):
        mine = around[number * OWN : (number + 1) * OWN]
        stacked = jnp.concatenate([mine[:, :128], mine[:, 128:]], axis=0)
        close = close + dot_nt(stacked, near[pl.ds(number * 256, 256), :])

    for copy in parents:
        copy.wait()

    @pl.when(edge_n)
    def _():
        ext[0:3] = jnp.zeros((3, 24, 128), F32)

    @pl.when(edge_s)
    def _():
        ext[11:14] = jnp.zeros((3, 24, 128), F32)

    @pl.when(edge_w)
    def _():
        ext[:, 0:8, :] = jnp.zeros((14, 8, 128), F32)

    @pl.when(edge_e)
    def _():
        ext[:, 16:24, :] = jnp.zeros((14, 8, 128), F32)

    numbers = {pair: number for number, pair in enumerate(displacements())}
    first = [jnp.zeros((4, PSIDE, 128), F32) for _ in range(2)]
    second = [jnp.zeros((4, PSIDE, 128), F32) for _ in range(2)]
    odd_column = (iota((7, 2, PSIDE, 128), 2) & 1) == 1
    for dx in range(-3, 4):
        tile = ext[:, 8 + dx : 16 + dx, :].reshape(7, 2, PSIDE, 128)
        if dx == -3:
            tile = jnp.where(odd_column, tile, 0.0)
        if dx == 3:
            tile = jnp.where(odd_column, 0.0, tile)
        for dy in range(-3, 4):
            if (dy, dx) not in numbers:
                continue
            number = numbers[dy, dx]
            wa = ta[number : number + 1, :].reshape(1, 1, 128)
            wb = tb[number : number + 1, :].reshape(1, 1, 128)
            for parity in range(2):
                if dy == (-3 if parity == 0 else 3):
                    continue
                start = 3 + dy + parity
                source = tile[start // 2 : start // 2 + 4, start % 2]
                first[parity] = first[parity] + wa * source
                second[parity] = second[parity] + wb * source
    first = jnp.stack(first, axis=1).reshape(64, 128)
    second = jnp.stack(second, axis=1).reshape(64, 128)
    incoming = first + pltpu.roll(second, 64, 1)

    high, low = split(incoming)
    wide = dot(jnp.concatenate([high, low], axis=0), mixed[:, 128:640])
    wide = wide[:64] + wide[64:]
    wide = wide[:, :256] + wide[:, 256:]
    left = iota((64, 128), 1) < 64
    pieces = []
    for pair in range(2):
        here = wide[:, pair * 128 : (pair + 1) * 128]
        turned = pltpu.roll(here, 64, 1)
        for value in (jnp.where(left, here, turned), jnp.where(left, turned, here)):
            top = value.astype(BF16).astype(F32)
            pieces.append(jnp.where(left, top, value - top).astype(BF16))
    chosen = dot(pick, jnp.concatenate(pieces, axis=0)).astype(BF16)
    outbox[...] = chosen.reshape(GROUPS, OWN, 128)

    posts = []
    for step in range(1, GROUPS):
        target = peer(step)
        copy = pltpu.make_async_remote_copy(
            src_ref=outbox.at[target[1]],
            dst_ref=inbox.at[group],
            send_sem=zs_sem.at[step - 1],
            recv_sem=zr_sem.at[step - 1],
            device_id=target,
            device_id_type=MESH,
        )
        copy.start()
        posts.append(copy)
    inbox[group] = outbox[group]
    loads[6].wait()
    for copy in posts:
        copy.wait()
    gathered = jnp.concatenate([inbox[g] for g in range(GROUPS)], axis=1)
    lower = dot(gathered, back[...])
    high, low = split(lower)
    far = dot(jnp.concatenate([high, low], axis=0), radm[...])
    far = far[:OWN] + far[OWN:]
    live = iota((OWN, 128), 0) + group * OWN < count_ref[0]
    real = far[:, :128] + (close[:OWN, :128] - close[OWN:, 128:])
    imag = far[:, 128:] + (close[OWN:, :128] + close[:OWN, 128:])
    out_ref[0] = jnp.where(live, real, 0.0).astype(BF16)
    out_ref[1] = jnp.where(live, imag, 0.0).astype(BF16)


def on_device(across, tables, currents, box_code, box_count, radiation, near_block, translation):
    mixed, phase, back = tables
    vmem = pl.BlockSpec(memory_space=pltpu.VMEM)
    smem = pl.BlockSpec(memory_space=pltpu.SMEM)
    anywhere = pl.BlockSpec(memory_space=pl.ANY)
    result = pl.pallas_call(
        functools.partial(kernel, across),
        out_shape=jax.ShapeDtypeStruct((2, OWN, U), BF16),
        in_specs=[vmem, smem] + [anywhere] * 7,
        out_specs=vmem,
        scratch_shapes=[
            pltpu.VMEM((256, 256), BF16),
            pltpu.VMEM((256, 128), BF16),
            pltpu.VMEM((9 * 256, 128), BF16),
            pltpu.VMEM((128, DISP), F32),
            pltpu.VMEM((128, 640), BF16),
            pltpu.VMEM((SAMPLES, 128), F32),
            pltpu.VMEM((GROUPS * 128, 256), BF16),
            pltpu.VMEM((4 * STRIP, 256), BF16),
            pltpu.VMEM((CELLS + 8 * STRIP, 256), BF16),
            pltpu.VMEM((14, 24, 128), F32),
            pltpu.VMEM((CELLS, 128), jnp.int32),
            pltpu.VMEM((DISP, 128), F32),
            pltpu.VMEM((DISP, 128), F32),
            pltpu.VMEM((256, 256), BF16),
            pltpu.VMEM((GROUPS, OWN, 128), BF16),
            pltpu.VMEM((GROUPS, OWN, 128), BF16),
            pltpu.SemaphoreType.DMA((7,)),
            pltpu.SemaphoreType.DMA((8,)),
            pltpu.SemaphoreType.DMA((8,)),
            pltpu.SemaphoreType.DMA((8,)),
            pltpu.SemaphoreType.DMA((8,)),
            pltpu.SemaphoreType.DMA((7,)),
            pltpu.SemaphoreType.DMA((7,)),
        ],
        compiler_params=pltpu.CompilerParams(
            collective_id=0, has_side_effects=True, vmem_limit_bytes=48 * 1024 * 1024
        ),
    )(
        box_code.reshape(1, CELLS),
        box_count,
        currents.reshape(2 * U, CELLS),
        radiation.reshape(2 * 128, U),
        near_block.reshape(9 * 2 * U, U),
        jnp.transpose(translation, (1, 2, 3, 0)).reshape(128, DISP),
        jnp.asarray(mixed),
        jnp.asarray(phase),
        jnp.asarray(back),
    )
    return jnp.transpose(result, (0, 2, 1))


def solution(mesh):
    across = math.isqrt(mesh.shape["box"])
    tables = make_tables()

    def step(*arrays):
        return on_device(across, tables, *arrays)

    placed = (P(None, None, "box"), P("box"), P("box"), P(), P(), P(None, None, None, "dir"))
    return jax.shard_map(
        step,
        mesh=mesh,
        in_specs=placed,
        out_specs=P(None, None, ("box", "dir")),
        check_vma=False,
    )
```

```python
import functools
import math

import jax
import jax.numpy as jnp
import ml_dtypes
import numpy as np
from jax import lax
from jax.experimental import pallas as pl
from jax.experimental.pallas import tpu as pltpu
from jax.sharding import PartitionSpec as P

U = 128
NT0 = 8
NP0 = 16
NT1 = 16
NP1 = 32
BSIDE = 16
PSIDE = 8
CELLS = 256
GROUPS = 8
QL = NP1 // GROUPS
SAMPLES = NT1 * QL
OWN = CELLS // GROUPS
STRIP = 16
DISP = 40
MESH = pl.DeviceIdType.MESH
F32 = jnp.float32
BF16 = jnp.bfloat16

FIELD_SENDS = (
    (1, 0, 1, 0),
    (-1, 0, 0, 1),
    (0, 1, 3, 2),
    (0, -1, 2, 3),
    (1, 1, 1, 4),
    (1, -1, 1, 5),
    (-1, 1, 0, 6),
    (-1, -1, 0, 7),
)


def lagrange(offset, node):
    first = -(offset - 1.0) * (offset - 2.0) * (offset - 3.0) / 6.0
    second = offset * (offset - 2.0) * (offset - 3.0) / 2.0
    third = -offset * (offset - 1.0) * (offset - 3.0) / 2.0
    fourth = offset * (offset - 1.0) * (offset - 2.0) / 6.0
    return (
        np.where(node == 0, first, 0.0)
        + np.where(node == 1, second, 0.0)
        + np.where(node == 2, third, 0.0)
        + np.where(node == 3, fourth, 0.0)
    )


def weight_tables():
    coarse = np.arange(NT1)[:, None]
    twice = 2 * coarse - 1
    base = np.clip(twice // 4 - 1, 0, NT0 - 4)
    theta = lagrange((twice - 4 * base) / 4.0, np.arange(NT0)[None, :] - base)
    coarse = np.arange(NP1)[:, None]
    twice = 2 * coarse - 1
    base = twice // 4 - 1
    phi = lagrange((twice - 4 * base) / 4.0, (np.arange(NP0)[None, :] - base) % NP0)
    return theta, phi


def halves(x):
    high = x.astype(ml_dtypes.bfloat16)
    low = (x - high.astype(np.float64)).astype(ml_dtypes.bfloat16)
    return high, low


def make_tables():
    theta, phi = weight_tables()
    polar = (np.arange(NT1) + 0.5) * math.pi / NT1
    azimuth = (np.arange(NP1) + 0.5) * 2.0 * math.pi / NP1
    mixed = np.zeros((GROUPS, 128, 128 + 512), ml_dtypes.bfloat16)
    phase = np.zeros((GROUPS, SAMPLES, 128), np.float32)
    for g in range(GROUPS):
        own = np.arange(g * QL, (g + 1) * QL)
        fold = np.einsum("it,qp->iqtp", theta, phi[own]).reshape(SAMPLES, NT0 * NP0)
        mixed[g, :, :128] = np.concatenate(halves(fold), axis=0)
        along_column = np.sin(polar)[:, None] * np.cos(azimuth[own])[None, :]
        along_row = np.sin(polar)[:, None] * np.sin(azimuth[own])[None, :]
        down = np.zeros((2, NT1, QL, 4, 2, NT0, QL))
        for child in range(4):
            oy, ox = child // 2, child % 2
            psi = math.pi * (along_column * (ox - 0.5) + along_row * (oy - 0.5))
            if child < 2:
                phase[g, :, 2 * child] = np.cos(psi).reshape(-1)
                phase[g, :, 2 * child + 1] = np.sin(psi).reshape(-1)
            for q in range(QL):
                real = 0.25 * theta * np.cos(psi[:, q])[:, None]
                imag = 0.25 * theta * np.sin(psi[:, q])[:, None]
                down[0, :, q, child, 0, :, q] = real
                down[1, :, q, child, 0, :, q] = -imag
                down[0, :, q, child, 1, :, q] = imag
                down[1, :, q, child, 1, :, q] = real
        mixed[g, :, 128:] = np.concatenate(halves(down.reshape(128, 256)), axis=1)
    back = np.zeros((GROUPS, 2, 2, NT0, QL, 2, NT0, NP0))
    for g in range(GROUPS):
        for part in range(2):
            for t in range(NT0):
                back[g, :, part, t, :, part, t, :] = phi[g * QL : (g + 1) * QL]
    back = back.reshape(GROUPS * 128, 256).astype(ml_dtypes.bfloat16)
    return mixed, phase, back


def split(x):
    high = x.astype(BF16)
    low = (x - high.astype(F32)).astype(BF16)
    return high, low


def iota(shape, dim):
    return lax.broadcasted_iota(jnp.int32, shape, dim)


def dot(a, b):
    return jnp.dot(a, b, preferred_element_type=F32)


def dot_nt(a, b):
    return lax.dot_general(a, b, (((1,), (1,)), ((), ())), preferred_element_type=F32)


def displacements():
    return [
        (dy, dx) for dy in range(-3, 4) for dx in range(-3, 4) if max(abs(dy), abs(dx)) >= 2
    ]


def kernel(
    across,
    code_hbm,
    count_ref,
    cur_hbm,
    rad_hbm,
    near_hbm,
    trans_hbm,
    mixed_hbm,
    phase_hbm,
    back_hbm,
    out_ref,
    code_ref,
    cur,
    rad,
    near,
    trans,
    mixed,
    phase,
    back,
    strips,
    fld,
    ext,
    index_col,
    ta,
    tb,
    radm,
    outbox,
    inbox,
    load_sem,
    fs_sem,
    fr_sem,
    ps_sem,
    pr_sem,
    zs_sem,
    zr_sem,
):
    block = lax.axis_index("box")
    group = lax.axis_index("dir")
    row = block // across
    col = block % across

    def neighbour(dr, dc):
        to_row = lax.rem(row + dr + across, across)
        to_col = lax.rem(col + dc + across, across)
        return (to_row * across + to_col, group)

    def peer(step):
        return (block, lax.rem(group + step, GROUPS))

    loads = []
    for number, (source, target) in enumerate(
        (
            (cur_hbm, cur),
            (rad_hbm, rad),
            (mixed_hbm.at[group], mixed),
            (phase_hbm.at[group], phase),
            (trans_hbm, trans),
            (near_hbm, near),
            (back_hbm, back),
            (code_hbm, code_ref),
        )
    ):
        copy = pltpu.make_async_copy(source, target, load_sem.at[number])
        copy.start()
        loads.append(copy)
    barrier = pltpu.get_barrier_semaphore()
    for dr, dc, _, _ in FIELD_SENDS:
        pl.semaphore_signal(barrier, inc=1, device_id=neighbour(dr, dc), device_id_type=MESH)
    for step in range(1, GROUPS):
        pl.semaphore_signal(barrier, inc=1, device_id=peer(step), device_id_type=MESH)

    loads[7].wait()
    code = code_ref[...]
    across_c = ((code >> 2) & 1) + ((code >> 4) & 1) * 2 + ((code >> 6) & 1) * 4
    down_r = ((code >> 3) & 1) + ((code >> 5) & 1) * 2 + ((code >> 7) & 1) * 4
    index_row = (code & 3) * 64 + down_r * 8 + across_c
    live_index = jnp.where(iota((1, CELLS), 1) < count_ref[0], index_row, -1)
    line = iota((64, CELLS), 0)
    kind = line // 16
    a, b = (line % 16) // 8, line % 8
    wanted = jnp.where(
        kind == 0,
        a * 64 + b,
        jnp.where(
            kind == 1,
            184 + a * 64 + b,
            jnp.where(kind == 2, a * 128 + b * 8, 71 + a * 128 + b * 8),
        ),
    )
    rows_wanted = jnp.concatenate([iota((CELLS, CELLS), 0), wanted], axis=0)
    place = jnp.where(rows_wanted == live_index, 1.0, 0.0).astype(BF16)
    loads[0].wait()
    placed = dot_nt(place, cur[...]).astype(BF16)
    fld[0:CELLS, :] = placed[:CELLS]
    strips[...] = placed[CELLS:]
    loads[1].wait()
    loads[2].wait()
    fold = mixed[:, 0:128]
    rr = dot(fold, rad[0:128, :])
    ri = dot(fold, rad[128:256, :])
    rr = rr[:64] + rr[64:]
    ri = ri[:64] + ri[64:]

    pl.semaphore_wait(barrier, len(FIELD_SENDS) + GROUPS - 1)
    sends = []
    for number, (dr, dc, which, slot) in enumerate(FIELD_SENDS):
        copy = pltpu.make_async_remote_copy(
            src_ref=strips.at[pl.ds(which * STRIP, STRIP)],
            dst_ref=fld.at[pl.ds(CELLS + slot * STRIP, STRIP)],
            send_sem=fs_sem.at[number],
            recv_sem=fr_sem.at[slot],
            device_id=neighbour(dr, dc),
            device_id_type=MESH,
        )
        copy.start()
        sends.append(copy)

    loads[3].wait()
    total = jnp.zeros((64, 256), F32)
    for pair in range(2):
        cosine = phase[:, 2 * pair : 2 * pair + 1]
        sine = phase[:, 2 * pair + 1 : 2 * pair + 2]
        cr, ci, sr, si = cosine * rr, cosine * ri, sine * rr, sine * ri
        for child, ar, ai in ((pair, cr + si, ci - sr), (3 - pair, cr - si, ci + sr)):
            arh, arl = split(ar)
            aih, ail = split(ai)
            matrix = jnp.concatenate(
                [
                    jnp.concatenate([arh, -aih], axis=1),
                    jnp.concatenate([aih, arh], axis=1),
                    jnp.concatenate([arl, -ail], axis=1),
                    jnp.concatenate([ail, arl], axis=1),
                ],
                axis=0,
            )
            total = total + dot_nt(placed[child * 64 : (child + 1) * 64], matrix)
    own_parent = total[:, :128] + total[:, 128:]
    ext[3:11, 8:16, :] = own_parent.reshape(PSIDE, PSIDE, 128)
    whole = (pl.ds(3, 8), pl.ds(8, 8))
    parent_sends = (
        (0, 1, whole, (pl.ds(3, 8), pl.ds(0, 8))),
        (0, -1, whole, (pl.ds(3, 8), pl.ds(16, 8))),
        (1, 0, (pl.ds(8, 3), pl.ds(8, 8)), (pl.ds(0, 3), pl.ds(8, 8))),
        (-1, 0, (pl.ds(3, 3), pl.ds(8, 8)), (pl.ds(11, 3), pl.ds(8, 8))),
        (1, 1, (pl.ds(8, 3), pl.ds(8, 8)), (pl.ds(0, 3), pl.ds(0, 8))),
        (1, -1, (pl.ds(8, 3), pl.ds(8, 8)), (pl.ds(0, 3), pl.ds(16, 8))),
        (-1, 1, (pl.ds(3, 3), pl.ds(8, 8)), (pl.ds(11, 3), pl.ds(0, 8))),
        (-1, -1, (pl.ds(3, 3), pl.ds(8, 8)), (pl.ds(11, 3), pl.ds(16, 8))),
    )
    parents = []
    for number, (dr, dc, source, target) in enumerate(parent_sends):
        copy = pltpu.make_async_remote_copy(
            src_ref=ext.at[source[0], source[1]],
            dst_ref=ext.at[target[0], target[1]],
            send_sem=ps_sem.at[number],
            recv_sem=pr_sem.at[number],
            device_id=neighbour(dr, dc),
            device_id_type=MESH,
        )
        copy.start()
        parents.append(copy)

    index_col[...] = jnp.transpose(jnp.broadcast_to(index_row, (128, CELLS)))
    by_slot = index_col[...]
    pick = jnp.concatenate(
        [
            jnp.where(by_slot == iota((CELLS, 128), 1) + first, 1.0, 0.0).astype(BF16)
            for first in (0, 128)
        ],
        axis=1,
    )
    loads[4].wait()
    by_disp = jnp.transpose(trans[...])
    turned = pltpu.roll(by_disp, 64, 1)
    left = iota((DISP, 128), 1) < 64
    ta[...] = jnp.where(left, by_disp, turned)
    tb[...] = jnp.where(left, turned, -by_disp)

    rad_real, rad_imag = rad[0:128, :], rad[128:256, :]
    radm[0:128, 0:128] = rad_real
    radm[0:128, 128:256] = -rad_imag
    radm[128:256, 0:128] = rad_imag
    radm[128:256, 128:256] = rad_real

    own_index = index_col[pl.ds(pl.multiple_of(group * OWN, OWN), OWN), :]
    own_r = ((own_index >> 3) & 7) * 2 + (own_index >> 7)
    own_c = (own_index & 7) * 2 + ((own_index >> 6) & 1)
    edge_n, edge_s = row == 0, row == across - 1
    edge_w, edge_e = col == 0, col == across - 1
    hot = []
    for dr in (-1, 0, 1):
        for dc in (-1, 0, 1):
            r, c = own_r + dr, own_c + dc
            rw, cw = r & 15, c & 15
            by_c = (cw & 1) * 8 + (cw >> 1)
            by_r = (rw & 1) * 8 + (rw >> 1)
            inside = ((rw & 1) * 2 + (cw & 1)) * 64 + (rw >> 1) * 8 + (cw >> 1)
            up, down, west, east = r < 0, r > 15, c < 0, c > 15
            at = jnp.where(west, 256 + 32 + by_r, jnp.where(east, 256 + 48 + by_r, inside))
            at = jnp.where(up, 256 + by_c + jnp.where(west, 64, jnp.where(east, 80, 0)), at)
            at = jnp.where(down, 256 + by_c + jnp.where(west, 96, jnp.where(east, 112, 16)), at)
            gone = (up & edge_n) | (down & edge_s) | (west & edge_w) | (east & edge_e)
            at = jnp.where(gone, -1, at)
            hot.append(
                jnp.concatenate(
                    [
                        jnp.where(at == iota((OWN, 128), 1) + first, 1.0, 0.0).astype(BF16)
                        for first in (0, 128, 256)
                    ],
                    axis=1,
                )
            )
    hot = jnp.concatenate(hot, axis=0)
    for copy in sends:
        copy.wait()
    around = dot(hot, fld[...]).astype(BF16)
    loads[5].wait()
    close = jnp.zeros((2 * OWN, 256), F32)
    for number in range(9):
        mine = around[number * OWN : (number + 1) * OWN]
        stacked = jnp.concatenate([mine[:, :128], mine[:, 128:]], axis=0)
        close = close + dot_nt(stacked, near[pl.ds(number * 256, 256), :])
    for copy in parents:
        copy.wait()

    @pl.when(edge_n)
    def _():
        ext[0:3] = jnp.zeros((3, 24, 128), F32)

    @pl.when(edge_s)
    def _():
        ext[11:14] = jnp.zeros((3, 24, 128), F32)

    @pl.when(edge_w)
    def _():
        ext[:, 0:8, :] = jnp.zeros((14, 8, 128), F32)

    @pl.when(edge_e)
    def _():
        ext[:, 16:24, :] = jnp.zeros((14, 8, 128), F32)

    numbers = {pair: number for number, pair in enumerate(displacements())}
    first = [jnp.zeros((4, PSIDE, 128), F32) for _ in range(2)]
    second = [jnp.zeros((4, PSIDE, 128), F32) for _ in range(2)]
    odd_column = (iota((7, 2, PSIDE, 128), 2) & 1) == 1
    for dx in range(-3, 4):
        tile = ext[:, 8 + dx : 16 + dx, :].reshape(7, 2, PSIDE, 128)
        if dx == -3:
            tile = jnp.where(odd_column, tile, 0.0)
        if dx == 3:
            tile = jnp.where(odd_column, 0.0, tile)
        for dy in range(-3, 4):
            if (dy, dx) not in numbers:
                continue
            number = numbers[dy, dx]
            wa = ta[number : number + 1, :].reshape(1, 1, 128)
            wb = tb[number : number + 1, :].reshape(1, 1, 128)
            for parity in range(2):
                if dy == (-3 if parity == 0 else 3):
                    continue
                start = 3 + dy + parity
                source = tile[start // 2 : start // 2 + 4, start % 2]
                first[parity] = first[parity] + wa * source
                second[parity] = second[parity] + wb * source
    first = jnp.stack(first, axis=1).reshape(64, 128)
    second = jnp.stack(second, axis=1).reshape(64, 128)
    incoming = first + pltpu.roll(second, 64, 1)
    high, low = split(incoming)
    wide = dot(jnp.concatenate([high, low], axis=0), mixed[:, 128:640])
    wide = wide[:64] + wide[64:]
    wide = wide[:, :256] + wide[:, 256:]
    left = iota((64, 128), 1) < 64
    pieces = []
    for pair in range(2):
        here = wide[:, pair * 128 : (pair + 1) * 128]
        turned = pltpu.roll(here, 64, 1)
        for value in (jnp.where(left, here, turned), jnp.where(left, turned, here)):
            top = value.astype(BF16).astype(F32)
            pieces.append(jnp.where(left, top, value - top).astype(BF16))
    chosen = dot(pick, jnp.concatenate(pieces, axis=0)).astype(BF16)
    outbox[...] = chosen.reshape(GROUPS, OWN, 128)
    posts = []
    for step in range(1, GROUPS):
        target = peer(step)
        copy = pltpu.make_async_remote_copy(
            src_ref=outbox.at[target[1]],
            dst_ref=inbox.at[group],
            send_sem=zs_sem.at[step - 1],
            recv_sem=zr_sem.at[step - 1],
            device_id=target,
            device_id_type=MESH,
        )
        copy.start()
        posts.append(copy)
    inbox[group] = outbox[group]
    loads[6].wait()
    for copy in posts:
        copy.wait()
    gathered = jnp.concatenate([inbox[g] for g in range(GROUPS)], axis=1)
    lower = dot(gathered, back[...])
    high, low = split(lower)
    far = dot(jnp.concatenate([high, low], axis=0), radm[...])
    far = far[:OWN] + far[OWN:]
    live = iota((OWN, 128), 0) + group * OWN < count_ref[0]
    real = far[:, :128] + (close[:OWN, :128] - close[OWN:, 128:])
    imag = far[:, 128:] + (close[OWN:, :128] + close[:OWN, 128:])
    out_ref[0] = jnp.where(live, real, 0.0).astype(BF16)
    out_ref[1] = jnp.where(live, imag, 0.0).astype(BF16)


def on_device(across, tables, currents, box_code, box_count, radiation, near_block, translation):
    mixed, phase, back = tables
    operands = (
        box_code.reshape(1, CELLS),
        box_count,
        currents.reshape(2 * U, CELLS),
        radiation.reshape(2 * 128, U),
        near_block.reshape(9 * 2 * U, U),
        jnp.transpose(translation, (1, 2, 3, 0)).reshape(128, DISP),
        jnp.asarray(mixed),
        jnp.asarray(phase),
        jnp.asarray(back),
    )
    vmem = pl.BlockSpec(memory_space=pltpu.VMEM)
    outside = pl.BlockSpec(memory_space=pltpu.HBM)
    result = pl.pallas_call(
        functools.partial(kernel, across),
        out_shape=jax.ShapeDtypeStruct((2, OWN, U), BF16),
        in_specs=[outside, pl.BlockSpec(memory_space=pltpu.SMEM)] + [outside] * 7,
        out_specs=vmem,
        scratch_shapes=[
            pltpu.VMEM((1, CELLS), jnp.int32),
            pltpu.VMEM((256, 256), BF16),
            pltpu.VMEM((256, 128), BF16),
            pltpu.VMEM((9 * 256, 128), BF16),
            pltpu.VMEM((128, DISP), F32),
            pltpu.VMEM((128, 640), BF16),
            pltpu.VMEM((SAMPLES, 128), F32),
            pltpu.VMEM((GROUPS * 128, 256), BF16),
            pltpu.VMEM((4 * STRIP, 256), BF16),
            pltpu.VMEM((CELLS + 8 * STRIP, 256), BF16),
            pltpu.VMEM((14, 24, 128), F32),
            pltpu.VMEM((CELLS, 128), jnp.int32),
            pltpu.VMEM((DISP, 128), F32),
            pltpu.VMEM((DISP, 128), F32),
            pltpu.VMEM((256, 256), BF16),
            pltpu.VMEM((GROUPS, OWN, 128), BF16),
            pltpu.VMEM((GROUPS, OWN, 128), BF16),
            pltpu.SemaphoreType.DMA((8,)),
            pltpu.SemaphoreType.DMA((8,)),
            pltpu.SemaphoreType.DMA((8,)),
            pltpu.SemaphoreType.DMA((8,)),
            pltpu.SemaphoreType.DMA((8,)),
            pltpu.SemaphoreType.DMA((7,)),
            pltpu.SemaphoreType.DMA((7,)),
        ],
        compiler_params=pltpu.CompilerParams(
            collective_id=0, has_side_effects=True, vmem_limit_bytes=48 * 1024 * 1024
        ),
    )(*(pltpu.with_memory_space_constraint(x, pltpu.HBM) if x.size > 1 else x for x in operands))
    return jnp.transpose(result, (0, 2, 1))


def solution(mesh):
    across = math.isqrt(mesh.shape["box"])
    tables = make_tables()

    def step(*arrays):
        return on_device(across, tables, *arrays)

    placed = (P(None, None, "box"), P("box"), P("box"), P(), P(), P(None, None, None, "dir"))
    return jax.shard_map(
        step,
        mesh=mesh,
        in_specs=placed,
        out_specs=P(None, None, ("box", "dir")),
        check_vma=False,
    )
```

```python
import functools
import math

import jax
import jax.numpy as jnp
import ml_dtypes
import numpy as np
from jax import lax
from jax.experimental import pallas as pl
from jax.experimental.pallas import tpu as pltpu
from jax.sharding import PartitionSpec as P

U = 128
NT0 = 8
NP0 = 16
NT1 = 16
NP1 = 32
PSIDE = 8
CELLS = 256
GROUPS = 8
QL = NP1 // GROUPS
SAMPLES = NT1 * QL
OWN = CELLS // GROUPS
DISP = 40
STAGE = 4
MESH = pl.DeviceIdType.MESH
F32 = jnp.float32
BF16 = jnp.bfloat16

STEPS = ((1, 0), (-1, 0), (0, 1), (0, -1), (1, 1), (-1, -1), (1, -1), (-1, 1))
PIECES = (
    ("own", 32, 32, 64),
    ("own", 0, 32, 96),
    ("side", 32, 32, 128),
    ("side", 0, 32, 160),
    ("side", 48, 16, 192),
    ("side", 0, 16, 240),
    ("side", 16, 16, 208),
    ("side", 32, 16, 224),
)


def lagrange(offset, node):
    first = -(offset - 1.0) * (offset - 2.0) * (offset - 3.0) / 6.0
    second = offset * (offset - 2.0) * (offset - 3.0) / 2.0
    third = -offset * (offset - 1.0) * (offset - 3.0) / 2.0
    fourth = offset * (offset - 1.0) * (offset - 2.0) / 6.0
    return (
        np.where(node == 0, first, 0.0)
        + np.where(node == 1, second, 0.0)
        + np.where(node == 2, third, 0.0)
        + np.where(node == 3, fourth, 0.0)
    )


def make_tables():
    coarse = np.arange(NT1)[:, None]
    twice = 2 * coarse - 1
    base = np.clip(twice // 4 - 1, 0, NT0 - 4)
    theta = lagrange((twice - 4 * base) / 4.0, np.arange(NT0)[None, :] - base)
    coarse = np.arange(NP1)[:, None]
    twice = 2 * coarse - 1
    base = twice // 4 - 1
    phi = lagrange((twice - 4 * base) / 4.0, (np.arange(NP0)[None, :] - base) % NP0)
    polar = (np.arange(NT1) + 0.5) * math.pi / NT1
    azimuth = (np.arange(NP1) + 0.5) * 2.0 * math.pi / NP1
    fold = np.zeros((GROUPS, 2 * SAMPLES, NT0 * NP0), ml_dtypes.bfloat16)
    phase = np.zeros((GROUPS, SAMPLES, 128), np.float32)
    for g in range(GROUPS):
        own = np.arange(g * QL, (g + 1) * QL)
        full = np.einsum("it,qp->iqtp", theta, phi[own]).reshape(SAMPLES, NT0 * NP0)
        high = full.astype(ml_dtypes.bfloat16)
        fold[g, :SAMPLES] = high
        fold[g, SAMPLES:] = (full - high.astype(np.float64)).astype(ml_dtypes.bfloat16)
        along_column = np.sin(polar)[:, None] * np.cos(azimuth[own])[None, :]
        along_row = np.sin(polar)[:, None] * np.sin(azimuth[own])[None, :]
        for child in range(2):
            psi = math.pi * (along_column * (child - 0.5) - along_row * 0.5)
            phase[g, :, 2 * child] = np.cos(psi).reshape(-1)
            phase[g, :, 2 * child + 1] = np.sin(psi).reshape(-1)
    return fold, phase


def split(x):
    high = x.astype(BF16)
    low = (x - high.astype(F32)).astype(BF16)
    return high, low


def iota(shape, dim):
    return lax.broadcasted_iota(jnp.int32, shape, dim)


def dot(a, b):
    return jnp.dot(a, b, preferred_element_type=F32)


def dot_nt(a, b):
    return lax.dot_general(a, b, (((1,), (1,)), ((), ())), preferred_element_type=F32)


def displacements():
    return [
        (dy, dx) for dy in range(-3, 4) for dx in range(-3, 4) if max(abs(dy), abs(dx)) >= 2
    ]


def translated(parents, ta, tb):
    numbers = {pair: number for number, pair in enumerate(displacements())}
    first = [jnp.zeros((4, PSIDE, 128), F32) for _ in range(2)]
    second = [jnp.zeros((4, PSIDE, 128), F32) for _ in range(2)]
    odd_column = (iota((8, 2, PSIDE, 128), 2) & 1) == 1
    for dx in range(-3, 4):
        tile = parents[:, 8 + dx : 16 + dx, :].reshape(8, 2, PSIDE, 128)
        if dx == -3:
            tile = jnp.where(odd_column, tile, 0.0)
        if dx == 3:
            tile = jnp.where(odd_column, 0.0, tile)
        for dy in range(-3, 4):
            if (dy, dx) not in numbers:
                continue
            number = numbers[dy, dx]
            wa = ta[number : number + 1, :].reshape(1, 1, 128)
            wb = tb[number : number + 1, :].reshape(1, 1, 128)
            for parity in range(2):
                if dy == (-3 if parity == 0 else 3):
                    continue
                start = 4 + dy + parity
                source = tile[start // 2 : start // 2 + 4, start % 2]
                first[parity] = first[parity] + wa * source
                second[parity] = second[parity] + wb * source
    first = jnp.stack(first, axis=1).reshape(64, 128)
    second = jnp.stack(second, axis=1).reshape(64, 128)
    return first + pltpu.roll(second, 64, 1)


def kernel(
    across,
    code_hbm,
    count_ref,
    cur_hbm,
    rad_hbm,
    near_hbm,
    trans_hbm,
    fold_hbm,
    phase_hbm,
    out_ref,
    code_ref,
    cur,
    rad,
    near,
    trans,
    fold,
    phase,
    ops,
    ta,
    tb,
    field,
    side,
    mats,
    ext,
    index_col,
    load_sem,
    fs_sem,
    fr_sem,
    ts_sem,
    tr_sem,
    next_sem,
    above_sem,
):
    block = lax.axis_index("box")
    group = lax.axis_index("dir")
    row = block // across
    col = block % across

    loads = []
    for number, (source, target) in enumerate(
        (
            (trans_hbm, trans),
            (code_hbm, code_ref),
            (cur_hbm, cur),
            (rad_hbm, rad),
            (fold_hbm, fold),
            (phase_hbm, phase),
            (near_hbm, near),
        )
    ):
        copy = pltpu.make_async_copy(source, target, load_sem.at[number])
        copy.start()
        loads.append(copy)

    def rank(r, c):
        return jnp.where(2 * r < across, r, 3 * across // 2 - 1 - r) * across + (c ^ 1)

    def beside(number):
        dr, dc = STEPS[number]
        r, c = row + dr, col + dc
        there = (r >= 0) & (r < across) & (c >= 0) & (c < across)
        return there, rank(r, c) < rank(row, col), (r * across + c, group)

    def peer(other):
        return (block, other)

    barrier = pltpu.get_barrier_semaphore()
    earlier = group
    for number in range(8):
        there, before, device = beside(number)

        @pl.when(there & jnp.logical_not(before))
        def _():
            pl.semaphore_signal(barrier, inc=1, device_id=device, device_id_type=MESH)

        earlier = earlier + jnp.where(there & before, 1, 0)
    for other in range(GROUPS):

        @pl.when(other > group)
        def _():
            pl.semaphore_signal(barrier, inc=1, device_id=peer(other), device_id_type=MESH)

    loads[0].wait()
    ops[group] = jnp.transpose(trans[...])

    @pl.when(earlier > 0)
    def _():
        pl.semaphore_wait(barrier, earlier)

    def send_ops(other):
        return pltpu.make_async_remote_copy(
            src_ref=ops.at[group],
            dst_ref=ops.at[group],
            send_sem=ts_sem.at[other],
            recv_sem=tr_sem.at[group],
            device_id=peer(other),
            device_id_type=MESH,
        )

    for other in range(GROUPS):

        @pl.when(other < group)
        def _():
            pl.semaphore_signal(
                above_sem.at[group], inc=1, device_id=peer(other), device_id_type=MESH
            )
            send_ops(other).start()

    for number in range(8):
        there, before, device = beside(number)

        @pl.when(there & before)
        def _():
            pl.semaphore_signal(
                next_sem.at[number ^ 1], inc=1, device_id=device, device_id_type=MESH
            )

    loads[1].wait()
    code = code_ref[...]
    across_c = ((code >> 2) & 1) + ((code >> 4) & 1) * 2 + ((code >> 6) & 1) * 4
    down_r = ((code >> 3) & 1) + ((code >> 5) & 1) * 2 + ((code >> 7) & 1) * 4
    index_row = (code & 3) * 64 + down_r * 8 + across_c
    live_index = jnp.where(iota((1, CELLS), 1) < count_ref[0], index_row, -1)
    line = iota((128, CELLS), 0)
    beyond = line - 64
    wanted = jnp.where(
        line < 64, line, ((beyond & 31) >> 2) * 8 + (beyond >> 5) * 4 + (beyond & 3)
    )
    loads[2].wait()
    place = jnp.concatenate(
        [
            jnp.where(wanted == live_index - child * 64, 1.0, 0.0).astype(BF16)
            for child in range(4)
        ],
        axis=0,
    )
    placed = dot_nt(place, cur[...]).astype(BF16).reshape(4, 128, 256)
    field[:, 0:64, :] = placed[:, :64]
    side[...] = placed[:, 64:]

    def send_field(number, device):
        buffer, start, size, target = PIECES[number]
        source = field if buffer == "own" else side
        return pltpu.make_async_remote_copy(
            src_ref=source.at[:, pl.ds(start, size), :],
            dst_ref=field.at[:, pl.ds(target, size), :],
            send_sem=fs_sem.at[number],
            recv_sem=fr_sem.at[number],
            device_id=device,
            device_id_type=MESH,
        )

    for first in (True, False):
        for number in range(8):
            there, before, device = beside(number)

            @pl.when(there & (before if first else jnp.logical_not(before)))
            def _():
                if not first:
                    pl.semaphore_wait(next_sem.at[number], 1)
                send_field(number, device).start()

    for edge, pieces in (
        (row == 0, ((64, 32), (192, 32))),
        (row == across - 1, ((96, 32), (224, 32))),
        (col == 0, ((128, 32), (192, 16), (224, 16))),
        (col == across - 1, ((160, 32), (208, 16), (240, 16))),
    ):

        @pl.when(edge)
        def _():
            for start, size in pieces:
                field[:, start : start + size, :] = jnp.zeros((4, size, 256), BF16)

    loads[3].wait()
    loads[4].wait()
    loads[5].wait()

    def prepare(g, _):
        weights = fold[pl.ds(pl.multiple_of(g * 128, 128), 128), :]
        rr = dot(weights, rad[0:128, :])
        ri = dot(weights, rad[128:256, :])
        rr = rr[:64] + rr[64:]
        ri = ri[:64] + ri[64:]
        turns = phase[g]
        total = jnp.zeros((64, 256), F32)
        for pair in range(2):
            cosine = turns[:, 2 * pair : 2 * pair + 1]
            sine = turns[:, 2 * pair + 1 : 2 * pair + 2]
            cr, ci, sr, si = cosine * rr, cosine * ri, sine * rr, sine * ri
            for child, ar, ai in ((pair, cr + si, ci - sr), (3 - pair, cr - si, ci + sr)):
                arh, arl = split(ar)
                aih, ail = split(ai)
                matrix = jnp.concatenate(
                    [
                        jnp.concatenate([arh, -aih], axis=1),
                        jnp.concatenate([aih, arh], axis=1),
                        jnp.concatenate([arl, -ail], axis=1),
                        jnp.concatenate([ail, arl], axis=1),
                    ],
                    axis=0,
                )
                mats[g, child] = matrix
                total = total + dot_nt(field[child, 0:64, :], matrix)
        total = total[:, :128] + total[:, 128:]
        ext[g, 4:12, 8:16, :] = total.reshape(PSIDE, PSIDE, 128)
        return 0

    lax.fori_loop(0, GROUPS, prepare, 0)

    index_col[...] = jnp.transpose(jnp.broadcast_to(index_row, (128, CELLS)))
    own_index = index_col[pl.ds(pl.multiple_of(group * OWN, OWN), OWN), :]
    pick = jnp.concatenate(
        [
            jnp.where(own_index[:, :64] == iota((OWN, 64), 1) + child * 64, 1.0, 0.0).astype(BF16)
            for child in range(4)
        ],
        axis=0,
    )
    own_r = ((own_index >> 3) & 7) * 2 + (own_index >> 7)
    own_c = (own_index & 7) * 2 + ((own_index >> 6) & 1)
    hot = []
    for dr in (-1, 0, 1):
        for dc in (-1, 0, 1):
            r, c = own_r + dr, own_c + dc
            child = (r & 1) * 2 + (c & 1)
            pr, pc = r >> 1, c >> 1
            north, south, west, east = pr < 0, pr > 7, pc < 0, pc > 7
            at = jnp.where(west, 131 + pr * 4, jnp.where(east, 160 + pr * 4, pr * 8 + pc))
            at = jnp.where(north, jnp.where(west, 207, jnp.where(east, 220, 88 + pc)), at)
            at = jnp.where(south, jnp.where(west, 227, jnp.where(east, 240, 96 + pc)), at)
            at = at + child * 256
            hot.append(
                jnp.concatenate(
                    [
                        jnp.where(at == iota((OWN, 128), 1) + start, 1.0, 0.0).astype(BF16)
                        for start in range(0, 1024, 128)
                    ],
                    axis=1,
                )
            )
    hot = jnp.concatenate(hot, axis=0)

    def send_up():
        for other in range(1, GROUPS):

            @pl.when(other > group)
            def _():
                pl.semaphore_wait(above_sem.at[other], 1)
                send_ops(other).start()

    pl.when(2 * group >= GROUPS)(send_up)
    for number in range(8):
        there, _, device = beside(number ^ 1)

        @pl.when(there)
        def _():
            send_field(number, device).wait_recv()

    around = dot(hot, field[...].reshape(1024, 256)).astype(BF16)
    loads[6].wait()
    close = jnp.zeros((2 * OWN, 256), F32)
    for number in range(9):
        mine = around[number * OWN : (number + 1) * OWN]
        stacked = jnp.concatenate([mine[:, :128], mine[:, 128:]], axis=0)
        close = close + dot_nt(stacked, near[pl.ds(number * 256, 256), :])

    def rim(g, _):
        total = jnp.zeros((192, 256), F32)
        for child in range(4):
            total = total + dot_nt(field[child, 64:256, :], mats[g, child])
        total = total[:, :128] + total[:, 128:]
        ext[g, 0:4, 8:16, :] = total[0:32].reshape(4, 8, 128)
        ext[g, 12:16, 8:16, :] = total[32:64].reshape(4, 8, 128)
        for r in range(8):
            ext[g, 4 + r, 4:8, :] = total[64 + 4 * r : 68 + 4 * r]
            ext[g, 4 + r, 16:20, :] = total[96 + 4 * r : 100 + 4 * r]
        for r in range(4):
            ext[g, r, 4:8, :] = total[128 + 4 * r : 132 + 4 * r]
            ext[g, r, 16:20, :] = total[144 + 4 * r : 148 + 4 * r]
            ext[g, 12 + r, 4:8, :] = total[160 + 4 * r : 164 + 4 * r]
            ext[g, 12 + r, 16:20, :] = total[176 + 4 * r : 180 + 4 * r]
        return 0

    lax.fori_loop(0, GROUPS, rim, 0)
    pl.when(2 * group < GROUPS)(send_up)

    left = iota((DISP, 128), 1) < 64
    far = jnp.zeros((2 * OWN, 256), F32)
    for stage in range(0, GROUPS, STAGE):
        for g in range(stage, stage + STAGE):

            @pl.when(g != group)
            def _():
                pltpu.make_async_remote_copy(
                    src_ref=ops.at[g],
                    dst_ref=ops.at[g],
                    send_sem=ts_sem.at[g],
                    recv_sem=tr_sem.at[g],
                    device_id=peer(g),
                    device_id_type=MESH,
                ).wait_recv()

        for g in range(stage, stage + STAGE):
            here = ops[g]
            turned = pltpu.roll(here, 64, 1)
            ta[g] = jnp.where(left, here, turned)
            tb[g] = jnp.where(left, turned, -here)
            high, low = split(translated(ext.at[g], ta.at[g], tb.at[g]))
            chosen = dot(pick, jnp.concatenate([high, low], axis=1)).astype(BF16)
            for child in range(4):
                mine = chosen[child * OWN : (child + 1) * OWN]
                high, low = mine[:, :128], mine[:, 128:]
                stacked = jnp.concatenate(
                    [
                        jnp.concatenate([high, high], axis=1),
                        jnp.concatenate([low, jnp.zeros_like(low)], axis=1),
                    ],
                    axis=0,
                )
                far = far + dot(stacked, mats[g, child])

    live = iota((OWN, 128), 0) + group * OWN < count_ref[0]
    far = 0.25 * (far[:OWN] + far[OWN:])
    real = far[:, :128] + (close[:OWN, :128] - close[OWN:, 128:])
    imag = far[:, 128:] + (close[OWN:, :128] + close[:OWN, 128:])
    out_ref[0] = jnp.where(live, real, 0.0).astype(BF16)
    out_ref[1] = jnp.where(live, imag, 0.0).astype(BF16)

    for number in range(8):
        there, _, device = beside(number)

        @pl.when(there)
        def _():
            send_field(number, device).wait_send()

    for other in range(GROUPS):

        @pl.when(other != group)
        def _():
            send_ops(other).wait_send()


def on_device(across, tables, currents, box_code, box_count, radiation, near_block, translation):
    fold, phase = tables
    operands = (
        box_code.reshape(1, CELLS),
        box_count,
        currents.reshape(2 * U, CELLS),
        radiation.reshape(2 * 128, U),
        near_block.reshape(9 * 2 * U, U),
        jnp.transpose(translation, (1, 2, 3, 0)).reshape(128, DISP),
        jnp.asarray(fold).reshape(GROUPS * 128, 128),
        jnp.asarray(phase),
    )
    outside = pl.BlockSpec(memory_space=pltpu.HBM)
    result = pl.pallas_call(
        functools.partial(kernel, across),
        out_shape=jax.ShapeDtypeStruct((2, OWN, U), BF16),
        in_specs=[outside, pl.BlockSpec(memory_space=pltpu.SMEM)] + [outside] * 6,
        out_specs=pl.BlockSpec(memory_space=pltpu.VMEM),
        scratch_shapes=[
            pltpu.VMEM((1, CELLS), jnp.int32),
            pltpu.VMEM((256, 256), BF16),
            pltpu.VMEM((256, 128), BF16),
            pltpu.VMEM((9 * 256, 128), BF16),
            pltpu.VMEM((128, DISP), F32),
            pltpu.VMEM((GROUPS * 128, 128), BF16),
            pltpu.VMEM((GROUPS, SAMPLES, 128), F32),
            pltpu.VMEM((GROUPS, DISP, 128), F32),
            pltpu.VMEM((GROUPS, DISP, 128), F32),
            pltpu.VMEM((GROUPS, DISP, 128), F32),
            pltpu.VMEM((4, 256, 256), BF16),
            pltpu.VMEM((4, 64, 256), BF16),
            pltpu.VMEM((GROUPS, 4, 256, 256), BF16),
            pltpu.VMEM((GROUPS, 16, 24, 128), F32),
            pltpu.VMEM((CELLS, 128), jnp.int32),
            pltpu.SemaphoreType.DMA((7,)),
            pltpu.SemaphoreType.DMA((8,)),
            pltpu.SemaphoreType.DMA((8,)),
            pltpu.SemaphoreType.DMA((GROUPS,)),
            pltpu.SemaphoreType.DMA((GROUPS,)),
            pltpu.SemaphoreType.REGULAR((8,)),
            pltpu.SemaphoreType.REGULAR((GROUPS,)),
        ],
        compiler_params=pltpu.CompilerParams(
            collective_id=0, has_side_effects=True, vmem_limit_bytes=48 * 1024 * 1024
        ),
    )(*(pltpu.with_memory_space_constraint(x, pltpu.HBM) if x.size > 1 else x for x in operands))
    return jnp.transpose(result, (0, 2, 1))


def solution(mesh):
    across = math.isqrt(mesh.shape["box"])
    tables = make_tables()

    def step(*arrays):
        return on_device(across, tables, *arrays)

    placed = (P(None, None, "box"), P("box"), P("box"), P(), P(), P(None, None, None, "dir"))
    return jax.shard_map(
        step,
        mesh=mesh,
        in_specs=placed,
        out_specs=P(None, None, ("box", "dir")),
        check_vma=False,
    )
```

```python
import functools
import math

import jax
import jax.numpy as jnp
import ml_dtypes
import numpy as np
from jax import lax
from jax.experimental import pallas as pl
from jax.experimental.pallas import tpu as pltpu
from jax.sharding import PartitionSpec as P

U = 128
NT0 = 8
NP0 = 16
NT1 = 16
NP1 = 32
PSIDE = 8
CELLS = 256
GROUPS = 8
QL = NP1 // GROUPS
SAMPLES = NT1 * QL
OWN = CELLS // GROUPS
DISP = 40
EARLY = 3
MESH = pl.DeviceIdType.MESH
F32 = jnp.float32
BF16 = jnp.bfloat16

STEPS = ((1, 1), (-1, -1), (1, -1), (-1, 1), (1, 0), (-1, 0), (0, 1), (0, -1))
PIECES = (
    ("side", 48, 16, 192),
    ("side", 0, 16, 240),
    ("side", 16, 16, 208),
    ("side", 32, 16, 224),
    ("own", 32, 32, 64),
    ("own", 0, 32, 96),
    ("side", 32, 32, 128),
    ("side", 0, 32, 160),
)


def lagrange(offset, node):
    first = -(offset - 1.0) * (offset - 2.0) * (offset - 3.0) / 6.0
    second = offset * (offset - 2.0) * (offset - 3.0) / 2.0
    third = -offset * (offset - 1.0) * (offset - 3.0) / 2.0
    fourth = offset * (offset - 1.0) * (offset - 2.0) / 6.0
    return (
        np.where(node == 0, first, 0.0)
        + np.where(node == 1, second, 0.0)
        + np.where(node == 2, third, 0.0)
        + np.where(node == 3, fourth, 0.0)
    )


def make_tables():
    coarse = np.arange(NT1)[:, None]
    twice = 2 * coarse - 1
    base = np.clip(twice // 4 - 1, 0, NT0 - 4)
    theta = lagrange((twice - 4 * base) / 4.0, np.arange(NT0)[None, :] - base)
    coarse = np.arange(NP1)[:, None]
    twice = 2 * coarse - 1
    base = twice // 4 - 1
    phi = lagrange((twice - 4 * base) / 4.0, (np.arange(NP0)[None, :] - base) % NP0)
    polar = (np.arange(NT1) + 0.5) * math.pi / NT1
    azimuth = (np.arange(NP1) + 0.5) * 2.0 * math.pi / NP1
    fold = np.zeros((GROUPS, 2 * SAMPLES, NT0 * NP0), ml_dtypes.bfloat16)
    phase = np.zeros((GROUPS, SAMPLES, 128), np.float32)
    turn = np.zeros((GROUPS, 8, 2, SAMPLES), np.float32)
    for g in range(GROUPS):
        own = np.arange(g * QL, (g + 1) * QL)
        full = np.einsum("it,qp->iqtp", theta, phi[own]).reshape(SAMPLES, NT0 * NP0)
        high = full.astype(ml_dtypes.bfloat16)
        fold[g, :SAMPLES] = high
        fold[g, SAMPLES:] = (full - high.astype(np.float64)).astype(ml_dtypes.bfloat16)
        along_column = np.sin(polar)[:, None] * np.cos(azimuth[own])[None, :]
        along_row = np.sin(polar)[:, None] * np.sin(azimuth[own])[None, :]
        for child in range(2):
            psi = math.pi * (along_column * (child - 0.5) - along_row * 0.5)
            phase[g, :, 2 * child] = np.cos(psi).reshape(-1)
            phase[g, :, 2 * child + 1] = np.sin(psi).reshape(-1)
            turn[g, 2 * child] = np.cos(psi).reshape(-1)
            turn[g, 2 * child + 1, 0] = -np.sin(psi).reshape(-1)
            turn[g, 2 * child + 1, 1] = np.sin(psi).reshape(-1)
    return fold, phase, turn


def split(x):
    high = x.astype(BF16)
    low = (x - high.astype(F32)).astype(BF16)
    return high, low


def iota(shape, dim):
    return lax.broadcasted_iota(jnp.int32, shape, dim)


def dot(a, b):
    return jnp.dot(a, b, preferred_element_type=F32)


def dot_nt(a, b):
    return lax.dot_general(a, b, (((1,), (1,)), ((), ())), preferred_element_type=F32)


def displacements():
    return [
        (dy, dx) for dy in range(-3, 4) for dx in range(-3, 4) if max(abs(dy), abs(dx)) >= 2
    ]


def translated(parents, ta, tb):
    numbers = {pair: number for number, pair in enumerate(displacements())}
    first = [jnp.zeros((4, PSIDE, 128), F32) for _ in range(2)]
    second = [jnp.zeros((4, PSIDE, 128), F32) for _ in range(2)]
    odd_column = (iota((8, 2, PSIDE, 128), 2) & 1) == 1
    for dx in range(-3, 4):
        tile = parents[:, 8 + dx : 16 + dx, :].reshape(8, 2, PSIDE, 128)
        if dx == -3:
            tile = jnp.where(odd_column, tile, 0.0)
        if dx == 3:
            tile = jnp.where(odd_column, 0.0, tile)
        for dy in range(-3, 4):
            if (dy, dx) not in numbers:
                continue
            number = numbers[dy, dx]
            wa = ta[number : number + 1, :].reshape(1, 1, 128)
            wb = tb[number : number + 1, :].reshape(1, 1, 128)
            for parity in range(2):
                if dy == (-3 if parity == 0 else 3):
                    continue
                start = 4 + dy + parity
                source = tile[start // 2 : start // 2 + 4, start % 2]
                first[parity] = first[parity] + wa * source
                second[parity] = second[parity] + wb * source
    first = jnp.stack(first, axis=1).reshape(64, 128)
    second = jnp.stack(second, axis=1).reshape(64, 128)
    return first + pltpu.roll(second, 64, 1)


def kernel(
    across,
    code_hbm,
    count_ref,
    cur_hbm,
    rad_hbm,
    near_hbm,
    trans_hbm,
    fold_hbm,
    phase_hbm,
    turn_hbm,
    out_ref,
    code_ref,
    cur,
    rad,
    near,
    trans,
    fold,
    phase,
    turn,
    ops,
    ta,
    tb,
    field,
    side,
    mats,
    base,
    found,
    ext,
    index_col,
    load_sem,
    fs_sem,
    fr_sem,
    ts_sem,
    tr_sem,
    next_sem,
    above_sem,
):
    block = lax.axis_index("box")
    group = lax.axis_index("dir")
    row = block // across
    col = block % across

    loads = []
    for number, (source, target) in enumerate(
        (
            (trans_hbm, trans),
            (code_hbm, code_ref),
            (cur_hbm, cur),
            (rad_hbm, rad),
            (fold_hbm, fold),
            (phase_hbm, phase),
            (near_hbm, near),
            (turn_hbm, turn),
        )
    ):
        copy = pltpu.make_async_copy(source, target, load_sem.at[number])
        loads.append(copy)

    loads[0].start()

    def rank(r, c):
        return jnp.where(2 * r < across, r, 3 * across // 2 - 1 - r) * across + (c ^ 1)

    def beside(number):
        dr, dc = STEPS[number]
        r, c = row + dr, col + dc
        there = (r >= 0) & (r < across) & (c >= 0) & (c < across)
        return there, rank(r, c) < rank(row, col), (r * across + c, group)

    def peer(other):
        return (block, other)

    barrier = pltpu.get_barrier_semaphore()
    earlier = group
    for number in range(8):
        there, before, device = beside(number)

        @pl.when(there & jnp.logical_not(before))
        def _():
            pl.semaphore_signal(barrier, inc=1, device_id=device, device_id_type=MESH)

        earlier = earlier + jnp.where(there & before, 1, 0)
    for other in range(GROUPS):

        @pl.when(other > group)
        def _():
            pl.semaphore_signal(barrier, inc=1, device_id=peer(other), device_id_type=MESH)

    for copy in loads[1:]:
        copy.start()

    @pl.when(earlier > 0)
    def _():
        pl.semaphore_wait(barrier, earlier)

    for other in range(GROUPS):

        @pl.when(other < group)
        def _():
            pl.semaphore_signal(
                above_sem.at[group], inc=1, device_id=peer(other), device_id_type=MESH
            )

    for number in range(8):
        there, before, device = beside(number)

        @pl.when(there & before)
        def _():
            pl.semaphore_signal(
                next_sem.at[number ^ 1], inc=1, device_id=device, device_id_type=MESH
            )

    loads[0].wait()
    ops[group] = jnp.transpose(trans[...])

    def send_ops(other):
        return pltpu.make_async_remote_copy(
            src_ref=ops.at[group],
            dst_ref=ops.at[group],
            send_sem=ts_sem.at[other],
            recv_sem=tr_sem.at[group],
            device_id=peer(other),
            device_id_type=MESH,
        )

    for other in range(GROUPS):

        @pl.when(other < group)
        def _():
            send_ops(other).start()

    loads[1].wait()
    code = code_ref[...]
    across_c = ((code >> 2) & 1) + ((code >> 4) & 1) * 2 + ((code >> 6) & 1) * 4
    down_r = ((code >> 3) & 1) + ((code >> 5) & 1) * 2 + ((code >> 7) & 1) * 4
    index_row = (code & 3) * 64 + down_r * 8 + across_c
    live_index = jnp.where(iota((1, CELLS), 1) < count_ref[0], index_row, -1)
    line = iota((128, CELLS), 0)
    beyond = line - 64
    wanted = jnp.where(
        line < 64, line, ((beyond & 31) >> 2) * 8 + (beyond >> 5) * 4 + (beyond & 3)
    )
    loads[2].wait()
    place = jnp.concatenate(
        [
            jnp.where(wanted == live_index - child * 64, 1.0, 0.0).astype(BF16)
            for child in range(4)
        ],
        axis=0,
    )
    placed = dot_nt(place, cur[...]).astype(BF16)
    for child in range(4):
        field[0:64, pl.ds(child * 256, 256)] = placed[child * 128 : child * 128 + 64]
        side[:, pl.ds(child * 256, 256)] = placed[child * 128 + 64 : child * 128 + 128]

    def send_field(number, device):
        buffer, start, size, target = PIECES[number]
        source = field if buffer == "own" else side
        return pltpu.make_async_remote_copy(
            src_ref=source.at[pl.ds(start, size)],
            dst_ref=field.at[pl.ds(target, size)],
            send_sem=fs_sem.at[number],
            recv_sem=fr_sem.at[number],
            device_id=device,
            device_id_type=MESH,
        )

    def send_fields(numbers, first):
        for number in numbers:
            there, before, device = beside(number)

            @pl.when(there & (before if first else jnp.logical_not(before)))
            def _():
                if not first:
                    pl.semaphore_wait(next_sem.at[number], 1)
                send_field(number, device).start()

    send_fields(range(8), True)

    for edge, pieces in (
        (row == 0, ((64, 32), (192, 32))),
        (row == across - 1, ((96, 32), (224, 32))),
        (col == 0, ((128, 32), (192, 16), (224, 16))),
        (col == across - 1, ((160, 32), (208, 16), (240, 16))),
    ):

        @pl.when(edge)
        def _():
            for start, size in pieces:
                field[start : start + size, :] = jnp.zeros((size, 1024), BF16)
    loads[3].wait()
    loads[4].wait()
    loads[5].wait()

    def prepare(g):
        weights = fold[pl.ds(g * 128, 128), :]
        rr = dot(weights, rad[0:128, :])
        ri = dot(weights, rad[128:256, :])
        rr = rr[:64] + rr[64:]
        ri = ri[:64] + ri[64:]
        rrh, rrl = split(rr)
        rih, ril = split(ri)
        base[pl.ds(g * 256, 64), :] = jnp.concatenate([rrh, -rih], axis=1)
        base[pl.ds(g * 256 + 64, 64), :] = jnp.concatenate([rih, rrh], axis=1)
        base[pl.ds(g * 256 + 128, 64), :] = jnp.concatenate([rrl, -ril], axis=1)
        base[pl.ds(g * 256 + 192, 64), :] = jnp.concatenate([ril, rrl], axis=1)
        turns = phase[g]
        for pair in range(2):
            cosine = turns[:, 2 * pair : 2 * pair + 1]
            sine = turns[:, 2 * pair + 1 : 2 * pair + 2]
            cr, ci, sr, si = cosine * rr, cosine * ri, sine * rr, sine * ri
            for child, ar, ai in ((pair, cr + si, ci - sr), (3 - pair, cr - si, ci + sr)):
                arh, arl = split(ar)
                aih, ail = split(ai)
                matrix = jnp.concatenate(
                    [
                        jnp.concatenate([arh, -aih], axis=1),
                        jnp.concatenate([aih, arh], axis=1),
                        jnp.concatenate([arl, -ail], axis=1),
                        jnp.concatenate([ail, arl], axis=1),
                    ],
                    axis=0,
                )
                mats[g, :, pl.ds(child * 256, 256)] = matrix
        total = dot_nt(field[0:64, :], mats[g])
        total = total[:, :128] + total[:, 128:]
        ext[g, 4:12, 8:16, :] = total.reshape(PSIDE, PSIDE, 128)

    for g in range(GROUPS):
        if g == EARLY:
            send_fields((0, 1, 2, 3, 4, 5), False)
        prepare(g)
    send_fields((6, 7), False)
    index_col[...] = jnp.transpose(jnp.broadcast_to(index_row, (128, CELLS)))
    own_index = index_col[pl.ds(pl.multiple_of(group * OWN, OWN), OWN), :]
    pick = jnp.where((own_index[:, :64] & 63) == iota((OWN, 64), 1), 1.0, 0.0).astype(BF16)
    own_child = own_index >> 6
    own_r = ((own_index >> 3) & 7) * 2 + (own_index >> 7)
    own_c = (own_index & 7) * 2 + ((own_index >> 6) & 1)
    hot = []
    for dr in (-1, 0, 1):
        for dc in (-1, 0, 1):
            r, c = own_r + dr, own_c + dc
            child = (r & 1) * 2 + (c & 1)
            pr, pc = r >> 1, c >> 1
            north, south, west, east = pr < 0, pr > 7, pc < 0, pc > 7
            at = jnp.where(west, 131 + pr * 4, jnp.where(east, 160 + pr * 4, pr * 8 + pc))
            at = jnp.where(north, jnp.where(west, 207, jnp.where(east, 220, 88 + pc)), at)
            at = jnp.where(south, jnp.where(west, 227, jnp.where(east, 240, 96 + pc)), at)
            at = at + child * 256
            hot.append(
                jnp.concatenate(
                    [
                        jnp.where(at == iota((OWN, 128), 1) + start, 1.0, 0.0).astype(BF16)
                        for start in range(0, 1024, 128)
                    ],
                    axis=1,
                )
            )
    hot = jnp.concatenate(hot, axis=0)
    def send_up():
        for other in range(1, GROUPS):

            @pl.when(other > group)
            def _():
                pl.semaphore_wait(above_sem.at[other], 1)
                send_ops(other).start()

    send_up()
    for number in range(8):
        there, _, device = beside(number ^ 1)

        @pl.when(there)
        def _():
            send_field(number, device).wait_recv()

    around = jnp.zeros((9 * OWN, 256), F32)
    for child in range(4):
        lanes = pl.ds(child * 256, 256)
        around = around + dot(hot[:, child * 256 : (child + 1) * 256], field[:, lanes])
    around = around.astype(BF16)
    loads[6].wait()
    loads[7].wait()
    close = jnp.zeros((2 * OWN, 256), F32)
    for number in range(9):
        mine = around[number * OWN : (number + 1) * OWN]
        stacked = jnp.concatenate([mine[:, :128], mine[:, 128:]], axis=0)
        close = close + dot_nt(stacked, near[pl.ds(number * 256, 256), :])
    def rim(g):
        total = dot_nt(field[64:256, :], mats[g])
        total = total[:, :128] + total[:, 128:]
        ext[g, 0:4, 8:16, :] = total[0:32].reshape(4, 8, 128)
        ext[g, 12:16, 8:16, :] = total[32:64].reshape(4, 8, 128)
        for r in range(8):
            ext[g, 4 + r, 4:8, :] = total[64 + 4 * r : 68 + 4 * r]
            ext[g, 4 + r, 16:20, :] = total[96 + 4 * r : 100 + 4 * r]
        for r in range(4):
            ext[g, r, 4:8, :] = total[128 + 4 * r : 132 + 4 * r]
            ext[g, r, 16:20, :] = total[144 + 4 * r : 148 + 4 * r]
            ext[g, 12 + r, 4:8, :] = total[160 + 4 * r : 164 + 4 * r]
            ext[g, 12 + r, 16:20, :] = total[176 + 4 * r : 180 + 4 * r]

    for g in range(GROUPS):
        rim(g)
    left = iota((DISP, 128), 1) < 64
    for g in range(GROUPS):

        @pl.when(g != group)
        def _():
            pltpu.make_async_remote_copy(
                src_ref=ops.at[g],
                dst_ref=ops.at[g],
                send_sem=ts_sem.at[g],
                recv_sem=tr_sem.at[g],
                device_id=peer(g),
                device_id_type=MESH,
            ).wait_recv()

        here = ops[g]
        turned = pltpu.roll(here, 64, 1)
        ta[g] = jnp.where(left, here, turned)
        tb[g] = jnp.where(left, turned, -here)
        high, low = split(translated(ext.at[g], ta.at[g], tb.at[g]))
        found[:, g * 256 : g * 256 + 128] = high
        found[:, g * 256 + 128 : g * 256 + 256] = low

    chosen = dot(pick, found[...])
    outer = (own_child == 0) | (own_child == 3)
    upper = own_child < 2
    tops, bottoms = [], []
    for g in range(GROUPS):
        value = chosen[:, g * 256 : g * 256 + 128] + chosen[:, g * 256 + 128 : g * 256 + 256]
        cosine = jnp.where(outer, turn[g, 0:1, :], turn[g, 2:3, :])
        sine = jnp.where(outer, turn[g, 1:2, :], turn[g, 3:4, :])
        sine = jnp.where(upper, sine, -sine)
        high, low = split(cosine * value + sine * pltpu.roll(value, 64, 1))
        tops += [high, high]
        bottoms += [low, jnp.zeros_like(low)]
    stacked = jnp.concatenate(
        [jnp.concatenate(tops, axis=1), jnp.concatenate(bottoms, axis=1)], axis=0
    )
    far = dot(stacked, base[...])

    live = iota((OWN, 128), 0) + group * OWN < count_ref[0]
    far = 0.25 * (far[:OWN] + far[OWN:])
    real = far[:, :128] + (close[:OWN, :128] - close[OWN:, 128:])
    imag = far[:, 128:] + (close[OWN:, :128] + close[:OWN, 128:])
    out_ref[0] = jnp.where(live, real, 0.0).astype(BF16)
    out_ref[1] = jnp.where(live, imag, 0.0).astype(BF16)

    for number in range(8):
        there, _, device = beside(number)

        @pl.when(there)
        def _():
            send_field(number, device).wait_send()

    for other in range(GROUPS):

        @pl.when(other != group)
        def _():
            send_ops(other).wait_send()


def on_device(across, tables, currents, box_code, box_count, radiation, near_block, translation):
    fold, phase, turn = tables
    operands = (
        box_code.reshape(1, CELLS),
        box_count,
        currents.reshape(2 * U, CELLS),
        radiation.reshape(2 * 128, U),
        near_block.reshape(9 * 2 * U, U),
        jnp.transpose(translation, (1, 2, 3, 0)).reshape(128, DISP),
        jnp.asarray(fold).reshape(GROUPS * 128, 128),
        jnp.asarray(phase),
        jnp.asarray(turn).reshape(GROUPS, 8, 128),
    )
    outside = pl.BlockSpec(memory_space=pltpu.HBM)
    result = pl.pallas_call(
        functools.partial(kernel, across),
        out_shape=jax.ShapeDtypeStruct((2, OWN, U), BF16),
        in_specs=[outside, pl.BlockSpec(memory_space=pltpu.SMEM)] + [outside] * 7,
        out_specs=pl.BlockSpec(memory_space=pltpu.VMEM),
        scratch_shapes=[
            pltpu.VMEM((1, CELLS), jnp.int32),
            pltpu.VMEM((256, 256), BF16),
            pltpu.VMEM((256, 128), BF16),
            pltpu.VMEM((9 * 256, 128), BF16),
            pltpu.VMEM((128, DISP), F32),
            pltpu.VMEM((GROUPS * 128, 128), BF16),
            pltpu.VMEM((GROUPS, SAMPLES, 128), F32),
            pltpu.VMEM((GROUPS, 8, 128), F32),
            pltpu.VMEM((GROUPS, DISP, 128), F32),
            pltpu.VMEM((GROUPS, DISP, 128), F32),
            pltpu.VMEM((GROUPS, DISP, 128), F32),
            pltpu.VMEM((256, 1024), BF16),
            pltpu.VMEM((64, 1024), BF16),
            pltpu.VMEM((GROUPS, 256, 1024), BF16),
            pltpu.VMEM((GROUPS * 256, 256), BF16),
            pltpu.VMEM((64, GROUPS * 256), BF16),
            pltpu.VMEM((GROUPS, 16, 24, 128), F32),
            pltpu.VMEM((CELLS, 128), jnp.int32),
            pltpu.SemaphoreType.DMA((8,)),
            pltpu.SemaphoreType.DMA((8,)),
            pltpu.SemaphoreType.DMA((8,)),
            pltpu.SemaphoreType.DMA((GROUPS,)),
            pltpu.SemaphoreType.DMA((GROUPS,)),
            pltpu.SemaphoreType.REGULAR((8,)),
            pltpu.SemaphoreType.REGULAR((GROUPS,)),
        ],
        compiler_params=pltpu.CompilerParams(
            collective_id=0, has_side_effects=True, vmem_limit_bytes=48 * 1024 * 1024
        ),
    )(*(pltpu.with_memory_space_constraint(x, pltpu.HBM) if x.size > 1 else x for x in operands))
    return jnp.transpose(result, (0, 2, 1))


def solution(mesh):
    across = math.isqrt(mesh.shape["box"])
    tables = make_tables()

    def step(*arrays):
        return on_device(across, tables, *arrays)

    placed = (P(None, None, "box"), P("box"), P("box"), P(), P(), P(None, None, None, "dir"))
    return jax.shard_map(
        step,
        mesh=mesh,
        in_specs=placed,
        out_specs=P(None, None, ("box", "dir")),
        check_vma=False,
    )
```

```python
import functools
import math

import jax
import jax.numpy as jnp
import ml_dtypes
import numpy as np
from jax import lax
from jax.experimental import pallas as pl
from jax.experimental.pallas import tpu as pltpu
from jax.sharding import PartitionSpec as P

U = 128
NT0 = 8
NP0 = 16
NT1 = 16
NP1 = 32
PSIDE = 8
CELLS = 256
GROUPS = 8
QL = NP1 // GROUPS
SAMPLES = NT1 * QL
OWN = CELLS // GROUPS
DISP = 40
EARLY = 3
MESH = pl.DeviceIdType.MESH
F32 = jnp.float32
BF16 = jnp.bfloat16

STEPS = ((1, 1), (-1, -1), (1, -1), (-1, 1), (1, 0), (-1, 0), (0, 1), (0, -1))
PIECES = (
    ("side", 48, 16, 192),
    ("side", 0, 16, 240),
    ("side", 16, 16, 208),
    ("side", 32, 16, 224),
    ("own", 32, 32, 64),
    ("own", 0, 32, 96),
    ("side", 32, 32, 128),
    ("side", 0, 32, 160),
)


def lagrange(offset, node):
    first = -(offset - 1.0) * (offset - 2.0) * (offset - 3.0) / 6.0
    second = offset * (offset - 2.0) * (offset - 3.0) / 2.0
    third = -offset * (offset - 1.0) * (offset - 3.0) / 2.0
    fourth = offset * (offset - 1.0) * (offset - 2.0) / 6.0
    return (
        np.where(node == 0, first, 0.0)
        + np.where(node == 1, second, 0.0)
        + np.where(node == 2, third, 0.0)
        + np.where(node == 3, fourth, 0.0)
    )


def make_tables():
    coarse = np.arange(NT1)[:, None]
    twice = 2 * coarse - 1
    base = np.clip(twice // 4 - 1, 0, NT0 - 4)
    theta = lagrange((twice - 4 * base) / 4.0, np.arange(NT0)[None, :] - base)
    coarse = np.arange(NP1)[:, None]
    twice = 2 * coarse - 1
    base = twice // 4 - 1
    phi = lagrange((twice - 4 * base) / 4.0, (np.arange(NP0)[None, :] - base) % NP0)
    polar = (np.arange(NT1) + 0.5) * math.pi / NT1
    azimuth = (np.arange(NP1) + 0.5) * 2.0 * math.pi / NP1
    fold = np.zeros((GROUPS, 2 * SAMPLES, NT0 * NP0), ml_dtypes.bfloat16)
    phase = np.zeros((GROUPS, SAMPLES, 128), np.float32)
    turn = np.zeros((GROUPS, 8, 2, SAMPLES), np.float32)
    for g in range(GROUPS):
        own = np.arange(g * QL, (g + 1) * QL)
        full = np.einsum("it,qp->iqtp", theta, phi[own]).reshape(SAMPLES, NT0 * NP0)
        high = full.astype(ml_dtypes.bfloat16)
        fold[g, :SAMPLES] = high
        fold[g, SAMPLES:] = (full - high.astype(np.float64)).astype(ml_dtypes.bfloat16)
        along_column = np.sin(polar)[:, None] * np.cos(azimuth[own])[None, :]
        along_row = np.sin(polar)[:, None] * np.sin(azimuth[own])[None, :]
        for child in range(2):
            psi = math.pi * (along_column * (child - 0.5) - along_row * 0.5)
            phase[g, :, 2 * child] = np.cos(psi).reshape(-1)
            phase[g, :, 2 * child + 1] = np.sin(psi).reshape(-1)
            turn[g, 2 * child] = np.cos(psi).reshape(-1)
            turn[g, 2 * child + 1, 0] = -np.sin(psi).reshape(-1)
            turn[g, 2 * child + 1, 1] = np.sin(psi).reshape(-1)
    return fold, phase, turn


def split(x):
    high = x.astype(BF16)
    low = (x - high.astype(F32)).astype(BF16)
    return high, low


def iota(shape, dim):
    return lax.broadcasted_iota(jnp.int32, shape, dim)


def dot(a, b):
    return jnp.dot(a, b, preferred_element_type=F32)


def dot_nt(a, b):
    return lax.dot_general(a, b, (((1,), (1,)), ((), ())), preferred_element_type=F32)


def displacements():
    return [
        (dy, dx) for dy in range(-3, 4) for dx in range(-3, 4) if max(abs(dy), abs(dx)) >= 2
    ]


def translated(parents, ta, tb):
    numbers = {pair: number for number, pair in enumerate(displacements())}
    first = [jnp.zeros((4, PSIDE, 128), F32) for _ in range(2)]
    second = [jnp.zeros((4, PSIDE, 128), F32) for _ in range(2)]
    odd_column = (iota((8, 2, PSIDE, 128), 2) & 1) == 1
    for dx in range(-3, 4):
        tile = parents[:, 8 + dx : 16 + dx, :].reshape(8, 2, PSIDE, 128)
        if dx == -3:
            tile = jnp.where(odd_column, tile, 0.0)
        if dx == 3:
            tile = jnp.where(odd_column, 0.0, tile)
        for dy in range(-3, 4):
            if (dy, dx) not in numbers:
                continue
            number = numbers[dy, dx]
            wa = ta[number : number + 1, :].reshape(1, 1, 128)
            wb = tb[number : number + 1, :].reshape(1, 1, 128)
            for parity in range(2):
                if dy == (-3 if parity == 0 else 3):
                    continue
                start = 4 + dy + parity
                source = tile[start // 2 : start // 2 + 4, start % 2]
                first[parity] = first[parity] + wa * source
                second[parity] = second[parity] + wb * source
    first = jnp.stack(first, axis=1).reshape(64, 128)
    second = jnp.stack(second, axis=1).reshape(64, 128)
    return first + pltpu.roll(second, 64, 1)


def kernel(
    across,
    code_hbm,
    count_ref,
    cur_hbm,
    rad_hbm,
    near_hbm,
    trans_hbm,
    fold_hbm,
    phase_hbm,
    turn_hbm,
    out_ref,
    code_ref,
    cur,
    rad,
    near,
    trans,
    fold,
    phase,
    turn,
    ops,
    ta,
    tb,
    field,
    side,
    mats,
    base,
    found,
    ext,
    index_col,
    load_sem,
    fs_sem,
    fr_sem,
    ts_sem,
    tr_sem,
    next_sem,
    above_sem,
):
    block = lax.axis_index("box")
    group = lax.axis_index("dir")
    row = block // across
    col = block % across

    loads = []
    for number, (source, target) in enumerate(
        (
            (trans_hbm, trans),
            (code_hbm, code_ref),
            (cur_hbm, cur),
            (rad_hbm, rad),
            (fold_hbm, fold),
            (phase_hbm, phase),
            (near_hbm, near),
            (turn_hbm, turn),
        )
    ):
        copy = pltpu.make_async_copy(source, target, load_sem.at[number])
        loads.append(copy)

    loads[0].start()

    def rank(r, c):
        usual = jnp.where(2 * r < across, r, 3 * across // 2 - 1 - r) * across + (c ^ 1)
        return jnp.where((group == 0) & (r == 0) & (c == 0), across * across, usual)

    def beside(number):
        dr, dc = STEPS[number]
        r, c = row + dr, col + dc
        there = (r >= 0) & (r < across) & (c >= 0) & (c < across)
        return there, rank(r, c) < rank(row, col), (r * across + c, group)

    def peer(other):
        return (block, other)

    barrier = pltpu.get_barrier_semaphore()
    earlier = group
    for number in range(8):
        there, before, device = beside(number)

        @pl.when(there & jnp.logical_not(before))
        def _():
            pl.semaphore_signal(barrier, inc=1, device_id=device, device_id_type=MESH)

        earlier = earlier + jnp.where(there & before, 1, 0)
    for other in range(GROUPS):

        @pl.when(other > group)
        def _():
            pl.semaphore_signal(barrier, inc=1, device_id=peer(other), device_id_type=MESH)

    for copy in loads[1:]:
        copy.start()

    @pl.when(earlier > 0)
    def _():
        pl.semaphore_wait(barrier, earlier)

    for other in range(GROUPS):

        @pl.when(other < group)
        def _():
            pl.semaphore_signal(
                above_sem.at[group], inc=1, device_id=peer(other), device_id_type=MESH
            )

    for number in range(8):
        there, before, device = beside(number)

        @pl.when(there & before)
        def _():
            pl.semaphore_signal(
                next_sem.at[number ^ 1], inc=1, device_id=device, device_id_type=MESH
            )

    loads[0].wait()
    ops[group] = jnp.transpose(trans[...])

    def send_ops(other):
        return pltpu.make_async_remote_copy(
            src_ref=ops.at[group],
            dst_ref=ops.at[group],
            send_sem=ts_sem.at[other],
            recv_sem=tr_sem.at[group],
            device_id=peer(other),
            device_id_type=MESH,
        )

    for other in range(GROUPS):

        @pl.when(other < group)
        def _():
            send_ops(other).start()

    loads[1].wait()
    code = code_ref[...]
    across_c = ((code >> 2) & 1) + ((code >> 4) & 1) * 2 + ((code >> 6) & 1) * 4
    down_r = ((code >> 3) & 1) + ((code >> 5) & 1) * 2 + ((code >> 7) & 1) * 4
    index_row = (code & 3) * 64 + down_r * 8 + across_c
    live_index = jnp.where(iota((1, CELLS), 1) < count_ref[0], index_row, -1)
    line = iota((128, CELLS), 0)
    beyond = line - 64
    wanted = jnp.where(
        line < 64, line, ((beyond & 31) >> 2) * 8 + (beyond >> 5) * 4 + (beyond & 3)
    )
    loads[2].wait()
    place = jnp.concatenate(
        [
            jnp.where(wanted == live_index - child * 64, 1.0, 0.0).astype(BF16)
            for child in range(4)
        ],
        axis=0,
    )
    placed = dot_nt(place, cur[...]).astype(BF16)
    for child in range(4):
        field[0:64, pl.ds(child * 256, 256)] = placed[child * 128 : child * 128 + 64]
        side[:, pl.ds(child * 256, 256)] = placed[child * 128 + 64 : child * 128 + 128]

    def send_field(number, device):
        buffer, start, size, target = PIECES[number]
        source = field if buffer == "own" else side
        return pltpu.make_async_remote_copy(
            src_ref=source.at[pl.ds(start, size)],
            dst_ref=field.at[pl.ds(target, size)],
            send_sem=fs_sem.at[number],
            recv_sem=fr_sem.at[number],
            device_id=device,
            device_id_type=MESH,
        )

    def send_fields(numbers, first):
        for number in numbers:
            there, before, device = beside(number)

            @pl.when(there & (before if first else jnp.logical_not(before)))
            def _():
                if not first:
                    pl.semaphore_wait(next_sem.at[number], 1)
                send_field(number, device).start()

    send_fields(range(8), True)

    for edge, pieces in (
        (row == 0, ((64, 32), (192, 32))),
        (row == across - 1, ((96, 32), (224, 32))),
        (col == 0, ((128, 32), (192, 16), (224, 16))),
        (col == across - 1, ((160, 32), (208, 16), (240, 16))),
    ):

        @pl.when(edge)
        def _():
            for start, size in pieces:
                field[start : start + size, :] = jnp.zeros((size, 1024), BF16)
    loads[3].wait()
    loads[4].wait()
    loads[5].wait()

    def prepare(g):
        weights = fold[pl.ds(g * 128, 128), :]
        rr = dot(weights, rad[0:128, :])
        ri = dot(weights, rad[128:256, :])
        rr = rr[:64] + rr[64:]
        ri = ri[:64] + ri[64:]
        rrh, rrl = split(rr)
        rih, ril = split(ri)
        base[pl.ds(g * 256, 64), :] = jnp.concatenate([rrh, -rih], axis=1)
        base[pl.ds(g * 256 + 64, 64), :] = jnp.concatenate([rih, rrh], axis=1)
        base[pl.ds(g * 256 + 128, 64), :] = jnp.concatenate([rrl, -ril], axis=1)
        base[pl.ds(g * 256 + 192, 64), :] = jnp.concatenate([ril, rrl], axis=1)
        turns = phase[g]
        for pair in range(2):
            cosine = turns[:, 2 * pair : 2 * pair + 1]
            sine = turns[:, 2 * pair + 1 : 2 * pair + 2]
            cr, ci, sr, si = cosine * rr, cosine * ri, sine * rr, sine * ri
            for child, ar, ai in ((pair, cr + si, ci - sr), (3 - pair, cr - si, ci + sr)):
                arh, arl = split(ar)
                aih, ail = split(ai)
                matrix = jnp.concatenate(
                    [
                        jnp.concatenate([arh, -aih], axis=1),
                        jnp.concatenate([aih, arh], axis=1),
                        jnp.concatenate([arl, -ail], axis=1),
                        jnp.concatenate([ail, arl], axis=1),
                    ],
                    axis=0,
                )
                mats[g, :, pl.ds(child * 256, 256)] = matrix
        total = dot_nt(field[0:64, :], mats[g])
        total = total[:, :128] + total[:, 128:]
        ext[g, 4:12, 8:16, :] = total.reshape(PSIDE, PSIDE, 128)

    for g in range(GROUPS):
        if g == EARLY:
            send_fields((0, 1, 2, 3, 4, 5), False)
        prepare(g)
    send_fields((6, 7), False)
    index_col[...] = jnp.transpose(jnp.broadcast_to(index_row, (128, CELLS)))
    own_index = index_col[pl.ds(pl.multiple_of(group * OWN, OWN), OWN), :]
    pick = jnp.where((own_index[:, :64] & 63) == iota((OWN, 64), 1), 1.0, 0.0).astype(BF16)
    own_child = own_index >> 6
    own_r = ((own_index >> 3) & 7) * 2 + (own_index >> 7)
    own_c = (own_index & 7) * 2 + ((own_index >> 6) & 1)
    hot = []
    for dr in (-1, 0, 1):
        for dc in (-1, 0, 1):
            r, c = own_r + dr, own_c + dc
            child = (r & 1) * 2 + (c & 1)
            pr, pc = r >> 1, c >> 1
            north, south, west, east = pr < 0, pr > 7, pc < 0, pc > 7
            at = jnp.where(west, 131 + pr * 4, jnp.where(east, 160 + pr * 4, pr * 8 + pc))
            at = jnp.where(north, jnp.where(west, 207, jnp.where(east, 220, 88 + pc)), at)
            at = jnp.where(south, jnp.where(west, 227, jnp.where(east, 240, 96 + pc)), at)
            at = at + child * 256
            hot.append(
                jnp.concatenate(
                    [
                        jnp.where(at == iota((OWN, 128), 1) + start, 1.0, 0.0).astype(BF16)
                        for start in range(0, 1024, 128)
                    ],
                    axis=1,
                )
            )
    hot = jnp.concatenate(hot, axis=0)
    def send_up():
        for other in range(1, GROUPS):

            @pl.when(other > group)
            def _():
                pl.semaphore_wait(above_sem.at[other], 1)
                send_ops(other).start()

    send_up()
    for number in range(8):
        there, _, device = beside(number ^ 1)

        @pl.when(there)
        def _():
            send_field(number, device).wait_recv()

    around = jnp.zeros((9 * OWN, 256), F32)
    for child in range(4):
        lanes = pl.ds(child * 256, 256)
        around = around + dot(hot[:, child * 256 : (child + 1) * 256], field[:, lanes])
    around = around.astype(BF16)
    loads[6].wait()
    loads[7].wait()
    close = jnp.zeros((2 * OWN, 256), F32)
    for number in range(9):
        mine = around[number * OWN : (number + 1) * OWN]
        stacked = jnp.concatenate([mine[:, :128], mine[:, 128:]], axis=0)
        close = close + dot_nt(stacked, near[pl.ds(number * 256, 256), :])
    def rim(g):
        total = dot_nt(field[64:256, :], mats[g])
        total = total[:, :128] + total[:, 128:]
        ext[g, 0:4, 8:16, :] = total[0:32].reshape(4, 8, 128)
        ext[g, 12:16, 8:16, :] = total[32:64].reshape(4, 8, 128)
        for r in range(8):
            ext[g, 4 + r, 4:8, :] = total[64 + 4 * r : 68 + 4 * r]
            ext[g, 4 + r, 16:20, :] = total[96 + 4 * r : 100 + 4 * r]
        for r in range(4):
            ext[g, r, 4:8, :] = total[128 + 4 * r : 132 + 4 * r]
            ext[g, r, 16:20, :] = total[144 + 4 * r : 148 + 4 * r]
            ext[g, 12 + r, 4:8, :] = total[160 + 4 * r : 164 + 4 * r]
            ext[g, 12 + r, 16:20, :] = total[176 + 4 * r : 180 + 4 * r]

    for g in range(GROUPS):
        rim(g)
    left = iota((DISP, 128), 1) < 64
    for g in range(GROUPS):

        @pl.when(g != group)
        def _():
            pltpu.make_async_remote_copy(
                src_ref=ops.at[g],
                dst_ref=ops.at[g],
                send_sem=ts_sem.at[g],
                recv_sem=tr_sem.at[g],
                device_id=peer(g),
                device_id_type=MESH,
            ).wait_recv()

        here = ops[g]
        turned = pltpu.roll(here, 64, 1)
        ta[g] = jnp.where(left, here, turned)
        tb[g] = jnp.where(left, turned, -here)
        high, low = split(translated(ext.at[g], ta.at[g], tb.at[g]))
        found[:, g * 256 : g * 256 + 128] = high
        found[:, g * 256 + 128 : g * 256 + 256] = low

    chosen = dot(pick, found[...])
    outer = (own_child == 0) | (own_child == 3)
    upper = own_child < 2
    tops, bottoms = [], []
    for g in range(GROUPS):
        value = chosen[:, g * 256 : g * 256 + 128] + chosen[:, g * 256 + 128 : g * 256 + 256]
        cosine = jnp.where(outer, turn[g, 0:1, :], turn[g, 2:3, :])
        sine = jnp.where(outer, turn[g, 1:2, :], turn[g, 3:4, :])
        sine = jnp.where(upper, sine, -sine)
        high, low = split(cosine * value + sine * pltpu.roll(value, 64, 1))
        tops += [high, high]
        bottoms += [low, jnp.zeros_like(low)]
    stacked = jnp.concatenate(
        [jnp.concatenate(tops, axis=1), jnp.concatenate(bottoms, axis=1)], axis=0
    )
    far = dot(stacked, base[...])

    live = iota((OWN, 128), 0) + group * OWN < count_ref[0]
    far = 0.25 * (far[:OWN] + far[OWN:])
    real = far[:, :128] + (close[:OWN, :128] - close[OWN:, 128:])
    imag = far[:, 128:] + (close[OWN:, :128] + close[:OWN, 128:])
    out_ref[0] = jnp.where(live, real, 0.0).astype(BF16)
    out_ref[1] = jnp.where(live, imag, 0.0).astype(BF16)

    for number in range(8):
        there, _, device = beside(number)

        @pl.when(there)
        def _():
            send_field(number, device).wait_send()

    for other in range(GROUPS):

        @pl.when(other != group)
        def _():
            send_ops(other).wait_send()


def on_device(across, tables, currents, box_code, box_count, radiation, near_block, translation):
    fold, phase, turn = tables
    operands = (
        box_code.reshape(1, CELLS),
        box_count,
        currents.reshape(2 * U, CELLS),
        radiation.reshape(2 * 128, U),
        near_block.reshape(9 * 2 * U, U),
        jnp.transpose(translation, (1, 2, 3, 0)).reshape(128, DISP),
        jnp.asarray(fold).reshape(GROUPS * 128, 128),
        jnp.asarray(phase),
        jnp.asarray(turn).reshape(GROUPS, 8, 128),
    )
    outside = pl.BlockSpec(memory_space=pltpu.HBM)
    result = pl.pallas_call(
        functools.partial(kernel, across),
        out_shape=jax.ShapeDtypeStruct((2, OWN, U), BF16),
        in_specs=[outside, pl.BlockSpec(memory_space=pltpu.SMEM)] + [outside] * 7,
        out_specs=pl.BlockSpec(memory_space=pltpu.VMEM),
        scratch_shapes=[
            pltpu.VMEM((1, CELLS), jnp.int32),
            pltpu.VMEM((256, 256), BF16),
            pltpu.VMEM((256, 128), BF16),
            pltpu.VMEM((9 * 256, 128), BF16),
            pltpu.VMEM((128, DISP), F32),
            pltpu.VMEM((GROUPS * 128, 128), BF16),
            pltpu.VMEM((GROUPS, SAMPLES, 128), F32),
            pltpu.VMEM((GROUPS, 8, 128), F32),
            pltpu.VMEM((GROUPS, DISP, 128), F32),
            pltpu.VMEM((GROUPS, DISP, 128), F32),
            pltpu.VMEM((GROUPS, DISP, 128), F32),
            pltpu.VMEM((256, 1024), BF16),
            pltpu.VMEM((64, 1024), BF16),
            pltpu.VMEM((GROUPS, 256, 1024), BF16),
            pltpu.VMEM((GROUPS * 256, 256), BF16),
            pltpu.VMEM((64, GROUPS * 256), BF16),
            pltpu.VMEM((GROUPS, 16, 24, 128), F32),
            pltpu.VMEM((CELLS, 128), jnp.int32),
            pltpu.SemaphoreType.DMA((8,)),
            pltpu.SemaphoreType.DMA((8,)),
            pltpu.SemaphoreType.DMA((8,)),
            pltpu.SemaphoreType.DMA((GROUPS,)),
            pltpu.SemaphoreType.DMA((GROUPS,)),
            pltpu.SemaphoreType.REGULAR((8,)),
            pltpu.SemaphoreType.REGULAR((GROUPS,)),
        ],
        compiler_params=pltpu.CompilerParams(
            collective_id=0, has_side_effects=True, vmem_limit_bytes=48 * 1024 * 1024
        ),
    )(*(pltpu.with_memory_space_constraint(x, pltpu.HBM) if x.size > 1 else x for x in operands))
    return jnp.transpose(result, (0, 2, 1))


def solution(mesh):
    across = math.isqrt(mesh.shape["box"])
    tables = make_tables()

    def step(*arrays):
        return on_device(across, tables, *arrays)

    placed = (P(None, None, "box"), P("box"), P("box"), P(), P(), P(None, None, None, "dir"))
    return jax.shard_map(
        step,
        mesh=mesh,
        in_specs=placed,
        out_specs=P(None, None, ("box", "dir")),
        check_vma=False,
    )
```

```python
import functools
import math

import jax
import jax.numpy as jnp
import ml_dtypes
import numpy as np
from jax import lax
from jax.experimental import pallas as pl
from jax.experimental.pallas import tpu as pltpu
from jax.sharding import PartitionSpec as P

U = 128
NT0 = 8
NP0 = 16
NT1 = 16
NP1 = 32
PSIDE = 8
CELLS = 256
GROUPS = 8
QL = NP1 // GROUPS
SAMPLES = NT1 * QL
OWN = CELLS // GROUPS
DISP = 40
EARLY = 1
MESH = pl.DeviceIdType.MESH
F32 = jnp.float32
BF16 = jnp.bfloat16

STEPS = ((1, 1), (-1, -1), (1, -1), (-1, 1), (1, 0), (-1, 0), (0, 1), (0, -1))
PIECES = (
    ("side", 48, 16, 192),
    ("side", 0, 16, 240),
    ("side", 16, 16, 208),
    ("side", 32, 16, 224),
    ("own", 32, 32, 64),
    ("own", 0, 32, 96),
    ("side", 32, 32, 128),
    ("side", 0, 32, 160),
)


def lagrange(offset, node):
    first = -(offset - 1.0) * (offset - 2.0) * (offset - 3.0) / 6.0
    second = offset * (offset - 2.0) * (offset - 3.0) / 2.0
    third = -offset * (offset - 1.0) * (offset - 3.0) / 2.0
    fourth = offset * (offset - 1.0) * (offset - 2.0) / 6.0
    return (
        np.where(node == 0, first, 0.0)
        + np.where(node == 1, second, 0.0)
        + np.where(node == 2, third, 0.0)
        + np.where(node == 3, fourth, 0.0)
    )


def make_tables():
    coarse = np.arange(NT1)[:, None]
    twice = 2 * coarse - 1
    base = np.clip(twice // 4 - 1, 0, NT0 - 4)
    theta = lagrange((twice - 4 * base) / 4.0, np.arange(NT0)[None, :] - base)
    coarse = np.arange(NP1)[:, None]
    twice = 2 * coarse - 1
    base = twice // 4 - 1
    phi = lagrange((twice - 4 * base) / 4.0, (np.arange(NP0)[None, :] - base) % NP0)
    polar = (np.arange(NT1) + 0.5) * math.pi / NT1
    azimuth = (np.arange(NP1) + 0.5) * 2.0 * math.pi / NP1
    fold = np.zeros((GROUPS, 2 * SAMPLES, NT0 * NP0), ml_dtypes.bfloat16)
    phase = np.zeros((GROUPS, SAMPLES, 128), np.float32)
    turn = np.zeros((GROUPS, 8, 2, SAMPLES), np.float32)
    for g in range(GROUPS):
        own = np.arange(g * QL, (g + 1) * QL)
        full = np.einsum("it,qp->iqtp", theta, phi[own]).reshape(SAMPLES, NT0 * NP0)
        high = full.astype(ml_dtypes.bfloat16)
        fold[g, :SAMPLES] = high
        fold[g, SAMPLES:] = (full - high.astype(np.float64)).astype(ml_dtypes.bfloat16)
        along_column = np.sin(polar)[:, None] * np.cos(azimuth[own])[None, :]
        along_row = np.sin(polar)[:, None] * np.sin(azimuth[own])[None, :]
        for child in range(2):
            psi = math.pi * (along_column * (child - 0.5) - along_row * 0.5)
            phase[g, :, 2 * child] = np.cos(psi).reshape(-1)
            phase[g, :, 2 * child + 1] = np.sin(psi).reshape(-1)
            turn[g, 2 * child] = np.cos(psi).reshape(-1)
            turn[g, 2 * child + 1, 0] = -np.sin(psi).reshape(-1)
            turn[g, 2 * child + 1, 1] = np.sin(psi).reshape(-1)
    return fold, phase, turn


def split(x):
    high = x.astype(BF16)
    low = (x - high.astype(F32)).astype(BF16)
    return high, low


def iota(shape, dim):
    return lax.broadcasted_iota(jnp.int32, shape, dim)


def dot(a, b):
    return jnp.dot(a, b, preferred_element_type=F32)


def dot_nt(a, b):
    return lax.dot_general(a, b, (((1,), (1,)), ((), ())), preferred_element_type=F32)


def displacements():
    return [
        (dy, dx) for dy in range(-3, 4) for dx in range(-3, 4) if max(abs(dy), abs(dx)) >= 2
    ]


def translated(parents, ta, tb):
    numbers = {pair: number for number, pair in enumerate(displacements())}
    first = [jnp.zeros((4, PSIDE, 128), F32) for _ in range(2)]
    second = [jnp.zeros((4, PSIDE, 128), F32) for _ in range(2)]
    odd_column = (iota((8, 2, PSIDE, 128), 2) & 1) == 1
    for dx in range(-3, 4):
        tile = parents[:, 8 + dx : 16 + dx, :].reshape(8, 2, PSIDE, 128)
        if dx == -3:
            tile = jnp.where(odd_column, tile, 0.0)
        if dx == 3:
            tile = jnp.where(odd_column, 0.0, tile)
        for dy in range(-3, 4):
            if (dy, dx) not in numbers:
                continue
            number = numbers[dy, dx]
            wa = ta[number : number + 1, :].reshape(1, 1, 128)
            wb = tb[number : number + 1, :].reshape(1, 1, 128)
            for parity in range(2):
                if dy == (-3 if parity == 0 else 3):
                    continue
                start = 4 + dy + parity
                source = tile[start // 2 : start // 2 + 4, start % 2]
                first[parity] = first[parity] + wa * source
                second[parity] = second[parity] + wb * source
    first = jnp.stack(first, axis=1).reshape(64, 128)
    second = jnp.stack(second, axis=1).reshape(64, 128)
    return first + pltpu.roll(second, 64, 1)


def kernel(
    across,
    code_hbm,
    count_ref,
    cur_hbm,
    rad_hbm,
    near_hbm,
    trans_hbm,
    fold_hbm,
    phase_hbm,
    turn_hbm,
    out_ref,
    code_ref,
    cur,
    rad,
    near,
    trans,
    fold,
    phase,
    turn,
    ops,
    ta,
    tb,
    field,
    side,
    mats,
    base,
    found,
    ext,
    index_col,
    load_sem,
    fs_sem,
    fr_sem,
    ts_sem,
    tr_sem,
    next_sem,
    above_sem,
):
    block = lax.axis_index("box")
    group = lax.axis_index("dir")
    row = block // across
    col = block % across

    loads = []
    for number, (source, target) in enumerate(
        (
            (trans_hbm, trans),
            (code_hbm, code_ref),
            (cur_hbm, cur),
            (rad_hbm, rad),
            (fold_hbm, fold),
            (phase_hbm, phase),
            (near_hbm, near),
            (turn_hbm, turn),
        )
    ):
        copy = pltpu.make_async_copy(source, target, load_sem.at[number])
        loads.append(copy)

    loads[0].start()

    def rank(r, c):
        usual = jnp.where(2 * r < across, 11 * r, 36 + 6 * (across - 1 - r))
        usual = (usual + 4 * c + 9 - 13 * (c & 1)) * across * across + r * across + c
        return jnp.where((group == 0) & (r == 0) & (c == 0), 1 << 20, usual)

    def beside(number):
        dr, dc = STEPS[number]
        r, c = row + dr, col + dc
        there = (r >= 0) & (r < across) & (c >= 0) & (c < across)
        return there, rank(r, c) < rank(row, col), (r * across + c, group)

    def peer(other):
        return (block, other)

    barrier = pltpu.get_barrier_semaphore()
    earlier = group
    for number in range(8):
        there, before, device = beside(number)

        @pl.when(there & jnp.logical_not(before))
        def _():
            pl.semaphore_signal(barrier, inc=1, device_id=device, device_id_type=MESH)

        earlier = earlier + jnp.where(there & before, 1, 0)
    for other in range(GROUPS):

        @pl.when(other > group)
        def _():
            pl.semaphore_signal(barrier, inc=1, device_id=peer(other), device_id_type=MESH)

    for copy in loads[1:6]:
        copy.start()

    @pl.when(earlier > 0)
    def _():
        pl.semaphore_wait(barrier, earlier)

    for other in range(GROUPS):

        @pl.when(other < group)
        def _():
            pl.semaphore_signal(
                above_sem.at[group], inc=1, device_id=peer(other), device_id_type=MESH
            )

    for number in range(8):
        there, before, device = beside(number)

        @pl.when(there & before)
        def _():
            pl.semaphore_signal(
                next_sem.at[number ^ 1], inc=1, device_id=device, device_id_type=MESH
            )

    loads[0].wait()
    ops[group] = jnp.transpose(trans[...])

    def send_ops(other):
        return pltpu.make_async_remote_copy(
            src_ref=ops.at[group],
            dst_ref=ops.at[group],
            send_sem=ts_sem.at[other],
            recv_sem=tr_sem.at[group],
            device_id=peer(other),
            device_id_type=MESH,
        )

    for other in range(GROUPS):

        @pl.when(other < group)
        def _():
            send_ops(other).start()

    for copy in loads[6:]:
        copy.start()

    loads[1].wait()
    code = code_ref[...]
    across_c = ((code >> 2) & 1) + ((code >> 4) & 1) * 2 + ((code >> 6) & 1) * 4
    down_r = ((code >> 3) & 1) + ((code >> 5) & 1) * 2 + ((code >> 7) & 1) * 4
    index_row = (code & 3) * 64 + down_r * 8 + across_c
    live_index = jnp.where(iota((1, CELLS), 1) < count_ref[0], index_row, -1)
    line = iota((128, CELLS), 0)
    beyond = line - 64
    wanted = jnp.where(
        line < 64, line, ((beyond & 31) >> 2) * 8 + (beyond >> 5) * 4 + (beyond & 3)
    )
    loads[2].wait()
    place = jnp.concatenate(
        [
            jnp.where(wanted == live_index - child * 64, 1.0, 0.0).astype(BF16)
            for child in range(4)
        ],
        axis=0,
    )
    placed = dot_nt(place, cur[...]).astype(BF16)
    for child in range(4):
        field[0:64, pl.ds(child * 256, 256)] = placed[child * 128 : child * 128 + 64]
        side[:, pl.ds(child * 256, 256)] = placed[child * 128 + 64 : child * 128 + 128]

    def send_field(number, device):
        buffer, start, size, target = PIECES[number]
        source = field if buffer == "own" else side
        return pltpu.make_async_remote_copy(
            src_ref=source.at[pl.ds(start, size)],
            dst_ref=field.at[pl.ds(target, size)],
            send_sem=fs_sem.at[number],
            recv_sem=fr_sem.at[number],
            device_id=device,
            device_id_type=MESH,
        )

    def send_fields(numbers, first):
        for number in numbers:
            there, before, device = beside(number)

            @pl.when(there & (before if first else jnp.logical_not(before)))
            def _():
                if not first:
                    pl.semaphore_wait(next_sem.at[number], 1)
                send_field(number, device).start()

    send_fields(range(8), True)

    for edge, pieces in (
        (row == 0, ((64, 32), (192, 32))),
        (row == across - 1, ((96, 32), (224, 32))),
        (col == 0, ((128, 32), (192, 16), (224, 16))),
        (col == across - 1, ((160, 32), (208, 16), (240, 16))),
    ):

        @pl.when(edge)
        def _():
            for start, size in pieces:
                field[start : start + size, :] = jnp.zeros((size, 1024), BF16)
    loads[3].wait()
    loads[4].wait()
    loads[5].wait()

    def prepare(g):
        weights = fold[pl.ds(g * 128, 128), :]
        rr = dot(weights, rad[0:128, :])
        ri = dot(weights, rad[128:256, :])
        rr = rr[:64] + rr[64:]
        ri = ri[:64] + ri[64:]
        rrh, rrl = split(rr)
        rih, ril = split(ri)
        base[pl.ds(g * 256, 64), :] = jnp.concatenate([rrh, -rih], axis=1)
        base[pl.ds(g * 256 + 64, 64), :] = jnp.concatenate([rih, rrh], axis=1)
        base[pl.ds(g * 256 + 128, 64), :] = jnp.concatenate([rrl, -ril], axis=1)
        base[pl.ds(g * 256 + 192, 64), :] = jnp.concatenate([ril, rrl], axis=1)
        turns = phase[g]
        for pair in range(2):
            cosine = turns[:, 2 * pair : 2 * pair + 1]
            sine = turns[:, 2 * pair + 1 : 2 * pair + 2]
            cr, ci, sr, si = cosine * rr, cosine * ri, sine * rr, sine * ri
            for child, ar, ai in ((pair, cr + si, ci - sr), (3 - pair, cr - si, ci + sr)):
                arh, arl = split(ar)
                aih, ail = split(ai)
                matrix = jnp.concatenate(
                    [
                        jnp.concatenate([arh, -aih], axis=1),
                        jnp.concatenate([aih, arh], axis=1),
                        jnp.concatenate([arl, -ail], axis=1),
                        jnp.concatenate([ail, arl], axis=1),
                    ],
                    axis=0,
                )
                mats[g, :, pl.ds(child * 256, 256)] = matrix
        total = dot_nt(field[0:64, :], mats[g])
        total = total[:, :128] + total[:, 128:]
        ext[g, 4:12, 8:16, :] = total.reshape(PSIDE, PSIDE, 128)

    for g in range(GROUPS):
        if g == EARLY:
            send_fields((0, 1, 2, 3, 4, 5), False)
        prepare(g)
    send_fields((6, 7), False)
    index_col[...] = jnp.transpose(jnp.broadcast_to(index_row, (128, CELLS)))
    own_index = index_col[pl.ds(pl.multiple_of(group * OWN, OWN), OWN), :]
    pick = jnp.where((own_index[:, :64] & 63) == iota((OWN, 64), 1), 1.0, 0.0).astype(BF16)
    own_child = own_index >> 6
    own_r = ((own_index >> 3) & 7) * 2 + (own_index >> 7)
    own_c = (own_index & 7) * 2 + ((own_index >> 6) & 1)
    hot = []
    for dr in (-1, 0, 1):
        for dc in (-1, 0, 1):
            r, c = own_r + dr, own_c + dc
            child = (r & 1) * 2 + (c & 1)
            pr, pc = r >> 1, c >> 1
            north, south, west, east = pr < 0, pr > 7, pc < 0, pc > 7
            at = jnp.where(west, 131 + pr * 4, jnp.where(east, 160 + pr * 4, pr * 8 + pc))
            at = jnp.where(north, jnp.where(west, 207, jnp.where(east, 220, 88 + pc)), at)
            at = jnp.where(south, jnp.where(west, 227, jnp.where(east, 240, 96 + pc)), at)
            at = at + child * 256
            hot.append(
                jnp.concatenate(
                    [
                        jnp.where(at == iota((OWN, 128), 1) + start, 1.0, 0.0).astype(BF16)
                        for start in range(0, 1024, 128)
                    ],
                    axis=1,
                )
            )
    hot = jnp.concatenate(hot, axis=0)
    def send_up(others):
        for other in others:

            @pl.when(other > group)
            def _():
                pl.semaphore_wait(above_sem.at[other], 1)
                send_ops(other).start()

    send_up(range(1, GROUPS // 2))

    @pl.when(group >= 1)
    def _():
        send_up(range(GROUPS // 2, GROUPS))

    for number in range(8):
        there, _, device = beside(number ^ 1)

        @pl.when(there)
        def _():
            send_field(number, device).wait_recv()

    around = jnp.zeros((9 * OWN, 256), F32)
    for child in range(4):
        lanes = pl.ds(child * 256, 256)
        around = around + dot(hot[:, child * 256 : (child + 1) * 256], field[:, lanes])
    around = around.astype(BF16)
    loads[6].wait()
    loads[7].wait()
    close = jnp.zeros((2 * OWN, 256), F32)
    for number in range(9):
        mine = around[number * OWN : (number + 1) * OWN]
        stacked = jnp.concatenate([mine[:, :128], mine[:, 128:]], axis=0)
        close = close + dot_nt(stacked, near[pl.ds(number * 256, 256), :])
    def rim(g):
        total = dot_nt(field[64:256, :], mats[g])
        total = total[:, :128] + total[:, 128:]
        ext[g, 0:4, 8:16, :] = total[0:32].reshape(4, 8, 128)
        ext[g, 12:16, 8:16, :] = total[32:64].reshape(4, 8, 128)
        for r in range(8):
            ext[g, 4 + r, 4:8, :] = total[64 + 4 * r : 68 + 4 * r]
            ext[g, 4 + r, 16:20, :] = total[96 + 4 * r : 100 + 4 * r]
        for r in range(4):
            ext[g, r, 4:8, :] = total[128 + 4 * r : 132 + 4 * r]
            ext[g, r, 16:20, :] = total[144 + 4 * r : 148 + 4 * r]
            ext[g, 12 + r, 4:8, :] = total[160 + 4 * r : 164 + 4 * r]
            ext[g, 12 + r, 16:20, :] = total[176 + 4 * r : 180 + 4 * r]

    for g in range(GROUPS):
        rim(g)
    @pl.when(group < 1)
    def _():
        send_up(range(GROUPS // 2, GROUPS))

    left = iota((DISP, 128), 1) < 64
    for g in range(GROUPS):

        @pl.when(g != group)
        def _():
            pltpu.make_async_remote_copy(
                src_ref=ops.at[g],
                dst_ref=ops.at[g],
                send_sem=ts_sem.at[g],
                recv_sem=tr_sem.at[g],
                device_id=peer(g),
                device_id_type=MESH,
            ).wait_recv()

        here = ops[g]
        turned = pltpu.roll(here, 64, 1)
        ta[g] = jnp.where(left, here, turned)
        tb[g] = jnp.where(left, turned, -here)
        high, low = split(translated(ext.at[g], ta.at[g], tb.at[g]))
        found[:, g * 256 : g * 256 + 128] = high
        found[:, g * 256 + 128 : g * 256 + 256] = low

    chosen = dot(pick, found[...])
    outer = (own_child == 0) | (own_child == 3)
    upper = own_child < 2
    tops, bottoms = [], []
    for g in range(GROUPS):
        value = chosen[:, g * 256 : g * 256 + 128] + chosen[:, g * 256 + 128 : g * 256 + 256]
        cosine = jnp.where(outer, turn[g, 0:1, :], turn[g, 2:3, :])
        sine = jnp.where(outer, turn[g, 1:2, :], turn[g, 3:4, :])
        sine = jnp.where(upper, sine, -sine)
        high, low = split(cosine * value + sine * pltpu.roll(value, 64, 1))
        tops += [high, high]
        bottoms += [low, jnp.zeros_like(low)]
    stacked = jnp.concatenate(
        [jnp.concatenate(tops, axis=1), jnp.concatenate(bottoms, axis=1)], axis=0
    )
    far = dot(stacked, base[...])

    live = iota((OWN, 128), 0) + group * OWN < count_ref[0]
    far = 0.25 * (far[:OWN] + far[OWN:])
    real = far[:, :128] + (close[:OWN, :128] - close[OWN:, 128:])
    imag = far[:, 128:] + (close[OWN:, :128] + close[:OWN, 128:])
    out_ref[0] = jnp.where(live, real, 0.0).astype(BF16)
    out_ref[1] = jnp.where(live, imag, 0.0).astype(BF16)

    for number in range(8):
        there, _, device = beside(number)

        @pl.when(there)
        def _():
            send_field(number, device).wait_send()

    for other in range(GROUPS):

        @pl.when(other != group)
        def _():
            send_ops(other).wait_send()


def on_device(across, tables, currents, box_code, box_count, radiation, near_block, translation):
    fold, phase, turn = tables
    operands = (
        box_code.reshape(1, CELLS),
        box_count,
        currents.reshape(2 * U, CELLS),
        radiation.reshape(2 * 128, U),
        near_block.reshape(9 * 2 * U, U),
        jnp.transpose(translation, (1, 2, 3, 0)).reshape(128, DISP),
        jnp.asarray(fold).reshape(GROUPS * 128, 128),
        jnp.asarray(phase),
        jnp.asarray(turn).reshape(GROUPS, 8, 128),
    )
    outside = pl.BlockSpec(memory_space=pltpu.HBM)
    result = pl.pallas_call(
        functools.partial(kernel, across),
        out_shape=jax.ShapeDtypeStruct((2, OWN, U), BF16),
        in_specs=[outside, pl.BlockSpec(memory_space=pltpu.SMEM)] + [outside] * 7,
        out_specs=pl.BlockSpec(memory_space=pltpu.VMEM),
        scratch_shapes=[
            pltpu.VMEM((1, CELLS), jnp.int32),
            pltpu.VMEM((256, 256), BF16),
            pltpu.VMEM((256, 128), BF16),
            pltpu.VMEM((9 * 256, 128), BF16),
            pltpu.VMEM((128, DISP), F32),
            pltpu.VMEM((GROUPS * 128, 128), BF16),
            pltpu.VMEM((GROUPS, SAMPLES, 128), F32),
            pltpu.VMEM((GROUPS, 8, 128), F32),
            pltpu.VMEM((GROUPS, DISP, 128), F32),
            pltpu.VMEM((GROUPS, DISP, 128), F32),
            pltpu.VMEM((GROUPS, DISP, 128), F32),
            pltpu.VMEM((256, 1024), BF16),
            pltpu.VMEM((64, 1024), BF16),
            pltpu.VMEM((GROUPS, 256, 1024), BF16),
            pltpu.VMEM((GROUPS * 256, 256), BF16),
            pltpu.VMEM((64, GROUPS * 256), BF16),
            pltpu.VMEM((GROUPS, 16, 24, 128), F32),
            pltpu.VMEM((CELLS, 128), jnp.int32),
            pltpu.SemaphoreType.DMA((8,)),
            pltpu.SemaphoreType.DMA((8,)),
            pltpu.SemaphoreType.DMA((8,)),
            pltpu.SemaphoreType.DMA((GROUPS,)),
            pltpu.SemaphoreType.DMA((GROUPS,)),
            pltpu.SemaphoreType.REGULAR((8,)),
            pltpu.SemaphoreType.REGULAR((GROUPS,)),
        ],
        compiler_params=pltpu.CompilerParams(
            collective_id=0, has_side_effects=True, vmem_limit_bytes=48 * 1024 * 1024
        ),
    )(*(pltpu.with_memory_space_constraint(x, pltpu.HBM) if x.size > 1 else x for x in operands))
    return jnp.transpose(result, (0, 2, 1))


def solution(mesh):
    across = math.isqrt(mesh.shape["box"])
    tables = make_tables()

    def step(*arrays):
        return on_device(across, tables, *arrays)

    placed = (P(None, None, "box"), P("box"), P("box"), P(), P(), P(None, None, None, "dir"))
    return jax.shard_map(
        step,
        mesh=mesh,
        in_specs=placed,
        out_specs=P(None, None, ("box", "dir")),
        check_vma=False,
    )
```

```python
import functools
import math

import jax
import jax.numpy as jnp
import ml_dtypes
import numpy as np
from jax import lax
from jax.experimental import pallas as pl
from jax.experimental.pallas import tpu as pltpu
from jax.sharding import PartitionSpec as P

U = 128
NT0 = 8
NP0 = 16
NT1 = 16
NP1 = 32
PSIDE = 8
CELLS = 256
GROUPS = 8
QL = NP1 // GROUPS
SAMPLES = NT1 * QL
OWN = CELLS // GROUPS
DISP = 40
EARLY = 1
MESH = pl.DeviceIdType.MESH
F32 = jnp.float32
BF16 = jnp.bfloat16

STEPS = ((1, 1), (-1, -1), (1, -1), (-1, 1), (1, 0), (-1, 0), (0, 1), (0, -1))
PIECES = (
    ("side", 48, 16, 192),
    ("side", 0, 16, 240),
    ("side", 16, 16, 208),
    ("side", 32, 16, 224),
    ("own", 32, 32, 64),
    ("own", 0, 32, 96),
    ("side", 32, 32, 128),
    ("side", 0, 32, 160),
)


def lagrange(offset, node):
    first = -(offset - 1.0) * (offset - 2.0) * (offset - 3.0) / 6.0
    second = offset * (offset - 2.0) * (offset - 3.0) / 2.0
    third = -offset * (offset - 1.0) * (offset - 3.0) / 2.0
    fourth = offset * (offset - 1.0) * (offset - 2.0) / 6.0
    return (
        np.where(node == 0, first, 0.0)
        + np.where(node == 1, second, 0.0)
        + np.where(node == 2, third, 0.0)
        + np.where(node == 3, fourth, 0.0)
    )


def make_tables():
    coarse = np.arange(NT1)[:, None]
    twice = 2 * coarse - 1
    base = np.clip(twice // 4 - 1, 0, NT0 - 4)
    theta = lagrange((twice - 4 * base) / 4.0, np.arange(NT0)[None, :] - base)
    coarse = np.arange(NP1)[:, None]
    twice = 2 * coarse - 1
    base = twice // 4 - 1
    phi = lagrange((twice - 4 * base) / 4.0, (np.arange(NP0)[None, :] - base) % NP0)
    polar = (np.arange(NT1) + 0.5) * math.pi / NT1
    azimuth = (np.arange(NP1) + 0.5) * 2.0 * math.pi / NP1
    fold = np.zeros((GROUPS, 2 * SAMPLES, NT0 * NP0), ml_dtypes.bfloat16)
    phase = np.zeros((GROUPS, SAMPLES, 128), np.float32)
    turn = np.zeros((GROUPS, 8, 2, SAMPLES), np.float32)
    for g in range(GROUPS):
        own = np.arange(g * QL, (g + 1) * QL)
        full = np.einsum("it,qp->iqtp", theta, phi[own]).reshape(SAMPLES, NT0 * NP0)
        high = full.astype(ml_dtypes.bfloat16)
        fold[g, :SAMPLES] = high
        fold[g, SAMPLES:] = (full - high.astype(np.float64)).astype(ml_dtypes.bfloat16)
        along_column = np.sin(polar)[:, None] * np.cos(azimuth[own])[None, :]
        along_row = np.sin(polar)[:, None] * np.sin(azimuth[own])[None, :]
        for child in range(2):
            psi = math.pi * (along_column * (child - 0.5) - along_row * 0.5)
            phase[g, :, 2 * child] = np.cos(psi).reshape(-1)
            phase[g, :, 2 * child + 1] = np.sin(psi).reshape(-1)
            turn[g, 2 * child] = np.cos(psi).reshape(-1)
            turn[g, 2 * child + 1, 0] = -np.sin(psi).reshape(-1)
            turn[g, 2 * child + 1, 1] = np.sin(psi).reshape(-1)
    return fold, phase, turn


def split(x):
    high = x.astype(BF16)
    low = (x - high.astype(F32)).astype(BF16)
    return high, low


def iota(shape, dim):
    return lax.broadcasted_iota(jnp.int32, shape, dim)


def dot(a, b):
    return jnp.dot(a, b, preferred_element_type=F32)


def dot_nt(a, b):
    return lax.dot_general(a, b, (((1,), (1,)), ((), ())), preferred_element_type=F32)


def displacements():
    return [
        (dy, dx) for dy in range(-3, 4) for dx in range(-3, 4) if max(abs(dy), abs(dx)) >= 2
    ]


def translated(parents, ta, tb):
    numbers = {pair: number for number, pair in enumerate(displacements())}
    first = [jnp.zeros((4, PSIDE, 128), F32) for _ in range(2)]
    second = [jnp.zeros((4, PSIDE, 128), F32) for _ in range(2)]
    odd_column = (iota((8, 2, PSIDE, 128), 2) & 1) == 1
    for dx in range(-3, 4):
        tile = parents[:, 8 + dx : 16 + dx, :].reshape(8, 2, PSIDE, 128)
        if dx == -3:
            tile = jnp.where(odd_column, tile, 0.0)
        if dx == 3:
            tile = jnp.where(odd_column, 0.0, tile)
        for dy in range(-3, 4):
            if (dy, dx) not in numbers:
                continue
            number = numbers[dy, dx]
            wa = ta[number : number + 1, :].reshape(1, 1, 128)
            wb = tb[number : number + 1, :].reshape(1, 1, 128)
            for parity in range(2):
                if dy == (-3 if parity == 0 else 3):
                    continue
                start = 4 + dy + parity
                source = tile[start // 2 : start // 2 + 4, start % 2]
                first[parity] = first[parity] + wa * source
                second[parity] = second[parity] + wb * source
    first = jnp.stack(first, axis=1).reshape(64, 128)
    second = jnp.stack(second, axis=1).reshape(64, 128)
    return first + pltpu.roll(second, 64, 1)


def kernel(
    across,
    code_hbm,
    count_ref,
    cur_hbm,
    rad_hbm,
    near_hbm,
    trans_hbm,
    fold_hbm,
    phase_hbm,
    turn_hbm,
    out_ref,
    code_ref,
    cur,
    rad,
    near,
    trans,
    fold,
    phase,
    turn,
    ops,
    ta,
    tb,
    field,
    side,
    mats,
    base,
    found,
    ext,
    index_col,
    load_sem,
    fs_sem,
    fr_sem,
    ts_sem,
    tr_sem,
    next_sem,
    above_sem,
):
    block = lax.axis_index("box")
    group = lax.axis_index("dir")
    row = block // across
    col = block % across

    loads = []
    for number, (source, target) in enumerate(
        (
            (trans_hbm, trans),
            (code_hbm, code_ref),
            (cur_hbm, cur),
            (rad_hbm, rad),
            (fold_hbm, fold),
            (phase_hbm, phase),
            (near_hbm, near),
            (turn_hbm, turn),
        )
    ):
        copy = pltpu.make_async_copy(source, target, load_sem.at[number])
        loads.append(copy)

    loads[0].start()

    def rank(r, c):
        usual = jnp.where(2 * r < across, 11 * r, 36 + 6 * (across - 1 - r))
        usual = (usual + 4 * c + 9 - 13 * (c & 1)) * across * across + r * across + c
        return jnp.where((group == 0) & (r == 0) & (c == 0), 1 << 20, usual)

    def beside(number):
        dr, dc = STEPS[number]
        r, c = row + dr, col + dc
        there = (r >= 0) & (r < across) & (c >= 0) & (c < across)
        return there, rank(r, c) < rank(row, col), (r * across + c, group)

    def peer(other):
        return (block, other)

    barrier = pltpu.get_barrier_semaphore()
    earlier = group
    for number in range(8):
        there, before, device = beside(number)

        @pl.when(there & jnp.logical_not(before))
        def _():
            pl.semaphore_signal(barrier, inc=1, device_id=device, device_id_type=MESH)

        earlier = earlier + jnp.where(there & before, 1, 0)
    for other in range(GROUPS):

        @pl.when(other > group)
        def _():
            pl.semaphore_signal(barrier, inc=1, device_id=peer(other), device_id_type=MESH)

    for copy in loads[1:6]:
        copy.start()

    @pl.when(earlier > 0)
    def _():
        pl.semaphore_wait(barrier, earlier)

    for other in range(GROUPS):

        @pl.when(other < group)
        def _():
            pl.semaphore_signal(
                above_sem.at[group], inc=1, device_id=peer(other), device_id_type=MESH
            )

    for number in range(8):
        there, before, device = beside(number)

        @pl.when(there & before)
        def _():
            pl.semaphore_signal(
                next_sem.at[number ^ 1], inc=1, device_id=device, device_id_type=MESH
            )

    loads[0].wait()
    ops[group] = jnp.transpose(trans[...])

    def send_ops(other):
        return pltpu.make_async_remote_copy(
            src_ref=ops.at[group],
            dst_ref=ops.at[group],
            send_sem=ts_sem.at[other],
            recv_sem=tr_sem.at[group],
            device_id=peer(other),
            device_id_type=MESH,
        )

    for other in range(GROUPS):

        @pl.when(other < group)
        def _():
            send_ops(other).start()

    for copy in loads[6:]:
        copy.start()

    loads[1].wait()
    code = code_ref[...]
    across_c = ((code >> 2) & 1) + ((code >> 4) & 1) * 2 + ((code >> 6) & 1) * 4
    down_r = ((code >> 3) & 1) + ((code >> 5) & 1) * 2 + ((code >> 7) & 1) * 4
    index_row = (code & 3) * 64 + down_r * 8 + across_c
    live_index = jnp.where(iota((1, CELLS), 1) < count_ref[0], index_row, -1)
    line = iota((128, CELLS), 0)
    beyond = line - 64
    wanted = jnp.where(
        line < 64, line, ((beyond & 31) >> 2) * 8 + (beyond >> 5) * 4 + (beyond & 3)
    )
    loads[2].wait()
    place = jnp.concatenate(
        [
            jnp.where(wanted == live_index - child * 64, 1.0, 0.0).astype(BF16)
            for child in range(4)
        ],
        axis=0,
    )
    placed = dot_nt(place, cur[...]).astype(BF16)
    for child in range(4):
        field[0:64, pl.ds(child * 256, 256)] = placed[child * 128 : child * 128 + 64]
        side[:, pl.ds(child * 256, 256)] = placed[child * 128 + 64 : child * 128 + 128]

    def send_field(number, device):
        buffer, start, size, target = PIECES[number]
        source = field if buffer == "own" else side
        return pltpu.make_async_remote_copy(
            src_ref=source.at[pl.ds(start, size)],
            dst_ref=field.at[pl.ds(target, size)],
            send_sem=fs_sem.at[number],
            recv_sem=fr_sem.at[number],
            device_id=device,
            device_id_type=MESH,
        )

    def send_fields(numbers, turn_of):
        for number in numbers:
            there, before, device = beside(number)
            last = (group == 0) & (device[0] == 0)
            if turn_of == "before":
                due = before
            elif turn_of == "after":
                due = jnp.logical_not(before | last)
            else:
                due = last

            @pl.when(there & due)
            def _():
                if turn_of != "before":
                    pl.semaphore_wait(next_sem.at[number], 1)
                send_field(number, device).start()

    send_fields(range(8), "before")

    for edge, pieces in (
        (row == 0, ((64, 32), (192, 32))),
        (row == across - 1, ((96, 32), (224, 32))),
        (col == 0, ((128, 32), (192, 16), (224, 16))),
        (col == across - 1, ((160, 32), (208, 16), (240, 16))),
    ):

        @pl.when(edge)
        def _():
            for start, size in pieces:
                field[start : start + size, :] = jnp.zeros((size, 1024), BF16)
    loads[3].wait()
    loads[4].wait()
    loads[5].wait()

    def prepare(g):
        weights = fold[pl.ds(g * 128, 128), :]
        rr = dot(weights, rad[0:128, :])
        ri = dot(weights, rad[128:256, :])
        rr = rr[:64] + rr[64:]
        ri = ri[:64] + ri[64:]
        rrh, rrl = split(rr)
        rih, ril = split(ri)
        base[pl.ds(g * 256, 64), :] = jnp.concatenate([rrh, -rih], axis=1)
        base[pl.ds(g * 256 + 64, 64), :] = jnp.concatenate([rih, rrh], axis=1)
        base[pl.ds(g * 256 + 128, 64), :] = jnp.concatenate([rrl, -ril], axis=1)
        base[pl.ds(g * 256 + 192, 64), :] = jnp.concatenate([ril, rrl], axis=1)
        turns = phase[g]
        for pair in range(2):
            cosine = turns[:, 2 * pair : 2 * pair + 1]
            sine = turns[:, 2 * pair + 1 : 2 * pair + 2]
            cr, ci, sr, si = cosine * rr, cosine * ri, sine * rr, sine * ri
            for child, ar, ai in ((pair, cr + si, ci - sr), (3 - pair, cr - si, ci + sr)):
                arh, arl = split(ar)
                aih, ail = split(ai)
                matrix = jnp.concatenate(
                    [
                        jnp.concatenate([arh, -aih], axis=1),
                        jnp.concatenate([aih, arh], axis=1),
                        jnp.concatenate([arl, -ail], axis=1),
                        jnp.concatenate([ail, arl], axis=1),
                    ],
                    axis=0,
                )
                mats[g, :, pl.ds(child * 256, 256)] = matrix
        total = dot_nt(field[0:64, :], mats[g])
        total = total[:, :128] + total[:, 128:]
        ext[g, 4:12, 8:16, :] = total.reshape(PSIDE, PSIDE, 128)

    for g in range(GROUPS):
        if g == EARLY:
            send_fields((0, 1, 2, 3, 4, 5), "after")
        prepare(g)
    send_fields((6, 7), "after")
    index_col[...] = jnp.transpose(jnp.broadcast_to(index_row, (128, CELLS)))
    own_index = index_col[pl.ds(pl.multiple_of(group * OWN, OWN), OWN), :]
    pick = jnp.where((own_index[:, :64] & 63) == iota((OWN, 64), 1), 1.0, 0.0).astype(BF16)
    own_child = own_index >> 6
    own_r = ((own_index >> 3) & 7) * 2 + (own_index >> 7)
    own_c = (own_index & 7) * 2 + ((own_index >> 6) & 1)
    hot = []
    for dr in (-1, 0, 1):
        for dc in (-1, 0, 1):
            r, c = own_r + dr, own_c + dc
            child = (r & 1) * 2 + (c & 1)
            pr, pc = r >> 1, c >> 1
            north, south, west, east = pr < 0, pr > 7, pc < 0, pc > 7
            at = jnp.where(west, 131 + pr * 4, jnp.where(east, 160 + pr * 4, pr * 8 + pc))
            at = jnp.where(north, jnp.where(west, 207, jnp.where(east, 220, 88 + pc)), at)
            at = jnp.where(south, jnp.where(west, 227, jnp.where(east, 240, 96 + pc)), at)
            at = at + child * 256
            hot.append(
                jnp.concatenate(
                    [
                        jnp.where(at == iota((OWN, 128), 1) + start, 1.0, 0.0).astype(BF16)
                        for start in range(0, 1024, 128)
                    ],
                    axis=1,
                )
            )
    hot = jnp.concatenate(hot, axis=0)
    def send_up(others):
        for other in others:

            @pl.when(other > group)
            def _():
                pl.semaphore_wait(above_sem.at[other], 1)
                send_ops(other).start()

    send_up(range(1, GROUPS // 2))

    @pl.when(group >= 1)
    def _():
        send_up(range(GROUPS // 2, GROUPS))

    send_fields(range(8), "last")
    for number in range(8):
        there, _, device = beside(number ^ 1)

        @pl.when(there)
        def _():
            send_field(number, device).wait_recv()

    around = jnp.zeros((9 * OWN, 256), F32)
    for child in range(4):
        lanes = pl.ds(child * 256, 256)
        around = around + dot(hot[:, child * 256 : (child + 1) * 256], field[:, lanes])
    around = around.astype(BF16)
    loads[6].wait()
    loads[7].wait()
    close = jnp.zeros((2 * OWN, 256), F32)
    for number in range(9):
        mine = around[number * OWN : (number + 1) * OWN]
        stacked = jnp.concatenate([mine[:, :128], mine[:, 128:]], axis=0)
        close = close + dot_nt(stacked, near[pl.ds(number * 256, 256), :])
    def rim(g):
        total = dot_nt(field[64:256, :], mats[g])
        total = total[:, :128] + total[:, 128:]
        ext[g, 0:4, 8:16, :] = total[0:32].reshape(4, 8, 128)
        ext[g, 12:16, 8:16, :] = total[32:64].reshape(4, 8, 128)
        for r in range(8):
            ext[g, 4 + r, 4:8, :] = total[64 + 4 * r : 68 + 4 * r]
            ext[g, 4 + r, 16:20, :] = total[96 + 4 * r : 100 + 4 * r]
        for r in range(4):
            ext[g, r, 4:8, :] = total[128 + 4 * r : 132 + 4 * r]
            ext[g, r, 16:20, :] = total[144 + 4 * r : 148 + 4 * r]
            ext[g, 12 + r, 4:8, :] = total[160 + 4 * r : 164 + 4 * r]
            ext[g, 12 + r, 16:20, :] = total[176 + 4 * r : 180 + 4 * r]

    for g in range(GROUPS):
        rim(g)
    @pl.when(group < 1)
    def _():
        send_up(range(GROUPS // 2, GROUPS))

    left = iota((DISP, 128), 1) < 64
    for g in range(GROUPS):

        @pl.when(g != group)
        def _():
            pltpu.make_async_remote_copy(
                src_ref=ops.at[g],
                dst_ref=ops.at[g],
                send_sem=ts_sem.at[g],
                recv_sem=tr_sem.at[g],
                device_id=peer(g),
                device_id_type=MESH,
            ).wait_recv()

        here = ops[g]
        turned = pltpu.roll(here, 64, 1)
        ta[g] = jnp.where(left, here, turned)
        tb[g] = jnp.where(left, turned, -here)
        high, low = split(translated(ext.at[g], ta.at[g], tb.at[g]))
        found[:, g * 256 : g * 256 + 128] = high
        found[:, g * 256 + 128 : g * 256 + 256] = low

    chosen = dot(pick, found[...])
    outer = (own_child == 0) | (own_child == 3)
    upper = own_child < 2
    tops, bottoms = [], []
    for g in range(GROUPS):
        value = chosen[:, g * 256 : g * 256 + 128] + chosen[:, g * 256 + 128 : g * 256 + 256]
        cosine = jnp.where(outer, turn[g, 0:1, :], turn[g, 2:3, :])
        sine = jnp.where(outer, turn[g, 1:2, :], turn[g, 3:4, :])
        sine = jnp.where(upper, sine, -sine)
        high, low = split(cosine * value + sine * pltpu.roll(value, 64, 1))
        tops += [high, high]
        bottoms += [low, jnp.zeros_like(low)]
    stacked = jnp.concatenate(
        [jnp.concatenate(tops, axis=1), jnp.concatenate(bottoms, axis=1)], axis=0
    )
    far = dot(stacked, base[...])

    live = iota((OWN, 128), 0) + group * OWN < count_ref[0]
    far = 0.25 * (far[:OWN] + far[OWN:])
    real = far[:, :128] + (close[:OWN, :128] - close[OWN:, 128:])
    imag = far[:, 128:] + (close[OWN:, :128] + close[:OWN, 128:])
    out_ref[0] = jnp.where(live, real, 0.0).astype(BF16)
    out_ref[1] = jnp.where(live, imag, 0.0).astype(BF16)

    for number in range(8):
        there, _, device = beside(number)

        @pl.when(there)
        def _():
            send_field(number, device).wait_send()

    for other in range(GROUPS):

        @pl.when(other != group)
        def _():
            send_ops(other).wait_send()


def on_device(across, tables, currents, box_code, box_count, radiation, near_block, translation):
    fold, phase, turn = tables
    operands = (
        box_code.reshape(1, CELLS),
        box_count,
        currents.reshape(2 * U, CELLS),
        radiation.reshape(2 * 128, U),
        near_block.reshape(9 * 2 * U, U),
        jnp.transpose(translation, (1, 2, 3, 0)).reshape(128, DISP),
        jnp.asarray(fold).reshape(GROUPS * 128, 128),
        jnp.asarray(phase),
        jnp.asarray(turn).reshape(GROUPS, 8, 128),
    )
    outside = pl.BlockSpec(memory_space=pltpu.HBM)
    result = pl.pallas_call(
        functools.partial(kernel, across),
        out_shape=jax.ShapeDtypeStruct((2, OWN, U), BF16),
        in_specs=[outside, pl.BlockSpec(memory_space=pltpu.SMEM)] + [outside] * 7,
        out_specs=pl.BlockSpec(memory_space=pltpu.VMEM),
        scratch_shapes=[
            pltpu.VMEM((1, CELLS), jnp.int32),
            pltpu.VMEM((256, 256), BF16),
            pltpu.VMEM((256, 128), BF16),
            pltpu.VMEM((9 * 256, 128), BF16),
            pltpu.VMEM((128, DISP), F32),
            pltpu.VMEM((GROUPS * 128, 128), BF16),
            pltpu.VMEM((GROUPS, SAMPLES, 128), F32),
            pltpu.VMEM((GROUPS, 8, 128), F32),
            pltpu.VMEM((GROUPS, DISP, 128), F32),
            pltpu.VMEM((GROUPS, DISP, 128), F32),
            pltpu.VMEM((GROUPS, DISP, 128), F32),
            pltpu.VMEM((256, 1024), BF16),
            pltpu.VMEM((64, 1024), BF16),
            pltpu.VMEM((GROUPS, 256, 1024), BF16),
            pltpu.VMEM((GROUPS * 256, 256), BF16),
            pltpu.VMEM((64, GROUPS * 256), BF16),
            pltpu.VMEM((GROUPS, 16, 24, 128), F32),
            pltpu.VMEM((CELLS, 128), jnp.int32),
            pltpu.SemaphoreType.DMA((8,)),
            pltpu.SemaphoreType.DMA((8,)),
            pltpu.SemaphoreType.DMA((8,)),
            pltpu.SemaphoreType.DMA((GROUPS,)),
            pltpu.SemaphoreType.DMA((GROUPS,)),
            pltpu.SemaphoreType.REGULAR((8,)),
            pltpu.SemaphoreType.REGULAR((GROUPS,)),
        ],
        compiler_params=pltpu.CompilerParams(
            collective_id=0, has_side_effects=True, vmem_limit_bytes=48 * 1024 * 1024
        ),
    )(*(pltpu.with_memory_space_constraint(x, pltpu.HBM) if x.size > 1 else x for x in operands))
    return jnp.transpose(result, (0, 2, 1))


def solution(mesh):
    across = math.isqrt(mesh.shape["box"])
    tables = make_tables()

    def step(*arrays):
        return on_device(across, tables, *arrays)

    placed = (P(None, None, "box"), P("box"), P("box"), P(), P(), P(None, None, None, "dir"))
    return jax.shard_map(
        step,
        mesh=mesh,
        in_specs=placed,
        out_specs=P(None, None, ("box", "dir")),
        check_vma=False,
    )
```

```python
import functools
import math

import jax
import jax.numpy as jnp
import ml_dtypes
import numpy as np
from jax import lax
from jax.experimental import pallas as pl
from jax.experimental.pallas import tpu as pltpu
from jax.sharding import PartitionSpec as P

U = 128
NT0 = 8
NP0 = 16
NT1 = 16
NP1 = 32
PSIDE = 8
CELLS = 256
GROUPS = 8
QL = NP1 // GROUPS
SAMPLES = NT1 * QL
OWN = CELLS // GROUPS
DISP = 40
EARLY = 1
MESH = pl.DeviceIdType.MESH
F32 = jnp.float32
BF16 = jnp.bfloat16

STEPS = ((1, 1), (-1, -1), (1, -1), (-1, 1), (1, 0), (-1, 0), (0, 1), (0, -1))
PIECES = (
    ("side", 48, 16, 192),
    ("side", 0, 16, 240),
    ("side", 16, 16, 208),
    ("side", 32, 16, 224),
    ("own", 32, 32, 64),
    ("own", 0, 32, 96),
    ("side", 32, 32, 128),
    ("side", 0, 32, 160),
)


def lagrange(offset, node):
    first = -(offset - 1.0) * (offset - 2.0) * (offset - 3.0) / 6.0
    second = offset * (offset - 2.0) * (offset - 3.0) / 2.0
    third = -offset * (offset - 1.0) * (offset - 3.0) / 2.0
    fourth = offset * (offset - 1.0) * (offset - 2.0) / 6.0
    return (
        np.where(node == 0, first, 0.0)
        + np.where(node == 1, second, 0.0)
        + np.where(node == 2, third, 0.0)
        + np.where(node == 3, fourth, 0.0)
    )


def make_tables():
    coarse = np.arange(NT1)[:, None]
    twice = 2 * coarse - 1
    base = np.clip(twice // 4 - 1, 0, NT0 - 4)
    theta = lagrange((twice - 4 * base) / 4.0, np.arange(NT0)[None, :] - base)
    coarse = np.arange(NP1)[:, None]
    twice = 2 * coarse - 1
    base = twice // 4 - 1
    phi = lagrange((twice - 4 * base) / 4.0, (np.arange(NP0)[None, :] - base) % NP0)
    polar = (np.arange(NT1) + 0.5) * math.pi / NT1
    azimuth = (np.arange(NP1) + 0.5) * 2.0 * math.pi / NP1
    fold = np.zeros((GROUPS, 2 * SAMPLES, NT0 * NP0), ml_dtypes.bfloat16)
    phase = np.zeros((GROUPS, SAMPLES, 128), np.float32)
    turn = np.zeros((GROUPS, 8, 2, SAMPLES), np.float32)
    for g in range(GROUPS):
        own = np.arange(g * QL, (g + 1) * QL)
        full = np.einsum("it,qp->iqtp", theta, phi[own]).reshape(SAMPLES, NT0 * NP0)
        high = full.astype(ml_dtypes.bfloat16)
        fold[g, :SAMPLES] = high
        fold[g, SAMPLES:] = (full - high.astype(np.float64)).astype(ml_dtypes.bfloat16)
        along_column = np.sin(polar)[:, None] * np.cos(azimuth[own])[None, :]
        along_row = np.sin(polar)[:, None] * np.sin(azimuth[own])[None, :]
        for child in range(2):
            psi = math.pi * (along_column * (child - 0.5) - along_row * 0.5)
            phase[g, :, 2 * child] = np.cos(psi).reshape(-1)
            phase[g, :, 2 * child + 1] = np.sin(psi).reshape(-1)
            turn[g, 2 * child] = np.cos(psi).reshape(-1)
            turn[g, 2 * child + 1, 0] = -np.sin(psi).reshape(-1)
            turn[g, 2 * child + 1, 1] = np.sin(psi).reshape(-1)
    return fold, phase, turn


def split(x):
    high = x.astype(BF16)
    low = (x - high.astype(F32)).astype(BF16)
    return high, low


def iota(shape, dim):
    return lax.broadcasted_iota(jnp.int32, shape, dim)


def dot(a, b):
    return jnp.dot(a, b, preferred_element_type=F32)


def dot_nt(a, b):
    return lax.dot_general(a, b, (((1,), (1,)), ((), ())), preferred_element_type=F32)


def displacements():
    return [
        (dy, dx) for dy in range(-3, 4) for dx in range(-3, 4) if max(abs(dy), abs(dx)) >= 2
    ]


def translated(parents, ta, tb):
    numbers = {pair: number for number, pair in enumerate(displacements())}
    first = [jnp.zeros((4, PSIDE, 128), F32) for _ in range(2)]
    second = [jnp.zeros((4, PSIDE, 128), F32) for _ in range(2)]
    odd_column = (iota((8, 2, PSIDE, 128), 2) & 1) == 1
    for dx in range(-3, 4):
        tile = parents[:, 8 + dx : 16 + dx, :].reshape(8, 2, PSIDE, 128)
        if dx == -3:
            tile = jnp.where(odd_column, tile, 0.0)
        if dx == 3:
            tile = jnp.where(odd_column, 0.0, tile)
        for dy in range(-3, 4):
            if (dy, dx) not in numbers:
                continue
            number = numbers[dy, dx]
            wa = ta[number : number + 1, :].reshape(1, 1, 128)
            wb = tb[number : number + 1, :].reshape(1, 1, 128)
            for parity in range(2):
                if dy == (-3 if parity == 0 else 3):
                    continue
                start = 4 + dy + parity
                source = tile[start // 2 : start // 2 + 4, start % 2]
                first[parity] = first[parity] + wa * source
                second[parity] = second[parity] + wb * source
    first = jnp.stack(first, axis=1).reshape(64, 128)
    second = jnp.stack(second, axis=1).reshape(64, 128)
    return first + pltpu.roll(second, 64, 1)


def kernel(
    across,
    code_hbm,
    count_ref,
    cur_hbm,
    rad_hbm,
    near_hbm,
    trans_hbm,
    fold_hbm,
    phase_hbm,
    turn_hbm,
    out_ref,
    code_ref,
    cur,
    rad,
    near,
    trans,
    fold,
    phase,
    turn,
    ops,
    ta,
    tb,
    field,
    side,
    mats,
    base,
    found,
    ext,
    index_col,
    load_sem,
    fs_sem,
    fr_sem,
    ts_sem,
    tr_sem,
    next_sem,
    above_sem,
):
    block = lax.axis_index("box")
    group = lax.axis_index("dir")
    row = block // across
    col = block % across

    loads = []
    for number, (source, target) in enumerate(
        (
            (trans_hbm.at[pl.ds(0, 64)], trans.at[pl.ds(0, 64)]),
            (code_hbm, code_ref),
            (cur_hbm, cur),
            (rad_hbm, rad),
            (fold_hbm, fold),
            (phase_hbm, phase),
            (near_hbm, near),
            (turn_hbm, turn),
            (trans_hbm.at[pl.ds(64, 64)], trans.at[pl.ds(64, 64)]),
        )
    ):
        copy = pltpu.make_async_copy(source, target, load_sem.at[number])
        loads.append(copy)

    loads[0].start()
    loads[8].start()

    def rank(r, c):
        usual = jnp.where(2 * r < across, 11 * r, 36 + 6 * (across - 1 - r))
        usual = (usual + 4 * c + 9 - 13 * (c & 1)) * across * across + r * across + c
        return jnp.where((group == 0) & (r == 0) & (c == 0), 1 << 20, usual)

    def beside(number):
        dr, dc = STEPS[number]
        r, c = row + dr, col + dc
        there = (r >= 0) & (r < across) & (c >= 0) & (c < across)
        return there, rank(r, c) < rank(row, col), (r * across + c, group)

    def peer(other):
        return (block, other)

    barrier = pltpu.get_barrier_semaphore()
    earlier = group
    for number in range(8):
        there, before, device = beside(number)

        @pl.when(there & jnp.logical_not(before))
        def _():
            pl.semaphore_signal(barrier, inc=1, device_id=device, device_id_type=MESH)

        earlier = earlier + jnp.where(there & before, 1, 0)
    for other in range(GROUPS):

        @pl.when(other > group)
        def _():
            pl.semaphore_signal(barrier, inc=1, device_id=peer(other), device_id_type=MESH)

    for copy in loads[1:6]:
        copy.start()

    @pl.when(earlier > 0)
    def _():
        pl.semaphore_wait(barrier, earlier)

    for other in range(GROUPS):

        @pl.when(other < group)
        def _():
            pl.semaphore_signal(
                above_sem.at[group], inc=1, device_id=peer(other), device_id_type=MESH
            )

    for number in range(8):
        there, before, device = beside(number)

        @pl.when(there & before)
        def _():
            pl.semaphore_signal(
                next_sem.at[number ^ 1], inc=1, device_id=device, device_id_type=MESH
            )

    loads[0].wait()
    loads[8].wait()
    ops[group] = jnp.transpose(trans[...])

    def send_ops(other):
        return pltpu.make_async_remote_copy(
            src_ref=ops.at[group],
            dst_ref=ops.at[group],
            send_sem=ts_sem.at[other],
            recv_sem=tr_sem.at[group],
            device_id=peer(other),
            device_id_type=MESH,
        )

    for other in range(GROUPS):

        @pl.when(other < group)
        def _():
            send_ops(other).start()

    for copy in loads[6:8]:
        copy.start()

    loads[1].wait()
    code = code_ref[...]
    across_c = ((code >> 2) & 1) + ((code >> 4) & 1) * 2 + ((code >> 6) & 1) * 4
    down_r = ((code >> 3) & 1) + ((code >> 5) & 1) * 2 + ((code >> 7) & 1) * 4
    index_row = (code & 3) * 64 + down_r * 8 + across_c
    live_index = jnp.where(iota((1, CELLS), 1) < count_ref[0], index_row, -1)
    line = iota((128, CELLS), 0)
    beyond = line - 64
    wanted = jnp.where(
        line < 64, line, ((beyond & 31) >> 2) * 8 + (beyond >> 5) * 4 + (beyond & 3)
    )
    loads[2].wait()
    place = jnp.concatenate(
        [
            jnp.where(wanted == live_index - child * 64, 1.0, 0.0).astype(BF16)
            for child in range(4)
        ],
        axis=0,
    )
    placed = dot_nt(place, cur[...]).astype(BF16)
    for child in range(4):
        field[0:64, pl.ds(child * 256, 256)] = placed[child * 128 : child * 128 + 64]
        side[:, pl.ds(child * 256, 256)] = placed[child * 128 + 64 : child * 128 + 128]

    def send_field(number, device):
        buffer, start, size, target = PIECES[number]
        source = field if buffer == "own" else side
        return pltpu.make_async_remote_copy(
            src_ref=source.at[pl.ds(start, size)],
            dst_ref=field.at[pl.ds(target, size)],
            send_sem=fs_sem.at[number],
            recv_sem=fr_sem.at[number],
            device_id=device,
            device_id_type=MESH,
        )

    def send_fields(numbers, turn_of):
        for number in numbers:
            there, before, device = beside(number)
            last = (group == 0) & (device[0] == 0)
            if turn_of == "before":
                due = before
            elif turn_of == "after":
                due = jnp.logical_not(before | last)
            else:
                due = last

            @pl.when(there & due)
            def _():
                if turn_of != "before":
                    pl.semaphore_wait(next_sem.at[number], 1)
                send_field(number, device).start()

    send_fields(range(8), "before")

    for edge, pieces in (
        (row == 0, ((64, 32), (192, 32))),
        (row == across - 1, ((96, 32), (224, 32))),
        (col == 0, ((128, 32), (192, 16), (224, 16))),
        (col == across - 1, ((160, 32), (208, 16), (240, 16))),
    ):

        @pl.when(edge)
        def _():
            for start, size in pieces:
                field[start : start + size, :] = jnp.zeros((size, 1024), BF16)
    loads[3].wait()
    loads[4].wait()
    loads[5].wait()

    def prepare(g):
        weights = fold[pl.ds(g * 128, 128), :]
        rr = dot(weights, rad[0:128, :])
        ri = dot(weights, rad[128:256, :])
        rr = rr[:64] + rr[64:]
        ri = ri[:64] + ri[64:]
        rrh, rrl = split(rr)
        rih, ril = split(ri)
        base[pl.ds(g * 256, 64), :] = jnp.concatenate([rrh, -rih], axis=1)
        base[pl.ds(g * 256 + 64, 64), :] = jnp.concatenate([rih, rrh], axis=1)
        base[pl.ds(g * 256 + 128, 64), :] = jnp.concatenate([rrl, -ril], axis=1)
        base[pl.ds(g * 256 + 192, 64), :] = jnp.concatenate([ril, rrl], axis=1)
        turns = phase[g]
        for pair in range(2):
            cosine = turns[:, 2 * pair : 2 * pair + 1]
            sine = turns[:, 2 * pair + 1 : 2 * pair + 2]
            cr, ci, sr, si = cosine * rr, cosine * ri, sine * rr, sine * ri
            for child, ar, ai in ((pair, cr + si, ci - sr), (3 - pair, cr - si, ci + sr)):
                arh, arl = split(ar)
                aih, ail = split(ai)
                matrix = jnp.concatenate(
                    [
                        jnp.concatenate([arh, -aih], axis=1),
                        jnp.concatenate([aih, arh], axis=1),
                        jnp.concatenate([arl, -ail], axis=1),
                        jnp.concatenate([ail, arl], axis=1),
                    ],
                    axis=0,
                )
                mats[g, :, pl.ds(child * 256, 256)] = matrix
        total = dot_nt(field[0:64, :], mats[g])
        total = total[:, :128] + total[:, 128:]
        ext[g, 4:12, 8:16, :] = total.reshape(PSIDE, PSIDE, 128)

    for g in range(GROUPS):
        if g == EARLY:
            send_fields((0, 1, 2, 3, 4, 5), "after")
        prepare(g)
    send_fields((6, 7), "after")
    index_col[...] = jnp.transpose(jnp.broadcast_to(index_row, (128, CELLS)))
    own_index = index_col[pl.ds(pl.multiple_of(group * OWN, OWN), OWN), :]
    pick = jnp.where((own_index[:, :64] & 63) == iota((OWN, 64), 1), 1.0, 0.0).astype(BF16)
    own_child = own_index >> 6
    own_r = ((own_index >> 3) & 7) * 2 + (own_index >> 7)
    own_c = (own_index & 7) * 2 + ((own_index >> 6) & 1)
    hot = []
    for dr in (-1, 0, 1):
        for dc in (-1, 0, 1):
            r, c = own_r + dr, own_c + dc
            child = (r & 1) * 2 + (c & 1)
            pr, pc = r >> 1, c >> 1
            north, south, west, east = pr < 0, pr > 7, pc < 0, pc > 7
            at = jnp.where(west, 131 + pr * 4, jnp.where(east, 160 + pr * 4, pr * 8 + pc))
            at = jnp.where(north, jnp.where(west, 207, jnp.where(east, 220, 88 + pc)), at)
            at = jnp.where(south, jnp.where(west, 227, jnp.where(east, 240, 96 + pc)), at)
            at = at + child * 256
            hot.append(
                jnp.concatenate(
                    [
                        jnp.where(at == iota((OWN, 128), 1) + start, 1.0, 0.0).astype(BF16)
                        for start in range(0, 1024, 128)
                    ],
                    axis=1,
                )
            )
    hot = jnp.concatenate(hot, axis=0)
    def send_up(others):
        for other in others:

            @pl.when(other > group)
            def _():
                pl.semaphore_wait(above_sem.at[other], 1)
                send_ops(other).start()

    send_up(range(1, GROUPS // 2))

    @pl.when(group >= 1)
    def _():
        send_up(range(GROUPS // 2, GROUPS))

    send_fields(range(8), "last")
    for number in range(8):
        there, _, device = beside(number ^ 1)

        @pl.when(there)
        def _():
            send_field(number, device).wait_recv()

    around = jnp.zeros((9 * OWN, 256), F32)
    for child in range(4):
        lanes = pl.ds(child * 256, 256)
        around = around + dot(hot[:, child * 256 : (child + 1) * 256], field[:, lanes])
    around = around.astype(BF16)
    loads[6].wait()
    loads[7].wait()
    close = jnp.zeros((2 * OWN, 256), F32)
    for number in range(9):
        mine = around[number * OWN : (number + 1) * OWN]
        stacked = jnp.concatenate([mine[:, :128], mine[:, 128:]], axis=0)
        close = close + dot_nt(stacked, near[pl.ds(number * 256, 256), :])
    def rim(g):
        total = dot_nt(field[64:256, :], mats[g])
        total = total[:, :128] + total[:, 128:]
        ext[g, 0:4, 8:16, :] = total[0:32].reshape(4, 8, 128)
        ext[g, 12:16, 8:16, :] = total[32:64].reshape(4, 8, 128)
        for r in range(8):
            ext[g, 4 + r, 4:8, :] = total[64 + 4 * r : 68 + 4 * r]
            ext[g, 4 + r, 16:20, :] = total[96 + 4 * r : 100 + 4 * r]
        for r in range(4):
            ext[g, r, 4:8, :] = total[128 + 4 * r : 132 + 4 * r]
            ext[g, r, 16:20, :] = total[144 + 4 * r : 148 + 4 * r]
            ext[g, 12 + r, 4:8, :] = total[160 + 4 * r : 164 + 4 * r]
            ext[g, 12 + r, 16:20, :] = total[176 + 4 * r : 180 + 4 * r]

    for g in range(GROUPS):
        rim(g)
    @pl.when(group < 1)
    def _():
        send_up(range(GROUPS // 2, GROUPS))

    left = iota((DISP, 128), 1) < 64
    for g in range(GROUPS):

        @pl.when(g != group)
        def _():
            pltpu.make_async_remote_copy(
                src_ref=ops.at[g],
                dst_ref=ops.at[g],
                send_sem=ts_sem.at[g],
                recv_sem=tr_sem.at[g],
                device_id=peer(g),
                device_id_type=MESH,
            ).wait_recv()

        here = ops[g]
        turned = pltpu.roll(here, 64, 1)
        ta[g] = jnp.where(left, here, turned)
        tb[g] = jnp.where(left, turned, -here)
        high, low = split(translated(ext.at[g], ta.at[g], tb.at[g]))
        found[:, g * 256 : g * 256 + 128] = high
        found[:, g * 256 + 128 : g * 256 + 256] = low

    chosen = dot(pick, found[...])
    outer = (own_child == 0) | (own_child == 3)
    upper = own_child < 2
    tops, bottoms = [], []
    for g in range(GROUPS):
        value = chosen[:, g * 256 : g * 256 + 128] + chosen[:, g * 256 + 128 : g * 256 + 256]
        cosine = jnp.where(outer, turn[g, 0:1, :], turn[g, 2:3, :])
        sine = jnp.where(outer, turn[g, 1:2, :], turn[g, 3:4, :])
        sine = jnp.where(upper, sine, -sine)
        high, low = split(cosine * value + sine * pltpu.roll(value, 64, 1))
        tops += [high, high]
        bottoms += [low, jnp.zeros_like(low)]
    stacked = jnp.concatenate(
        [jnp.concatenate(tops, axis=1), jnp.concatenate(bottoms, axis=1)], axis=0
    )
    far = dot(stacked, base[...])

    live = iota((OWN, 128), 0) + group * OWN < count_ref[0]
    far = 0.25 * (far[:OWN] + far[OWN:])
    real = far[:, :128] + (close[:OWN, :128] - close[OWN:, 128:])
    imag = far[:, 128:] + (close[OWN:, :128] + close[:OWN, 128:])
    out_ref[0] = jnp.where(live, real, 0.0).astype(BF16)
    out_ref[1] = jnp.where(live, imag, 0.0).astype(BF16)

    for number in range(8):
        there, _, device = beside(number)

        @pl.when(there)
        def _():
            send_field(number, device).wait_send()

    for other in range(GROUPS):

        @pl.when(other != group)
        def _():
            send_ops(other).wait_send()


def on_device(across, tables, currents, box_code, box_count, radiation, near_block, translation):
    fold, phase, turn = tables
    operands = (
        box_code.reshape(1, CELLS),
        box_count,
        currents.reshape(2 * U, CELLS),
        radiation.reshape(2 * 128, U),
        near_block.reshape(9 * 2 * U, U),
        jnp.transpose(translation, (1, 2, 3, 0)).reshape(128, DISP),
        jnp.asarray(fold).reshape(GROUPS * 128, 128),
        jnp.asarray(phase),
        jnp.asarray(turn).reshape(GROUPS, 8, 128),
    )
    outside = pl.BlockSpec(memory_space=pltpu.HBM)
    result = pl.pallas_call(
        functools.partial(kernel, across),
        out_shape=jax.ShapeDtypeStruct((2, OWN, U), BF16),
        in_specs=[outside, pl.BlockSpec(memory_space=pltpu.SMEM)] + [outside] * 7,
        out_specs=pl.BlockSpec(memory_space=pltpu.VMEM),
        scratch_shapes=[
            pltpu.VMEM((1, CELLS), jnp.int32),
            pltpu.VMEM((256, 256), BF16),
            pltpu.VMEM((256, 128), BF16),
            pltpu.VMEM((9 * 256, 128), BF16),
            pltpu.VMEM((128, DISP), F32),
            pltpu.VMEM((GROUPS * 128, 128), BF16),
            pltpu.VMEM((GROUPS, SAMPLES, 128), F32),
            pltpu.VMEM((GROUPS, 8, 128), F32),
            pltpu.VMEM((GROUPS, DISP, 128), F32),
            pltpu.VMEM((GROUPS, DISP, 128), F32),
            pltpu.VMEM((GROUPS, DISP, 128), F32),
            pltpu.VMEM((256, 1024), BF16),
            pltpu.VMEM((64, 1024), BF16),
            pltpu.VMEM((GROUPS, 256, 1024), BF16),
            pltpu.VMEM((GROUPS * 256, 256), BF16),
            pltpu.VMEM((64, GROUPS * 256), BF16),
            pltpu.VMEM((GROUPS, 16, 24, 128), F32),
            pltpu.VMEM((CELLS, 128), jnp.int32),
            pltpu.SemaphoreType.DMA((9,)),
            pltpu.SemaphoreType.DMA((8,)),
            pltpu.SemaphoreType.DMA((8,)),
            pltpu.SemaphoreType.DMA((GROUPS,)),
            pltpu.SemaphoreType.DMA((GROUPS,)),
            pltpu.SemaphoreType.REGULAR((8,)),
            pltpu.SemaphoreType.REGULAR((GROUPS,)),
        ],
        compiler_params=pltpu.CompilerParams(
            collective_id=0, has_side_effects=True, vmem_limit_bytes=48 * 1024 * 1024
        ),
    )(*(pltpu.with_memory_space_constraint(x, pltpu.HBM) if x.size > 1 else x for x in operands))
    return jnp.transpose(result, (0, 2, 1))


def solution(mesh):
    across = math.isqrt(mesh.shape["box"])
    tables = make_tables()

    def step(*arrays):
        return on_device(across, tables, *arrays)

    placed = (P(None, None, "box"), P("box"), P("box"), P(), P(), P(None, None, None, "dir"))
    return jax.shard_map(
        step,
        mesh=mesh,
        in_specs=placed,
        out_specs=P(None, None, ("box", "dir")),
        check_vma=False,
    )
```

```python
import functools
import math

import jax
import jax.numpy as jnp
import ml_dtypes
import numpy as np
from jax import lax
from jax.experimental import pallas as pl
from jax.experimental.pallas import tpu as pltpu
from jax.sharding import PartitionSpec as P

U = 128
NT0 = 8
NP0 = 16
NT1 = 16
NP1 = 32
PSIDE = 8
CELLS = 256
GROUPS = 8
QL = NP1 // GROUPS
SAMPLES = NT1 * QL
OWN = CELLS // GROUPS
DISP = 40
EARLY = 1
MESH = pl.DeviceIdType.MESH
F32 = jnp.float32
BF16 = jnp.bfloat16

STEPS = ((1, 1), (-1, -1), (1, -1), (-1, 1), (1, 0), (-1, 0), (0, 1), (0, -1))
PIECES = (
    ("side", 48, 16, 192),
    ("side", 0, 16, 240),
    ("side", 16, 16, 208),
    ("side", 32, 16, 224),
    ("own", 32, 32, 64),
    ("own", 0, 32, 96),
    ("side", 32, 32, 128),
    ("side", 0, 32, 160),
)


def lagrange(offset, node):
    first = -(offset - 1.0) * (offset - 2.0) * (offset - 3.0) / 6.0
    second = offset * (offset - 2.0) * (offset - 3.0) / 2.0
    third = -offset * (offset - 1.0) * (offset - 3.0) / 2.0
    fourth = offset * (offset - 1.0) * (offset - 2.0) / 6.0
    return (
        np.where(node == 0, first, 0.0)
        + np.where(node == 1, second, 0.0)
        + np.where(node == 2, third, 0.0)
        + np.where(node == 3, fourth, 0.0)
    )


def make_tables():
    coarse = np.arange(NT1)[:, None]
    twice = 2 * coarse - 1
    base = np.clip(twice // 4 - 1, 0, NT0 - 4)
    theta = lagrange((twice - 4 * base) / 4.0, np.arange(NT0)[None, :] - base)
    coarse = np.arange(NP1)[:, None]
    twice = 2 * coarse - 1
    base = twice // 4 - 1
    phi = lagrange((twice - 4 * base) / 4.0, (np.arange(NP0)[None, :] - base) % NP0)
    polar = (np.arange(NT1) + 0.5) * math.pi / NT1
    azimuth = (np.arange(NP1) + 0.5) * 2.0 * math.pi / NP1
    fold = np.zeros((GROUPS, 2 * SAMPLES, NT0 * NP0), ml_dtypes.bfloat16)
    phase = np.zeros((GROUPS, SAMPLES, 128), np.float32)
    turn = np.zeros((GROUPS, 8, 2, SAMPLES), np.float32)
    for g in range(GROUPS):
        own = np.arange(g * QL, (g + 1) * QL)
        full = np.einsum("it,qp->iqtp", theta, phi[own]).reshape(SAMPLES, NT0 * NP0)
        high = full.astype(ml_dtypes.bfloat16)
        fold[g, :SAMPLES] = high
        fold[g, SAMPLES:] = (full - high.astype(np.float64)).astype(ml_dtypes.bfloat16)
        along_column = np.sin(polar)[:, None] * np.cos(azimuth[own])[None, :]
        along_row = np.sin(polar)[:, None] * np.sin(azimuth[own])[None, :]
        for child in range(2):
            psi = math.pi * (along_column * (child - 0.5) - along_row * 0.5)
            phase[g, :, 2 * child] = np.cos(psi).reshape(-1)
            phase[g, :, 2 * child + 1] = np.sin(psi).reshape(-1)
            turn[g, 2 * child] = np.cos(psi).reshape(-1)
            turn[g, 2 * child + 1, 0] = -np.sin(psi).reshape(-1)
            turn[g, 2 * child + 1, 1] = np.sin(psi).reshape(-1)
    return fold, phase, turn


def split(x):
    high = x.astype(BF16)
    low = (x - high.astype(F32)).astype(BF16)
    return high, low


def iota(shape, dim):
    return lax.broadcasted_iota(jnp.int32, shape, dim)


def dot(a, b):
    return jnp.dot(a, b, preferred_element_type=F32)


def dot_nt(a, b):
    return lax.dot_general(a, b, (((1,), (1,)), ((), ())), preferred_element_type=F32)


def displacements():
    return [
        (dy, dx) for dy in range(-3, 4) for dx in range(-3, 4) if max(abs(dy), abs(dx)) >= 2
    ]


def translated(parents, ta, tb):
    numbers = {pair: number for number, pair in enumerate(displacements())}
    first = [jnp.zeros((4, PSIDE, 128), F32) for _ in range(2)]
    second = [jnp.zeros((4, PSIDE, 128), F32) for _ in range(2)]
    odd_column = (iota((8, 2, PSIDE, 128), 2) & 1) == 1
    for dx in range(-3, 4):
        tile = parents[:, 8 + dx : 16 + dx, :].reshape(8, 2, PSIDE, 128)
        if dx == -3:
            tile = jnp.where(odd_column, tile, 0.0)
        if dx == 3:
            tile = jnp.where(odd_column, 0.0, tile)
        for dy in range(-3, 4):
            if (dy, dx) not in numbers:
                continue
            number = numbers[dy, dx]
            wa = ta[number : number + 1, :].reshape(1, 1, 128)
            wb = tb[number : number + 1, :].reshape(1, 1, 128)
            for parity in range(2):
                if dy == (-3 if parity == 0 else 3):
                    continue
                start = 4 + dy + parity
                source = tile[start // 2 : start // 2 + 4, start % 2]
                first[parity] = first[parity] + wa * source
                second[parity] = second[parity] + wb * source
    first = jnp.stack(first, axis=1).reshape(64, 128)
    second = jnp.stack(second, axis=1).reshape(64, 128)
    return first + pltpu.roll(second, 64, 1)


def kernel(
    across,
    code_hbm,
    count_ref,
    cur_hbm,
    rad_hbm,
    near_hbm,
    trans_hbm,
    fold_hbm,
    phase_hbm,
    turn_hbm,
    out_ref,
    code_ref,
    cur,
    rad,
    near,
    trans,
    fold,
    phase,
    turn,
    ops,
    ta,
    tb,
    field,
    side,
    mats,
    base,
    found,
    ext,
    index_col,
    load_sem,
    fs_sem,
    fr_sem,
    ts_sem,
    tr_sem,
    next_sem,
    above_sem,
):
    block = lax.axis_index("box")
    group = lax.axis_index("dir")
    row = block // across
    col = block % across

    loads = []
    for number, (source, target) in enumerate(
        (
            (trans_hbm.at[pl.ds(0, 64)], trans.at[pl.ds(0, 64)]),
            (code_hbm, code_ref),
            (cur_hbm, cur),
            (rad_hbm, rad),
            (fold_hbm, fold),
            (phase_hbm, phase),
            (near_hbm, near),
            (turn_hbm, turn),
            (trans_hbm.at[pl.ds(64, 64)], trans.at[pl.ds(64, 64)]),
        )
    ):
        copy = pltpu.make_async_copy(source, target, load_sem.at[number])
        loads.append(copy)

    loads[0].start()
    loads[8].start()

    def rank(r, c):
        usual = jnp.where(2 * r < across, 11 * r, 36 + 6 * (across - 1 - r))
        usual = (usual + 4 * c + 9 - 13 * (c & 1)) * across * across + r * across + c
        return jnp.where((group == 0) & (r == 0) & (c == 0), 1 << 20, usual)

    def beside(number):
        dr, dc = STEPS[number]
        r, c = row + dr, col + dc
        there = (r >= 0) & (r < across) & (c >= 0) & (c < across)
        return there, rank(r, c) < rank(row, col), (r * across + c, group)

    def peer(other):
        return (block, other)

    barrier = pltpu.get_barrier_semaphore()
    earlier = group
    for number in range(8):
        there, before, device = beside(number)

        @pl.when(there & jnp.logical_not(before))
        def _():
            pl.semaphore_signal(barrier, inc=1, device_id=device, device_id_type=MESH)

        earlier = earlier + jnp.where(there & before, 1, 0)
    for other in range(GROUPS):

        @pl.when(other > group)
        def _():
            pl.semaphore_signal(barrier, inc=1, device_id=peer(other), device_id_type=MESH)

    for copy in loads[1:6]:
        copy.start()

    loads[0].wait()
    loads[8].wait()
    ops[group] = jnp.transpose(trans[...])

    @pl.when(earlier > 0)
    def _():
        pl.semaphore_wait(barrier, earlier)

    def send_ops(other):
        return pltpu.make_async_remote_copy(
            src_ref=ops.at[group],
            dst_ref=ops.at[group],
            send_sem=ts_sem.at[other],
            recv_sem=tr_sem.at[group],
            device_id=peer(other),
            device_id_type=MESH,
        )

    for other in range(GROUPS):

        @pl.when(other < group)
        def _():
            send_ops(other).start()

    for other in range(GROUPS):

        @pl.when(other < group)
        def _():
            pl.semaphore_signal(
                above_sem.at[group], inc=1, device_id=peer(other), device_id_type=MESH
            )

    for number in range(8):
        there, before, device = beside(number)

        @pl.when(there & before)
        def _():
            pl.semaphore_signal(
                next_sem.at[number ^ 1], inc=1, device_id=device, device_id_type=MESH
            )


    for copy in loads[6:8]:
        copy.start()

    loads[1].wait()
    code = code_ref[...]
    across_c = ((code >> 2) & 1) + ((code >> 4) & 1) * 2 + ((code >> 6) & 1) * 4
    down_r = ((code >> 3) & 1) + ((code >> 5) & 1) * 2 + ((code >> 7) & 1) * 4
    index_row = (code & 3) * 64 + down_r * 8 + across_c
    live_index = jnp.where(iota((1, CELLS), 1) < count_ref[0], index_row, -1)
    line = iota((128, CELLS), 0)
    beyond = line - 64
    wanted = jnp.where(
        line < 64, line, ((beyond & 31) >> 2) * 8 + (beyond >> 5) * 4 + (beyond & 3)
    )
    loads[2].wait()
    place = jnp.concatenate(
        [
            jnp.where(wanted == live_index - child * 64, 1.0, 0.0).astype(BF16)
            for child in range(4)
        ],
        axis=0,
    )
    placed = dot_nt(place, cur[...]).astype(BF16)
    for child in range(4):
        field[0:64, pl.ds(child * 256, 256)] = placed[child * 128 : child * 128 + 64]
        side[:, pl.ds(child * 256, 256)] = placed[child * 128 + 64 : child * 128 + 128]

    def send_field(number, device):
        buffer, start, size, target = PIECES[number]
        source = field if buffer == "own" else side
        return pltpu.make_async_remote_copy(
            src_ref=source.at[pl.ds(start, size)],
            dst_ref=field.at[pl.ds(target, size)],
            send_sem=fs_sem.at[number],
            recv_sem=fr_sem.at[number],
            device_id=device,
            device_id_type=MESH,
        )

    def send_fields(numbers, turn_of):
        for number in numbers:
            there, before, device = beside(number)
            last = (group == 0) & (device[0] == 0)
            if turn_of == "before":
                due = before
            elif turn_of == "after":
                due = jnp.logical_not(before | last)
            else:
                due = last

            @pl.when(there & due)
            def _():
                if turn_of != "before":
                    pl.semaphore_wait(next_sem.at[number], 1)
                send_field(number, device).start()

    send_fields(range(8), "before")

    for edge, pieces in (
        (row == 0, ((64, 32), (192, 32))),
        (row == across - 1, ((96, 32), (224, 32))),
        (col == 0, ((128, 32), (192, 16), (224, 16))),
        (col == across - 1, ((160, 32), (208, 16), (240, 16))),
    ):

        @pl.when(edge)
        def _():
            for start, size in pieces:
                field[start : start + size, :] = jnp.zeros((size, 1024), BF16)
    loads[3].wait()
    loads[4].wait()
    loads[5].wait()

    def prepare(g):
        weights = fold[pl.ds(g * 128, 128), :]
        rr = dot(weights, rad[0:128, :])
        ri = dot(weights, rad[128:256, :])
        rr = rr[:64] + rr[64:]
        ri = ri[:64] + ri[64:]
        rrh, rrl = split(rr)
        rih, ril = split(ri)
        base[pl.ds(g * 256, 64), :] = jnp.concatenate([rrh, -rih], axis=1)
        base[pl.ds(g * 256 + 64, 64), :] = jnp.concatenate([rih, rrh], axis=1)
        base[pl.ds(g * 256 + 128, 64), :] = jnp.concatenate([rrl, -ril], axis=1)
        base[pl.ds(g * 256 + 192, 64), :] = jnp.concatenate([ril, rrl], axis=1)
        turns = phase[g]
        for pair in range(2):
            cosine = turns[:, 2 * pair : 2 * pair + 1]
            sine = turns[:, 2 * pair + 1 : 2 * pair + 2]
            cr, ci, sr, si = cosine * rr, cosine * ri, sine * rr, sine * ri
            for child, ar, ai in ((pair, cr + si, ci - sr), (3 - pair, cr - si, ci + sr)):
                arh, arl = split(ar)
                aih, ail = split(ai)
                matrix = jnp.concatenate(
                    [
                        jnp.concatenate([arh, -aih], axis=1),
                        jnp.concatenate([aih, arh], axis=1),
                        jnp.concatenate([arl, -ail], axis=1),
                        jnp.concatenate([ail, arl], axis=1),
                    ],
                    axis=0,
                )
                mats[g, :, pl.ds(child * 256, 256)] = matrix
        total = dot_nt(field[0:64, :], mats[g])
        total = total[:, :128] + total[:, 128:]
        ext[g, 4:12, 8:16, :] = total.reshape(PSIDE, PSIDE, 128)

    for g in range(GROUPS):
        if g == EARLY:
            send_fields((0, 1, 2, 3, 4, 5), "after")
        prepare(g)
    send_fields((6, 7), "after")
    index_col[...] = jnp.transpose(jnp.broadcast_to(index_row, (128, CELLS)))
    own_index = index_col[pl.ds(pl.multiple_of(group * OWN, OWN), OWN), :]
    pick = jnp.where((own_index[:, :64] & 63) == iota((OWN, 64), 1), 1.0, 0.0).astype(BF16)
    own_child = own_index >> 6
    own_r = ((own_index >> 3) & 7) * 2 + (own_index >> 7)
    own_c = (own_index & 7) * 2 + ((own_index >> 6) & 1)
    hot = []
    for dr in (-1, 0, 1):
        for dc in (-1, 0, 1):
            r, c = own_r + dr, own_c + dc
            child = (r & 1) * 2 + (c & 1)
            pr, pc = r >> 1, c >> 1
            north, south, west, east = pr < 0, pr > 7, pc < 0, pc > 7
            at = jnp.where(west, 131 + pr * 4, jnp.where(east, 160 + pr * 4, pr * 8 + pc))
            at = jnp.where(north, jnp.where(west, 207, jnp.where(east, 220, 88 + pc)), at)
            at = jnp.where(south, jnp.where(west, 227, jnp.where(east, 240, 96 + pc)), at)
            at = at + child * 256
            hot.append(
                jnp.concatenate(
                    [
                        jnp.where(at == iota((OWN, 128), 1) + start, 1.0, 0.0).astype(BF16)
                        for start in range(0, 1024, 128)
                    ],
                    axis=1,
                )
            )
    hot = jnp.concatenate(hot, axis=0)
    def send_up(others):
        for other in others:

            @pl.when(other > group)
            def _():
                pl.semaphore_wait(above_sem.at[other], 1)
                send_ops(other).start()

    send_up(range(1, GROUPS // 2))

    @pl.when(group >= 1)
    def _():
        send_up(range(GROUPS // 2, GROUPS))

    send_fields(range(8), "last")
    for number in range(8):
        there, _, device = beside(number ^ 1)

        @pl.when(there)
        def _():
            send_field(number, device).wait_recv()

    around = jnp.zeros((9 * OWN, 256), F32)
    for child in range(4):
        lanes = pl.ds(child * 256, 256)
        around = around + dot(hot[:, child * 256 : (child + 1) * 256], field[:, lanes])
    around = around.astype(BF16)
    loads[6].wait()
    loads[7].wait()
    close = jnp.zeros((2 * OWN, 256), F32)
    for number in range(9):
        mine = around[number * OWN : (number + 1) * OWN]
        stacked = jnp.concatenate([mine[:, :128], mine[:, 128:]], axis=0)
        close = close + dot_nt(stacked, near[pl.ds(number * 256, 256), :])
    def rim(g):
        total = dot_nt(field[64:256, :], mats[g])
        total = total[:, :128] + total[:, 128:]
        ext[g, 0:4, 8:16, :] = total[0:32].reshape(4, 8, 128)
        ext[g, 12:16, 8:16, :] = total[32:64].reshape(4, 8, 128)
        for r in range(8):
            ext[g, 4 + r, 4:8, :] = total[64 + 4 * r : 68 + 4 * r]
            ext[g, 4 + r, 16:20, :] = total[96 + 4 * r : 100 + 4 * r]
        for r in range(4):
            ext[g, r, 4:8, :] = total[128 + 4 * r : 132 + 4 * r]
            ext[g, r, 16:20, :] = total[144 + 4 * r : 148 + 4 * r]
            ext[g, 12 + r, 4:8, :] = total[160 + 4 * r : 164 + 4 * r]
            ext[g, 12 + r, 16:20, :] = total[176 + 4 * r : 180 + 4 * r]

    for g in range(GROUPS):
        rim(g)
    @pl.when(group < 1)
    def _():
        send_up(range(GROUPS // 2, GROUPS))

    left = iota((DISP, 128), 1) < 64
    for g in range(GROUPS):

        @pl.when(g != group)
        def _():
            pltpu.make_async_remote_copy(
                src_ref=ops.at[g],
                dst_ref=ops.at[g],
                send_sem=ts_sem.at[g],
                recv_sem=tr_sem.at[g],
                device_id=peer(g),
                device_id_type=MESH,
            ).wait_recv()

        here = ops[g]
        turned = pltpu.roll(here, 64, 1)
        ta[g] = jnp.where(left, here, turned)
        tb[g] = jnp.where(left, turned, -here)
        high, low = split(translated(ext.at[g], ta.at[g], tb.at[g]))
        found[:, g * 256 : g * 256 + 128] = high
        found[:, g * 256 + 128 : g * 256 + 256] = low

    chosen = dot(pick, found[...])
    outer = (own_child == 0) | (own_child == 3)
    upper = own_child < 2
    tops, bottoms = [], []
    for g in range(GROUPS):
        value = chosen[:, g * 256 : g * 256 + 128] + chosen[:, g * 256 + 128 : g * 256 + 256]
        cosine = jnp.where(outer, turn[g, 0:1, :], turn[g, 2:3, :])
        sine = jnp.where(outer, turn[g, 1:2, :], turn[g, 3:4, :])
        sine = jnp.where(upper, sine, -sine)
        high, low = split(cosine * value + sine * pltpu.roll(value, 64, 1))
        tops += [high, high]
        bottoms += [low, jnp.zeros_like(low)]
    stacked = jnp.concatenate(
        [jnp.concatenate(tops, axis=1), jnp.concatenate(bottoms, axis=1)], axis=0
    )
    far = dot(stacked, base[...])

    live = iota((OWN, 128), 0) + group * OWN < count_ref[0]
    far = 0.25 * (far[:OWN] + far[OWN:])
    real = far[:, :128] + (close[:OWN, :128] - close[OWN:, 128:])
    imag = far[:, 128:] + (close[OWN:, :128] + close[:OWN, 128:])
    out_ref[0] = jnp.where(live, real, 0.0).astype(BF16)
    out_ref[1] = jnp.where(live, imag, 0.0).astype(BF16)

    for number in range(8):
        there, _, device = beside(number)

        @pl.when(there)
        def _():
            send_field(number, device).wait_send()

    for other in range(GROUPS):

        @pl.when(other != group)
        def _():
            send_ops(other).wait_send()


def on_device(across, tables, currents, box_code, box_count, radiation, near_block, translation):
    fold, phase, turn = tables
    operands = (
        box_code.reshape(1, CELLS),
        box_count,
        currents.reshape(2 * U, CELLS),
        radiation.reshape(2 * 128, U),
        near_block.reshape(9 * 2 * U, U),
        jnp.transpose(translation, (1, 2, 3, 0)).reshape(128, DISP),
        jnp.asarray(fold).reshape(GROUPS * 128, 128),
        jnp.asarray(phase),
        jnp.asarray(turn).reshape(GROUPS, 8, 128),
    )
    outside = pl.BlockSpec(memory_space=pltpu.HBM)
    result = pl.pallas_call(
        functools.partial(kernel, across),
        out_shape=jax.ShapeDtypeStruct((2, OWN, U), BF16),
        in_specs=[outside, pl.BlockSpec(memory_space=pltpu.SMEM)] + [outside] * 7,
        out_specs=pl.BlockSpec(memory_space=pltpu.VMEM),
        scratch_shapes=[
            pltpu.VMEM((1, CELLS), jnp.int32),
            pltpu.VMEM((256, 256), BF16),
            pltpu.VMEM((256, 128), BF16),
            pltpu.VMEM((9 * 256, 128), BF16),
            pltpu.VMEM((128, DISP), F32),
            pltpu.VMEM((GROUPS * 128, 128), BF16),
            pltpu.VMEM((GROUPS, SAMPLES, 128), F32),
            pltpu.VMEM((GROUPS, 8, 128), F32),
            pltpu.VMEM((GROUPS, DISP, 128), F32),
            pltpu.VMEM((GROUPS, DISP, 128), F32),
            pltpu.VMEM((GROUPS, DISP, 128), F32),
            pltpu.VMEM((256, 1024), BF16),
            pltpu.VMEM((64, 1024), BF16),
            pltpu.VMEM((GROUPS, 256, 1024), BF16),
            pltpu.VMEM((GROUPS * 256, 256), BF16),
            pltpu.VMEM((64, GROUPS * 256), BF16),
            pltpu.VMEM((GROUPS, 16, 24, 128), F32),
            pltpu.VMEM((CELLS, 128), jnp.int32),
            pltpu.SemaphoreType.DMA((9,)),
            pltpu.SemaphoreType.DMA((8,)),
            pltpu.SemaphoreType.DMA((8,)),
            pltpu.SemaphoreType.DMA((GROUPS,)),
            pltpu.SemaphoreType.DMA((GROUPS,)),
            pltpu.SemaphoreType.REGULAR((8,)),
            pltpu.SemaphoreType.REGULAR((GROUPS,)),
        ],
        compiler_params=pltpu.CompilerParams(
            collective_id=0, has_side_effects=True, vmem_limit_bytes=48 * 1024 * 1024
        ),
    )(*(pltpu.with_memory_space_constraint(x, pltpu.HBM) if x.size > 1 else x for x in operands))
    return jnp.transpose(result, (0, 2, 1))


def solution(mesh):
    across = math.isqrt(mesh.shape["box"])
    tables = make_tables()

    def step(*arrays):
        return on_device(across, tables, *arrays)

    placed = (P(None, None, "box"), P("box"), P("box"), P(), P(), P(None, None, None, "dir"))
    return jax.shard_map(
        step,
        mesh=mesh,
        in_specs=placed,
        out_specs=P(None, None, ("box", "dir")),
        check_vma=False,
    )
```

```python
import functools
import math

import jax
import jax.numpy as jnp
import ml_dtypes
import numpy as np
from jax import lax
from jax.experimental import pallas as pl
from jax.experimental.pallas import tpu as pltpu
from jax.sharding import PartitionSpec as P

U = 128
NT0 = 8
NP0 = 16
NT1 = 16
NP1 = 32
PSIDE = 8
CELLS = 256
GROUPS = 8
QL = NP1 // GROUPS
SAMPLES = NT1 * QL
OWN = CELLS // GROUPS
DISP = 40
EARLY = 1
MESH = pl.DeviceIdType.MESH
F32 = jnp.float32
BF16 = jnp.bfloat16

STEPS = ((1, 1), (-1, -1), (1, -1), (-1, 1), (1, 0), (-1, 0), (0, 1), (0, -1))
PIECES = (
    ("side", 48, 16, 192),
    ("side", 0, 16, 240),
    ("side", 16, 16, 208),
    ("side", 32, 16, 224),
    ("own", 32, 32, 64),
    ("own", 0, 32, 96),
    ("side", 32, 32, 128),
    ("side", 0, 32, 160),
)


def lagrange(offset, node):
    first = -(offset - 1.0) * (offset - 2.0) * (offset - 3.0) / 6.0
    second = offset * (offset - 2.0) * (offset - 3.0) / 2.0
    third = -offset * (offset - 1.0) * (offset - 3.0) / 2.0
    fourth = offset * (offset - 1.0) * (offset - 2.0) / 6.0
    return (
        np.where(node == 0, first, 0.0)
        + np.where(node == 1, second, 0.0)
        + np.where(node == 2, third, 0.0)
        + np.where(node == 3, fourth, 0.0)
    )


def make_tables():
    coarse = np.arange(NT1)[:, None]
    twice = 2 * coarse - 1
    base = np.clip(twice // 4 - 1, 0, NT0 - 4)
    theta = lagrange((twice - 4 * base) / 4.0, np.arange(NT0)[None, :] - base)
    coarse = np.arange(NP1)[:, None]
    twice = 2 * coarse - 1
    base = twice // 4 - 1
    phi = lagrange((twice - 4 * base) / 4.0, (np.arange(NP0)[None, :] - base) % NP0)
    polar = (np.arange(NT1) + 0.5) * math.pi / NT1
    azimuth = (np.arange(NP1) + 0.5) * 2.0 * math.pi / NP1
    fold = np.zeros((GROUPS, 2 * SAMPLES, NT0 * NP0), ml_dtypes.bfloat16)
    phase = np.zeros((GROUPS, SAMPLES, 128), np.float32)
    turn = np.zeros((GROUPS, 8, 2, SAMPLES), np.float32)
    for g in range(GROUPS):
        own = np.arange(g * QL, (g + 1) * QL)
        full = np.einsum("it,qp->iqtp", theta, phi[own]).reshape(SAMPLES, NT0 * NP0)
        high = full.astype(ml_dtypes.bfloat16)
        fold[g, :SAMPLES] = high
        fold[g, SAMPLES:] = (full - high.astype(np.float64)).astype(ml_dtypes.bfloat16)
        along_column = np.sin(polar)[:, None] * np.cos(azimuth[own])[None, :]
        along_row = np.sin(polar)[:, None] * np.sin(azimuth[own])[None, :]
        for child in range(2):
            psi = math.pi * (along_column * (child - 0.5) - along_row * 0.5)
            phase[g, :, 2 * child] = np.cos(psi).reshape(-1)
            phase[g, :, 2 * child + 1] = np.sin(psi).reshape(-1)
            turn[g, 2 * child] = np.cos(psi).reshape(-1)
            turn[g, 2 * child + 1, 0] = -np.sin(psi).reshape(-1)
            turn[g, 2 * child + 1, 1] = np.sin(psi).reshape(-1)
    return fold, phase, turn


def split(x):
    high = x.astype(BF16)
    low = (x - high.astype(F32)).astype(BF16)
    return high, low


def iota(shape, dim):
    return lax.broadcasted_iota(jnp.int32, shape, dim)


def dot(a, b):
    return jnp.dot(a, b, preferred_element_type=F32)


def dot_nt(a, b):
    return lax.dot_general(a, b, (((1,), (1,)), ((), ())), preferred_element_type=F32)


def displacements():
    return [
        (dy, dx) for dy in range(-3, 4) for dx in range(-3, 4) if max(abs(dy), abs(dx)) >= 2
    ]


def translated(parents, ta, tb):
    numbers = {pair: number for number, pair in enumerate(displacements())}
    first = [jnp.zeros((4, PSIDE, 128), F32) for _ in range(2)]
    second = [jnp.zeros((4, PSIDE, 128), F32) for _ in range(2)]
    odd_column = (iota((8, 2, PSIDE, 128), 2) & 1) == 1
    for dx in range(-3, 4):
        tile = parents[:, 8 + dx : 16 + dx, :].reshape(8, 2, PSIDE, 128)
        if dx == -3:
            tile = jnp.where(odd_column, tile, 0.0)
        if dx == 3:
            tile = jnp.where(odd_column, 0.0, tile)
        for dy in range(-3, 4):
            if (dy, dx) not in numbers:
                continue
            number = numbers[dy, dx]
            wa = ta[number : number + 1, :].reshape(1, 1, 128)
            wb = tb[number : number + 1, :].reshape(1, 1, 128)
            for parity in range(2):
                if dy == (-3 if parity == 0 else 3):
                    continue
                start = 4 + dy + parity
                source = tile[start // 2 : start // 2 + 4, start % 2]
                first[parity] = first[parity] + wa * source
                second[parity] = second[parity] + wb * source
    first = jnp.stack(first, axis=1).reshape(64, 128)
    second = jnp.stack(second, axis=1).reshape(64, 128)
    return first + pltpu.roll(second, 64, 1)


def kernel(
    across,
    code_hbm,
    count_ref,
    cur_hbm,
    rad_hbm,
    near_hbm,
    trans_hbm,
    fold_hbm,
    phase_hbm,
    turn_hbm,
    out_ref,
    code_ref,
    cur,
    rad,
    near,
    trans,
    fold,
    phase,
    turn,
    ops,
    ta,
    tb,
    field,
    side,
    mats,
    base,
    found,
    ext,
    index_col,
    load_sem,
    fs_sem,
    fr_sem,
    ts_sem,
    tr_sem,
    next_sem,
    above_sem,
):
    block = lax.axis_index("box")
    group = lax.axis_index("dir")
    row = block // across
    col = block % across

    loads = []
    for number, (source, target) in enumerate(
        (
            (trans_hbm.at[pl.ds(0, 64)], trans.at[pl.ds(0, 64)]),
            (code_hbm, code_ref),
            (cur_hbm, cur),
            (rad_hbm, rad),
            (fold_hbm, fold),
            (phase_hbm, phase),
            (near_hbm, near),
            (turn_hbm, turn),
            (trans_hbm.at[pl.ds(64, 64)], trans.at[pl.ds(64, 64)]),
        )
    ):
        copy = pltpu.make_async_copy(source, target, load_sem.at[number])
        loads.append(copy)

    loads[0].start()
    loads[8].start()

    def rank(r, c):
        usual = jnp.where(2 * r < across, 11 * r, 36 + 6 * (across - 1 - r))
        usual = (usual + 4 * c + 9 - 13 * (c & 1)) * across * across + r * across + c
        return jnp.where((group == 0) & (r == 0) & (c == 0), 1 << 20, usual)

    def beside(number):
        dr, dc = STEPS[number]
        r, c = row + dr, col + dc
        there = (r >= 0) & (r < across) & (c >= 0) & (c < across)
        return there, rank(r, c) < rank(row, col), (r * across + c, group)

    def peer(other):
        return (block, other)

    barrier = pltpu.get_barrier_semaphore()
    earlier = group
    for number in range(8):
        there, before, device = beside(number)

        @pl.when(there & jnp.logical_not(before))
        def _():
            pl.semaphore_signal(barrier, inc=1, device_id=device, device_id_type=MESH)

        earlier = earlier + jnp.where(there & before, 1, 0)
    for other in range(GROUPS):

        @pl.when(other > group)
        def _():
            pl.semaphore_signal(barrier, inc=1, device_id=peer(other), device_id_type=MESH)

    for copy in loads[1:6]:
        copy.start()

    loads[0].wait()
    loads[8].wait()
    ops[group] = jnp.transpose(trans[...])

    @pl.when(earlier > 0)
    def _():
        pl.semaphore_wait(barrier, earlier)

    def send_ops(other):
        return pltpu.make_async_remote_copy(
            src_ref=ops.at[group],
            dst_ref=ops.at[group],
            send_sem=ts_sem.at[other],
            recv_sem=tr_sem.at[group],
            device_id=peer(other),
            device_id_type=MESH,
        )

    for other in range(GROUPS):

        @pl.when(other < group)
        def _():
            pl.semaphore_signal(
                above_sem.at[group], inc=1, device_id=peer(other), device_id_type=MESH
            )

    for number in range(8):
        there, before, device = beside(number)

        @pl.when(there & before)
        def _():
            pl.semaphore_signal(
                next_sem.at[number ^ 1], inc=1, device_id=device, device_id_type=MESH
            )

    for other in range(GROUPS):

        @pl.when(other < group)
        def _():
            send_ops(other).start()

    for copy in loads[6:8]:
        copy.start()

    loads[1].wait()
    code = code_ref[...]
    across_c = ((code >> 2) & 1) + ((code >> 4) & 1) * 2 + ((code >> 6) & 1) * 4
    down_r = ((code >> 3) & 1) + ((code >> 5) & 1) * 2 + ((code >> 7) & 1) * 4
    index_row = (code & 3) * 64 + down_r * 8 + across_c
    live_index = jnp.where(iota((1, CELLS), 1) < count_ref[0], index_row, -1)
    line = iota((128, CELLS), 0)
    beyond = line - 64
    wanted = jnp.where(
        line < 64, line, ((beyond & 31) >> 2) * 8 + (beyond >> 5) * 4 + (beyond & 3)
    )
    loads[2].wait()
    place = jnp.concatenate(
        [
            jnp.where(wanted == live_index - child * 64, 1.0, 0.0).astype(BF16)
            for child in range(4)
        ],
        axis=0,
    )
    placed = dot_nt(place, cur[...]).astype(BF16)
    for child in range(4):
        field[0:64, pl.ds(child * 256, 256)] = placed[child * 128 : child * 128 + 64]
        side[:, pl.ds(child * 256, 256)] = placed[child * 128 + 64 : child * 128 + 128]

    def send_field(number, device):
        buffer, start, size, target = PIECES[number]
        source = field if buffer == "own" else side
        return pltpu.make_async_remote_copy(
            src_ref=source.at[pl.ds(start, size)],
            dst_ref=field.at[pl.ds(target, size)],
            send_sem=fs_sem.at[number],
            recv_sem=fr_sem.at[number],
            device_id=device,
            device_id_type=MESH,
        )

    def send_fields(numbers, turn_of):
        for number in numbers:
            there, before, device = beside(number)
            last = (group == 0) & (device[0] == 0)
            if turn_of == "before":
                due = before
            elif turn_of == "after":
                due = jnp.logical_not(before | last)
            else:
                due = last

            @pl.when(there & due)
            def _():
                if turn_of != "before":
                    pl.semaphore_wait(next_sem.at[number], 1)
                send_field(number, device).start()

    send_fields(range(8), "before")

    for edge, pieces in (
        (row == 0, ((64, 32), (192, 32))),
        (row == across - 1, ((96, 32), (224, 32))),
        (col == 0, ((128, 32), (192, 16), (224, 16))),
        (col == across - 1, ((160, 32), (208, 16), (240, 16))),
    ):

        @pl.when(edge)
        def _():
            for start, size in pieces:
                field[start : start + size, :] = jnp.zeros((size, 1024), BF16)
    loads[3].wait()
    loads[4].wait()
    loads[5].wait()

    def prepare(g):
        weights = fold[pl.ds(g * 128, 128), :]
        rr = dot(weights, rad[0:128, :])
        ri = dot(weights, rad[128:256, :])
        rr = rr[:64] + rr[64:]
        ri = ri[:64] + ri[64:]
        rrh, rrl = split(rr)
        rih, ril = split(ri)
        base[pl.ds(g * 256, 64), :] = jnp.concatenate([rrh, -rih], axis=1)
        base[pl.ds(g * 256 + 64, 64), :] = jnp.concatenate([rih, rrh], axis=1)
        base[pl.ds(g * 256 + 128, 64), :] = jnp.concatenate([rrl, -ril], axis=1)
        base[pl.ds(g * 256 + 192, 64), :] = jnp.concatenate([ril, rrl], axis=1)
        turns = phase[g]
        for pair in range(2):
            cosine = turns[:, 2 * pair : 2 * pair + 1]
            sine = turns[:, 2 * pair + 1 : 2 * pair + 2]
            cr, ci, sr, si = cosine * rr, cosine * ri, sine * rr, sine * ri
            for child, ar, ai in ((pair, cr + si, ci - sr), (3 - pair, cr - si, ci + sr)):
                arh, arl = split(ar)
                aih, ail = split(ai)
                matrix = jnp.concatenate(
                    [
                        jnp.concatenate([arh, -aih], axis=1),
                        jnp.concatenate([aih, arh], axis=1),
                        jnp.concatenate([arl, -ail], axis=1),
                        jnp.concatenate([ail, arl], axis=1),
                    ],
                    axis=0,
                )
                mats[g, :, pl.ds(child * 256, 256)] = matrix
        total = dot_nt(field[0:64, :], mats[g])
        total = total[:, :128] + total[:, 128:]
        ext[g, 4:12, 8:16, :] = total.reshape(PSIDE, PSIDE, 128)

    for g in range(GROUPS):
        if g == EARLY:
            send_fields((0, 1, 2, 3, 4, 5), "after")
        prepare(g)
    send_fields((6, 7), "after")
    index_col[...] = jnp.transpose(jnp.broadcast_to(index_row, (128, CELLS)))
    own_index = index_col[pl.ds(pl.multiple_of(group * OWN, OWN), OWN), :]
    pick = jnp.where((own_index[:, :64] & 63) == iota((OWN, 64), 1), 1.0, 0.0).astype(BF16)
    own_child = own_index >> 6
    own_r = ((own_index >> 3) & 7) * 2 + (own_index >> 7)
    own_c = (own_index & 7) * 2 + ((own_index >> 6) & 1)
    hot = []
    for dr in (-1, 0, 1):
        for dc in (-1, 0, 1):
            r, c = own_r + dr, own_c + dc
            child = (r & 1) * 2 + (c & 1)
            pr, pc = r >> 1, c >> 1
            north, south, west, east = pr < 0, pr > 7, pc < 0, pc > 7
            at = jnp.where(west, 131 + pr * 4, jnp.where(east, 160 + pr * 4, pr * 8 + pc))
            at = jnp.where(north, jnp.where(west, 207, jnp.where(east, 220, 88 + pc)), at)
            at = jnp.where(south, jnp.where(west, 227, jnp.where(east, 240, 96 + pc)), at)
            at = at + child * 256
            hot.append(
                jnp.concatenate(
                    [
                        jnp.where(at == iota((OWN, 128), 1) + start, 1.0, 0.0).astype(BF16)
                        for start in range(0, 1024, 128)
                    ],
                    axis=1,
                )
            )
    hot = jnp.concatenate(hot, axis=0)
    def send_up(others):
        for other in others:

            @pl.when(other > group)
            def _():
                pl.semaphore_wait(above_sem.at[other], 1)
                send_ops(other).start()

    send_up(range(1, GROUPS // 2))

    @pl.when(group >= 1)
    def _():
        send_up(range(GROUPS // 2, GROUPS))

    send_fields(range(8), "last")
    for number in range(8):
        there, _, device = beside(number ^ 1)

        @pl.when(there)
        def _():
            send_field(number, device).wait_recv()

    around = jnp.zeros((9 * OWN, 256), F32)
    for child in range(4):
        lanes = pl.ds(child * 256, 256)
        around = around + dot(hot[:, child * 256 : (child + 1) * 256], field[:, lanes])
    around = around.astype(BF16)
    loads[6].wait()
    loads[7].wait()
    close = jnp.zeros((2 * OWN, 256), F32)
    for number in range(9):
        mine = around[number * OWN : (number + 1) * OWN]
        stacked = jnp.concatenate([mine[:, :128], mine[:, 128:]], axis=0)
        close = close + dot_nt(stacked, near[pl.ds(number * 256, 256), :])
    def rim(g):
        total = dot_nt(field[64:256, :], mats[g])
        total = total[:, :128] + total[:, 128:]
        ext[g, 0:4, 8:16, :] = total[0:32].reshape(4, 8, 128)
        ext[g, 12:16, 8:16, :] = total[32:64].reshape(4, 8, 128)
        for r in range(8):
            ext[g, 4 + r, 4:8, :] = total[64 + 4 * r : 68 + 4 * r]
            ext[g, 4 + r, 16:20, :] = total[96 + 4 * r : 100 + 4 * r]
        for r in range(4):
            ext[g, r, 4:8, :] = total[128 + 4 * r : 132 + 4 * r]
            ext[g, r, 16:20, :] = total[144 + 4 * r : 148 + 4 * r]
            ext[g, 12 + r, 4:8, :] = total[160 + 4 * r : 164 + 4 * r]
            ext[g, 12 + r, 16:20, :] = total[176 + 4 * r : 180 + 4 * r]

    for g in range(GROUPS):
        rim(g)
    @pl.when(group < 1)
    def _():
        send_up(range(GROUPS // 2, GROUPS))

    left = iota((DISP, 128), 1) < 64
    for g in range(GROUPS):

        @pl.when(g != group)
        def _():
            pltpu.make_async_remote_copy(
                src_ref=ops.at[g],
                dst_ref=ops.at[g],
                send_sem=ts_sem.at[g],
                recv_sem=tr_sem.at[g],
                device_id=peer(g),
                device_id_type=MESH,
            ).wait_recv()

        here = ops[g]
        turned = pltpu.roll(here, 64, 1)
        ta[g] = jnp.where(left, here, turned)
        tb[g] = jnp.where(left, turned, -here)
        high, low = split(translated(ext.at[g], ta.at[g], tb.at[g]))
        found[:, g * 256 : g * 256 + 128] = high
        found[:, g * 256 + 128 : g * 256 + 256] = low

    chosen = dot(pick, found[...])
    outer = (own_child == 0) | (own_child == 3)
    upper = own_child < 2
    tops, bottoms = [], []
    for g in range(GROUPS):
        value = chosen[:, g * 256 : g * 256 + 128] + chosen[:, g * 256 + 128 : g * 256 + 256]
        cosine = jnp.where(outer, turn[g, 0:1, :], turn[g, 2:3, :])
        sine = jnp.where(outer, turn[g, 1:2, :], turn[g, 3:4, :])
        sine = jnp.where(upper, sine, -sine)
        high, low = split(cosine * value + sine * pltpu.roll(value, 64, 1))
        tops += [high, high]
        bottoms += [low, jnp.zeros_like(low)]
    stacked = jnp.concatenate(
        [jnp.concatenate(tops, axis=1), jnp.concatenate(bottoms, axis=1)], axis=0
    )
    far = dot(stacked, base[...])

    live = iota((OWN, 128), 0) + group * OWN < count_ref[0]
    far = 0.25 * (far[:OWN] + far[OWN:])
    real = far[:, :128] + (close[:OWN, :128] - close[OWN:, 128:])
    imag = far[:, 128:] + (close[OWN:, :128] + close[:OWN, 128:])
    out_ref[0] = jnp.where(live, real, 0.0).astype(BF16)
    out_ref[1] = jnp.where(live, imag, 0.0).astype(BF16)

    for number in range(8):
        there, _, device = beside(number)

        @pl.when(there)
        def _():
            send_field(number, device).wait_send()

    for other in range(GROUPS):

        @pl.when(other != group)
        def _():
            send_ops(other).wait_send()


def on_device(across, tables, currents, box_code, box_count, radiation, near_block, translation):
    fold, phase, turn = tables
    operands = (
        box_code.reshape(1, CELLS),
        box_count,
        currents.reshape(2 * U, CELLS),
        radiation.reshape(2 * 128, U),
        near_block.reshape(9 * 2 * U, U),
        jnp.transpose(translation, (1, 2, 3, 0)).reshape(128, DISP),
        jnp.asarray(fold).reshape(GROUPS * 128, 128),
        jnp.asarray(phase),
        jnp.asarray(turn).reshape(GROUPS, 8, 128),
    )
    outside = pl.BlockSpec(memory_space=pltpu.HBM)
    result = pl.pallas_call(
        functools.partial(kernel, across),
        out_shape=jax.ShapeDtypeStruct((2, OWN, U), BF16),
        in_specs=[outside, pl.BlockSpec(memory_space=pltpu.SMEM)] + [outside] * 7,
        out_specs=pl.BlockSpec(memory_space=pltpu.VMEM),
        scratch_shapes=[
            pltpu.VMEM((1, CELLS), jnp.int32),
            pltpu.VMEM((256, 256), BF16),
            pltpu.VMEM((256, 128), BF16),
            pltpu.VMEM((9 * 256, 128), BF16),
            pltpu.VMEM((128, DISP), F32),
            pltpu.VMEM((GROUPS * 128, 128), BF16),
            pltpu.VMEM((GROUPS, SAMPLES, 128), F32),
            pltpu.VMEM((GROUPS, 8, 128), F32),
            pltpu.VMEM((GROUPS, DISP, 128), F32),
            pltpu.VMEM((GROUPS, DISP, 128), F32),
            pltpu.VMEM((GROUPS, DISP, 128), F32),
            pltpu.VMEM((256, 1024), BF16),
            pltpu.VMEM((64, 1024), BF16),
            pltpu.VMEM((GROUPS, 256, 1024), BF16),
            pltpu.VMEM((GROUPS * 256, 256), BF16),
            pltpu.VMEM((64, GROUPS * 256), BF16),
            pltpu.VMEM((GROUPS, 16, 24, 128), F32),
            pltpu.VMEM((CELLS, 128), jnp.int32),
            pltpu.SemaphoreType.DMA((9,)),
            pltpu.SemaphoreType.DMA((8,)),
            pltpu.SemaphoreType.DMA((8,)),
            pltpu.SemaphoreType.DMA((GROUPS,)),
            pltpu.SemaphoreType.DMA((GROUPS,)),
            pltpu.SemaphoreType.REGULAR((8,)),
            pltpu.SemaphoreType.REGULAR((GROUPS,)),
        ],
        compiler_params=pltpu.CompilerParams(
            collective_id=0, has_side_effects=True, vmem_limit_bytes=48 * 1024 * 1024
        ),
    )(*(pltpu.with_memory_space_constraint(x, pltpu.HBM) if x.size > 1 else x for x in operands))
    return jnp.transpose(result, (0, 2, 1))


def solution(mesh):
    across = math.isqrt(mesh.shape["box"])
    tables = make_tables()

    def step(*arrays):
        return on_device(across, tables, *arrays)

    placed = (P(None, None, "box"), P("box"), P("box"), P(), P(), P(None, None, None, "dir"))
    return jax.shard_map(
        step,
        mesh=mesh,
        in_specs=placed,
        out_specs=P(None, None, ("box", "dir")),
        check_vma=False,
    )
```
